256 devices in a mesh: tm: 8 (over x, core), src: 32 (over z, y).
Axes of the slice: x: 4, y: 4, z: 8, core: 2. Of those that a mesh axis runs over, the one named last changes fastest.
Arguments:
- src_deriv: bfloat16 [32768, 5, 128], P(('tm', 'src')), may hold values from -6 to 6
- att_deriv: bfloat16 [32768, 12, 128], P(('tm', 'src')), may hold values from -6 to 6
- cal_deriv: bfloat16 [32768, 24, 128], P(('tm', 'src')), may hold values from -6 to 6
- obs_resid: float32 [32768, 128], P(('tm', 'src')), may hold values from -8 to 8
- obs_weight: float32 [32768, 128], P(('tm', 'src')), may hold values from 0.25 to 4
- src_id: int32 [32768], P(('tm', 'src')), may hold values from 0 to 1023
- tile_knot: int32 [32768], P(('tm', 'src')), may hold values from 0 to 32761, as said below
- row_offset: int32 [32768, 128], P(('tm', 'src')), may hold values from 0 to 3
- cal_unit: int32 [32768], P(('tm', 'src')), may hold values from 0 to 63
- src_prior: float32 [5, 32768], P(None, 'src'), may hold values from 100 to 1000
- att_ridge: float32 [98304], P('tm'), may hold values from 100 to 1000
Outputs:
- source_update: float32 [5, 32768], P(None, 'src')
- attitude_update: float32 [98304], P('tm')
- calib_update: float32 [24, 64], replicated
- residual_out: float32 [32768, 128], P(('tm', 'src'))
The draws below stay inside these ranges and needn't reach their ends.
Inputs may be any that keep to these rules, and one draw needn't show every extreme that they name: `tile_knot`: tile t belongs to time slab t // 4096; its knot lies in that slab's knots, from slab * 4096 to slab * 4096 + 4095, and is at most 32761.
All inputs are finite; a program needn't handle non-finite values.
Results may differ from the reference program's by a relative error of at most 0.0003.
Values sent between devices are 32-bit elements; how exact they have to be, the bound alone decides.
A program may use at most 128 MiB of HBM per device.

```python
import math
import jax
import jax.numpy as jnp
import numpy as np
from jax import lax

ROWS = 128
SRC_PAR = 5
ATT_PAR = 12
CAL_PAR = 24
TILE_DEV = 128
SRC_GRP = 1024
KN = 4096
NCU = 64
CG_ITERS = 6
SOURCES = 32768
KNOTS = 32768
ATT_PAR_ALL = 98304
SLAB_TILES = 4096
TILES_ALL = 32768
N_SRC = 32


def draw_tile_knot(key, part):
    key = jax.random.fold_in(key, 7)
    tile_place = jnp.arange(TILES_ALL, dtype=jnp.int32)
    slab_start = tile_place // SLAB_TILES * KN
    knot_index = slab_start + jax.random.randint(key, (TILES_ALL,), 0, KN, dtype=jnp.int32)
    knot_index = jnp.minimum(knot_index, KNOTS - 7)
    knot_index = knot_index.at[0].set(0).at[TILES_ALL - 1].set(KNOTS - 7)
    return knot_index.astype(jnp.int32)


def place_ends(drawn, rng, low, high):
    dims = drawn.shape
    place = [jax.random.randint(jax.random.fold_in(rng, axis), (), 0, dims[axis]) for axis in range(len(dims))]
    drawn = drawn.at[tuple(place)].set(low)
    longest = dims.index(max(dims))
    place[longest] = (place[longest] + 1) % dims[longest]
    return drawn.at[tuple(place)].set(high)


def levels(stream_key, dims, cuts, smallest, largest):
    def one(axis_at, shards_of):
        heights = jax.random.uniform(jax.random.fold_in(jax.random.fold_in(stream_key, 6), axis_at), (shards_of,), jnp.float32, smallest / len(cuts), largest / len(cuts))
        return jnp.repeat(jnp.exp(heights), dims[axis_at] // shards_of).reshape((-1,) + (1,) * (len(dims) - axis_at - 1))

    loudness = one(*cuts[0])
    for cut in cuts[1:]:
        loudness = loudness * one(*cut)
    return loudness


def centred(stream_key, dims, deviation, reach, cuts=(), kind=jnp.bfloat16):
    values = jax.random.normal(stream_key, dims, jnp.float32) * deviation
    if len(cuts) > 0:
        values = levels(stream_key, dims, cuts, -0.22, 0.18) * values
    return jnp.clip(values, min=-reach, max=reach).astype(kind)


def setup_inputs(seed: int = 0) -> dict:
    splits = jax.random.split(jax.random.key(seed), 12)
    return {
        "src_deriv": centred(splits[0], (TILES_ALL, SRC_PAR, ROWS), 1.0, 6.0, ((0, 256),)),
        "att_deriv": centred(splits[1], (TILES_ALL, ATT_PAR, ROWS), 1.0, 6.0, ((0, 256),)),
        "cal_deriv": centred(splits[2], (TILES_ALL, CAL_PAR, ROWS), 1.0, 6.0, ((0, 256),)),
        "obs_resid": centred(splits[3], (TILES_ALL, ROWS), 1.0, 8.0, ((0, 256),), jnp.float32),
        "obs_weight": jnp.clip(jnp.exp(math.log(4.0) - 2.7725887 * jax.random.uniform(splits[4], (TILES_ALL, ROWS), jnp.float32) ** levels(splits[4], (TILES_ALL, ROWS), ((0, 256),), -0.2, 0.2)), 0.25, 4.0),
        "src_id": place_ends(jax.random.randint(splits[5], (TILES_ALL,), 0, SRC_GRP), jax.random.fold_in(splits[5], 1), 0, SRC_GRP - 1).astype(jnp.int32),
        "tile_knot": draw_tile_knot(jax.random.fold_in(splits[11], 71), 0),
        "row_offset": place_ends(jax.random.randint(splits[7], (TILES_ALL, ROWS), 0, 4), jax.random.fold_in(splits[7], 1), 0, 3).astype(jnp.int32),
        "cal_unit": place_ends(jax.random.randint(splits[8], (TILES_ALL,), 0, NCU), jax.random.fold_in(splits[8], 1), 0, NCU - 1).astype(jnp.int32),
        "src_prior": jnp.clip(jnp.exp(math.log(1000.0) - 2.3025851 * jax.random.uniform(splits[9], (SRC_PAR, SOURCES), jnp.float32) ** levels(splits[9], (SRC_PAR, SOURCES), ((1, 32),), -0.2, 0.2)), 100.0, 1000.0),
        "att_ridge": jnp.clip(jnp.exp(math.log(1000.0) - 2.3025851 * jax.random.uniform(splits[10], (ATT_PAR_ALL,), jnp.float32) ** levels(splits[10], (ATT_PAR_ALL,), ((0, 8),), -0.2, 0.2)), 100.0, 1000.0),
    }


HIGH = lax.Precision.HIGHEST

def lag_table():
    first_index = np.arange(21)[None, :]
    lag_rows = np.arange(12)[:, None]
    second = first_index + lag_rows
    flat_index = first_index * 21 + np.minimum(second, 20)
    return (flat_index, (second < 21).astype(np.float32))

def solve_spd(matrix, right):
    order = right.shape[0]
    factor = [[None] * order for column in range(order)]
    for j in range(order):
        diag_sum = matrix[j, j]
        for m in range(j):
            diag_sum = diag_sum - factor[j][m] * factor[j][m]
        root_value = jnp.sqrt(diag_sum)
        factor[j][j] = root_value
        for i in range(j + 1, order):
            entry = matrix[i, j]
            for m in range(j):
                entry = entry - factor[i][m] * factor[j][m]
            factor[i][j] = entry / root_value
    forward = []
    for i in range(order):
        entry = right[i]
        for m in range(i):
            entry = entry - factor[i][m] * forward[m]
        forward.append(entry / factor[i][i])
    answer = [None] * order
    for i in range(order - 1, -1, -1):
        entry = forward[i]
        for m in range(i + 1, order):
            entry = entry - factor[m][i] * answer[m]
        answer[i] = entry / factor[i][i]
    return jnp.stack(answer)

def tile_normals(deriv, weight, resid):
    values = deriv.astype(jnp.float32)
    weighted = values * weight[:, None, :]
    normal = jnp.einsum('tkr,tlr->tkl', weighted, values, precision=HIGH)
    right = jnp.einsum('tkr,tr->tk', weighted, resid, precision=HIGH)
    return jnp.concatenate([normal.reshape(normal.shape[0], -1), right], axis=1)

def small_solve(sums, prior, order):
    count = sums.shape[1]
    matrix = sums[:order * order].reshape(order, order, count)
    if prior is not None:
        matrix = matrix + jnp.eye(order, dtype=jnp.float32)[:, :, None] * prior[:, None, :]
    return solve_spd(matrix, sums[order * order:])

def window_rows(att_deriv, row_offset):
    values = att_deriv.astype(jnp.float32)
    window = jnp.zeros((values.shape[0], 21, values.shape[2]), jnp.float32)
    for knot_step in range(4):
        placed = jnp.pad(values, ((0, 0), (3 * knot_step, 9 - 3 * knot_step), (0, 0)))
        window = window + jnp.where((row_offset == knot_step)[:, None, :], placed, 0.0)
    return window

def attitude_terms(window, weight, resid):
    weighted = window * weight[:, None, :]
    normal = jnp.einsum('tjr,tlr->tjl', weighted, window, precision=HIGH)
    right = jnp.einsum('tjr,tr->tj', weighted, resid, precision=HIGH)
    flat_index, valid_lag = lag_table()
    banded = normal.reshape(normal.shape[0], 441)[:, flat_index] * valid_lag
    return jnp.concatenate([banded, right[:, None, :]], axis=1)

def conjugate(band_rows, right, ridge_part, band_edge, extend, inner_sum):
    count = right.shape[0]
    lagged = jnp.concatenate([band_edge, band_rows[1:]], axis=1)

    def apply(vector):
        padded = extend(vector)
        result = ridge_part * vector
        for d in range(12):
            result = result + band_rows[d] * padded[11 + d:11 + d + count]
        for d in range(1, 12):
            result = result + lagged[d - 1, 11 - d:11 - d + count] * padded[11 - d:11 - d + count]
        return result
    solution = jnp.zeros_like(right)
    residual = right
    direction = right
    norm_now = inner_sum(residual, residual)
    for iteration in range(CG_ITERS):
        image = apply(direction)
        step_size = norm_now / inner_sum(direction, image)
        solution = solution + step_size * direction
        residual = residual - step_size * image
        norm_next = inner_sum(residual, residual)
        direction = residual + norm_next / norm_now * direction
        norm_now = norm_next
    return solution

def pad_vector(vector):
    return jnp.pad(vector, 11)

def plain_inner(first_vec, second_vec):
    return jnp.sum(first_vec * second_vec)

def reference(src_deriv, att_deriv, cal_deriv, obs_resid, obs_weight, src_id, tile_knot, row_offset, cal_unit, src_prior, att_ridge):
    blocks = TILES_ALL // TILE_DEV

    def split(array):
        return array.reshape((blocks, TILE_DEV) + array.shape[1:])
    tile_place = jnp.arange(TILES_ALL, dtype=jnp.int32) // TILE_DEV
    source_index = tile_place % N_SRC * SRC_GRP + src_id

    def add_sources(carry, pieces):
        deriv, weight, resid, index = pieces
        return (carry + jax.ops.segment_sum(tile_normals(deriv, weight, resid), index, num_segments=SOURCES), None)
    source_sums = lax.scan(add_sources, jnp.zeros((SOURCES, 30), jnp.float32), (split(src_deriv), split(obs_weight), split(obs_resid), split(source_index)))[0]
    source_update = small_solve(source_sums.T, src_prior, 5)
    resid_a = obs_resid - jnp.einsum('tkr,kt->tr', src_deriv.astype(jnp.float32), source_update[:, source_index], precision=HIGH)
    knot_cols = jnp.arange(21, dtype=jnp.int32)[None, :]

    def add_attitude(carry, pieces):
        deriv, offset, weight, resid, knot = pieces
        values = attitude_terms(window_rows(deriv, offset), weight, resid)
        columns = 3 * knot[:, None] + knot_cols
        return (carry + jax.ops.segment_sum(values.transpose(0, 2, 1).reshape(-1, 13), columns.reshape(-1), num_segments=ATT_PAR_ALL), None)
    att_sums = lax.scan(add_attitude, jnp.zeros((ATT_PAR_ALL, 13), jnp.float32), (split(att_deriv), split(row_offset), split(obs_weight), split(resid_a), split(tile_knot)))[0].T
    band_edge = jnp.zeros((11, 11), jnp.float32)
    attitude_update = conjugate(att_sums[:12], att_sums[12], att_ridge, band_edge, pad_vector, plain_inner)

    def correct_attitude(pieces):
        deriv, offset, resid, knot = pieces
        columns = 3 * knot[:, None] + knot_cols
        return resid - jnp.einsum('tjr,tj->tr', window_rows(deriv, offset), attitude_update[columns], precision=HIGH)
    resid_b = lax.map(correct_attitude, (split(att_deriv), split(row_offset), split(resid_a), split(tile_knot))).reshape(TILES_ALL, ROWS)

    def add_calib(carry, pieces):
        deriv, weight, resid, unit = pieces
        return (carry + jax.ops.segment_sum(tile_normals(deriv, weight, resid), unit, num_segments=NCU), None)
    calib_sums = lax.scan(add_calib, jnp.zeros((NCU, 600), jnp.float32), (split(cal_deriv), split(obs_weight), split(resid_b), split(cal_unit)))[0]
    calib_update = small_solve(calib_sums.T, None, 24)
    residual_out = resid_b - jnp.einsum('tkr,kt->tr', cal_deriv.astype(jnp.float32), calib_update[:, cal_unit], precision=HIGH)
    return (source_update, attitude_update, calib_update, residual_out)
```

```python
import functools

import jax
import jax.numpy as jnp
import numpy as np
from jax import lax
from jax.experimental import pallas as pl
from jax.experimental.pallas import tpu as pltpu
from jax.sharding import PartitionSpec as P

NCU = 64
CG_ITERS = 6


HIGH = lax.Precision.HIGHEST


def padded_2(cells, sides, width):
    for axis, dim in sides:
        count = lax.axis_size(axis)
        ends = count - 1
        head = lax.slice_in_dim(cells, 0, width, axis=dim)
        tail = lax.slice_in_dim(cells, cells.shape[dim] - width, cells.shape[dim], axis=dim)
        cells = jnp.concatenate(
            [
                lax.ppermute(tail, axis, [(i, (i + 1) % count) for i in range(ends)]),
                cells,
                lax.ppermute(head, axis, [((i + 1) % count, i) for i in range(ends)]),
            ],
            axis=dim,
        )
    return cells


def from_behind(array, axis, by):
    devices = lax.axis_size(axis)
    pairs = [(i, i + by) for i in range(devices) if 0 <= i + by < devices]
    return lax.ppermute(array, axis, pairs)


def lag_table():
    first_index = np.arange(21)[None, :]
    lag_rows = np.arange(12)[:, None]
    second = first_index + lag_rows
    flat_index = first_index * 21 + np.minimum(second, 20)
    return (flat_index, (second < 21).astype(np.float32))


def solve_spd(matrix, right):
    order = right.shape[0]
    rows = jnp.arange(order)[:, None]

    def column(j, state):
        rest, factor = state
        col = jnp.where(rows >= j, rest[:, j] / jnp.sqrt(rest[j, j]), 0.0)
        return rest - col[:, None, :] * col[None, :, :], factor.at[:, j].set(col)

    factor = lax.fori_loop(0, order, column, (matrix, jnp.zeros_like(matrix)))[1]

    def forward(i, answer):
        value = right[i] - jnp.sum(jnp.where(rows < i, factor[i] * answer, 0.0), axis=0)
        return answer.at[i].set(value / factor[i, i])

    halfway = lax.fori_loop(0, order, forward, jnp.zeros_like(right))

    def backward(step, answer):
        i = order - 1 - step
        value = halfway[i] - jnp.sum(jnp.where(rows > i, factor[:, i] * answer, 0.0), axis=0)
        return answer.at[i].set(value / factor[i, i])

    return lax.fori_loop(0, order, backward, jnp.zeros_like(right))


def tile_normals(deriv, weight, resid):
    values = deriv.astype(jnp.float32)
    weighted = values * weight[:, None, :]
    normal = jnp.einsum("tkr,tlr->tkl", weighted, values, precision=HIGH)
    right = jnp.einsum("tkr,tr->tk", weighted, resid, precision=HIGH)
    return jnp.concatenate([normal.reshape(normal.shape[0], -1), right], axis=1)


def small_solve(sums, prior, order):
    count = sums.shape[1]
    matrix = sums[: order * order].reshape(order, order, count)
    if prior is not None:
        matrix = matrix + jnp.eye(order, dtype=jnp.float32)[:, :, None] * prior[:, None, :]
    return solve_spd(matrix, sums[order * order :])


def window_rows(att_deriv, row_offset):
    values = att_deriv.astype(jnp.float32)
    window = jnp.zeros((values.shape[0], 21, values.shape[2]), jnp.float32)
    for knot_step in range(4):
        placed = jnp.pad(values, ((0, 0), (3 * knot_step, 9 - 3 * knot_step), (0, 0)))
        window = window + jnp.where((row_offset == knot_step)[:, None, :], placed, 0.0)
    return window


def attitude_terms(window, weight, resid):
    weighted = window * weight[:, None, :]
    normal = jnp.einsum("tjr,tlr->tjl", weighted, window, precision=HIGH)
    right = jnp.einsum("tjr,tr->tj", weighted, resid, precision=HIGH)
    flat_index, valid_lag = lag_table()
    banded = normal.reshape(normal.shape[0], 441)[:, flat_index] * valid_lag
    return jnp.concatenate([banded, right[:, None, :]], axis=1)


def conjugate(band_rows, right, ridge_part, band_edge, extend, inner_sum):
    count = right.shape[0]
    lagged = jnp.concatenate([band_edge, band_rows[1:]], axis=1)
    solution = jnp.zeros_like(right)
    residual = right
    direction = right
    norm_now = inner_sum(residual, residual)
    for iteration in range(CG_ITERS):
        padded = extend(direction)
        result = ridge_part * direction
        for d in range(12):
            result = result + band_rows[d] * padded[11 + d : 11 + d + count]
        for d in range(1, 12):
            result = (
                result + lagged[d - 1, 11 - d : 11 - d + count] * padded[11 - d : 11 - d + count]
            )
        step_size = norm_now / inner_sum(direction, result)
        solution = solution + step_size * direction
        residual = residual - step_size * result
        norm_next = inner_sum(residual, residual)
        direction = residual + norm_next / norm_now * direction
        norm_now = norm_next
    return solution


def slab_extend(vector):
    return padded_2(vector, (("tm", 0),), 11)


def slab_dot(first_vec, second_vec):
    return lax.psum(jnp.sum(first_vec * second_vec), "tm")


def shards(
    src_deriv,
    att_deriv,
    cal_deriv,
    obs_resid,
    obs_weight,
    src_id,
    tile_knot,
    row_offset,
    cal_unit,
    src_prior,
    att_ridge,
):
    slab_pos = lax.axis_index("tm")
    groups = src_prior.shape[1]
    normal_sums = jax.ops.segment_sum(
        tile_normals(src_deriv, obs_weight, obs_resid), src_id, num_segments=groups
    ).T
    summed = lax.psum(normal_sums, "tm")
    source_update = small_solve(summed, src_prior, 5)
    resid_a = obs_resid - jnp.einsum(
        "tkr,kt->tr", src_deriv.astype(jnp.float32), source_update[:, src_id], precision=HIGH
    )
    slab_params = att_ridge.shape[0]
    window = window_rows(att_deriv, row_offset)
    local_knot = tile_knot - slab_pos * (slab_params // 3)
    columns = 3 * local_knot[:, None] + jnp.arange(21, dtype=jnp.int32)[None, :]
    values = attitude_terms(window, obs_weight, resid_a)
    slab_sums = jax.ops.segment_sum(
        values.transpose(0, 2, 1).reshape(-1, 13),
        columns.reshape(-1),
        num_segments=slab_params + 21,
    ).T
    carried = from_behind(slab_sums[:, slab_params:], "tm", 1)
    head_sums = slab_sums[:, :slab_params].at[:, :21].add(carried)
    summed_band = lax.psum(head_sums, "src")
    band_edge = from_behind(summed_band[1:12, -11:], "tm", 1)
    attitude_update = conjugate(
        summed_band[:12], summed_band[12], att_ridge, band_edge, slab_extend, slab_dot
    )
    next_params = from_behind(attitude_update[:21], "tm", -1)
    extended = jnp.concatenate([attitude_update, next_params])
    resid_b = resid_a - jnp.einsum("tjr,tj->tr", window, extended[columns], precision=HIGH)
    calib_sums = jax.ops.segment_sum(
        tile_normals(cal_deriv, obs_weight, resid_b), cal_unit, num_segments=NCU
    ).T
    calib_total = lax.psum(calib_sums, ("tm", "src"))
    calib_update = small_solve(calib_total, None, 24)
    residual_out = resid_b - jnp.einsum(
        "tkr,kt->tr", cal_deriv.astype(jnp.float32), calib_update[:, cal_unit], precision=HIGH
    )
    return (source_update, attitude_update, calib_update, residual_out)


F32 = jnp.float32
BF16 = jnp.bfloat16
MESH = pl.DeviceIdType.MESH
MROWS = 40
TRUST = 0.01


def pieces_2(x):
    high = x.astype(BF16)
    return high, (x - high.astype(F32)).astype(BF16)


def pieces_3(x):
    high = x.astype(BF16)
    rest = x - high.astype(F32)
    mid = rest.astype(BF16)
    return high, mid, (rest - mid.astype(F32)).astype(BF16)


def dot_nn(a, b):
    return lax.dot_general(a, b, (((1,), (0,)), ((), ())), preferred_element_type=F32)


def dot_nt(a, b):
    return lax.dot_general(a, b, (((1,), (1,)), ((), ())), preferred_element_type=F32)


def iota(shape, dim):
    return lax.broadcasted_iota(jnp.int32, shape, dim)


def hot(match):
    return jnp.where(match, 1.0, 0.0).astype(BF16)


def band_slots():
    slots = [(0, c, d) for c in range(3) for d in range(c, 3)]
    for delta in range(1, 4):
        slots += [(delta, c, d) for c in range(3) for d in range(3)]
    return slots


SLOTS = band_slots()
SLOT_AT = {slot: v for v, slot in enumerate(SLOTS)}
SRC_PAIRS = [(k, l) for k in range(5) for l in range(k, 5)]
SRC_AT = {pair: e for e, pair in enumerate(SRC_PAIRS)}
GRAM_PAIRS = [(i, j) for i in range(CG_ITERS) for j in range(i, CG_ITERS)]


def cal_row(k, l):
    if k < 8:
        return 24 * k + l
    if k < 16:
        return 192 + 16 * (k - 8) + l - 8
    return 320 + 8 * (k - 16) + l - 16


def place_lanes(lo_row):
    inside = iota((128, 128), 0) - lo_row
    return inside, iota((8, 128), 0) + 128 - lo_row


def local_kernel(
    n_src,
    n_hi,
    src_ref,
    att_ref,
    cal_ref,
    resid_ref,
    weight_ref,
    offset_ref,
    meta_ref,
    prior_ref,
    ridge_ref,
    win_ref,
    w_ref,
    r_ref,
    vs_ref,
    mb_ref,
    cp_ref,
    po_ref,
    winp,
    srcp,
    calp,
    offp,
    vm,
    vc,
):
    w_ref[...] = weight_ref[...].T
    r_ref[...] = resid_ref[...].T
    offp[...] = offset_ref[...].astype(F32).T.astype(jnp.int32)
    vm[...] = jnp.zeros_like(vm)
    mb_ref[...] = jnp.zeros_like(mb_ref)

    def windows(i, carry):
        rows = pl.ds(pl.multiple_of(i * 16, 16), 16)
        values = [att_ref[k, rows, :].astype(F32) for k in range(12)]
        step = offp[rows, :]
        for j in range(21):
            placed = jnp.zeros((16, 128), F32)
            for o in range(4):
                if 0 <= j - 3 * o < 12:
                    placed = jnp.where(step == o, values[j - 3 * o], placed)
            winp[j, rows, :] = placed
            win_ref[j, rows, :] = placed.astype(BF16)
        for k in range(5):
            srcp[k, rows, :] = src_ref[k, rows, :].astype(F32)
        for k in range(24):
            calp[k, rows, :] = cal_ref[k, rows, :].astype(F32)
        return carry

    lax.fori_loop(0, 8, windows, 0)

    def summed(count, terms):
        def body(i, sums):
            rows = pl.ds(pl.multiple_of(i * 8, 8), 8)
            return tuple(s + t for s, t in zip(sums, terms(rows)))

        sums = lax.fori_loop(0, 16, body, tuple(jnp.zeros((8, 128), F32) for _ in range(count)))
        return [jnp.sum(s, axis=0, keepdims=True) for s in sums]

    def src_terms(rows):
        x = [srcp[k, rows, :] for k in range(5)]
        w = w_ref[rows, :]
        y = [w * v for v in x]
        r = r_ref[rows, :]
        return [y[k] * x[l] for k, l in SRC_PAIRS] + [v * r for v in y]

    vs_ref[...] = jnp.zeros_like(vs_ref)
    for e, row in enumerate(summed(20, src_terms)):
        vs_ref[e : e + 1, :] = row
    vs_ref[20:21, :] = meta_ref[0:1, :].astype(F32)

    trace = jnp.sum(ridge_ref[...], axis=0, keepdims=True) * (1.0 / n_src)
    for m in range(7):
        slots = [s for s in SLOTS if m + s[0] < 7]

        def att_terms(rows, m=m, slots=slots):
            x = [winp[j, rows, :] for j in range(3 * m, min(3 * m + 12, 21))]
            w = w_ref[rows, :]
            y = [w * x[c] for c in range(3)]
            return [y[c] * x[3 * delta + d] for delta, c, d in slots]

        for slot, row in zip(slots, summed(len(slots), att_terms)):
            vm[m, SLOT_AT[slot] : SLOT_AT[slot] + 1, :] = row
            if slot[0] == 0 and slot[1] == slot[2]:
                trace = trace + row
    vs_ref[21:22, :] = trace

    for kg in range(6):
        for lg in range(kg // 2, 3):

            def cal_terms(rows, kg=kg, lg=lg):
                w = w_ref[rows, :]
                y = [w * calp[4 * kg + k, rows, :] for k in range(4)]
                x = [calp[8 * lg + l, rows, :] for l in range(8)]
                return [y[k] * x[l] for k in range(4) for l in range(8)]

            sums = summed(32, cal_terms)
            for k in range(4):
                at = cal_row(4 * kg + k, 8 * lg)
                vc[at : at + 8, :] = jnp.concatenate(sums[8 * k : 8 * k + 8], axis=0)
    unit_hot = hot(iota((NCU, 128), 0) == meta_ref[2:3, :])
    unit_hot = jnp.concatenate([unit_hot, unit_hot], axis=1)
    units = dot_nt(jnp.concatenate(pieces_2(vc[...]), axis=1), unit_hot)
    cp_ref[...] = jnp.concatenate([units[:192], units[192:]], axis=1)

    knot = meta_ref[1:2, :]
    block, place = knot >> 7, knot & 127
    inside, past = place_lanes(place)
    blocks = iota((n_hi + 8, 128), 0)
    here, after = hot(blocks == block), hot(blocks == block + 1)
    left = jnp.concatenate([here, here, after, after], axis=1)
    rest = jnp.zeros((120, 128), F32)
    for v, (delta, c, d) in enumerate(SLOTS):
        spread = jnp.zeros((128, 128), F32)
        over = jnp.zeros((8, 128), F32)
        for m in range(7 - delta):
            row = vm[m, v : v + 1, :]
            spread = jnp.where(inside == m, row, spread)
            over = jnp.where(past == m, row, over)
        over = jnp.concatenate([over, rest], axis=0)
        right = jnp.concatenate(pieces_2(spread) + pieces_2(over), axis=1)
        mb_ref[pl.ds(v, n_hi, stride=MROWS), :] = dot_nt(left, right)[:n_hi]

    groups = prior_ref.shape[1]
    source_hot = hot(iota((groups, 128), 0) == meta_ref[0:1, :])
    owned = dot_nn(jnp.concatenate(pieces_3(prior_ref[...]), axis=0), source_hot)
    po_ref[...] = owned[0:8] + owned[8:16] + owned[16:24]


def ldl_solve(entry, right, order):
    low = {}
    pivots, inverse, shares = [], [], []
    for j in range(order):
        pivot = entry(j, j)
        for m in range(j):
            pivot = pivot - low[j, m] * low[j, m] * pivots[m]
        shares.append(pivot / entry(j, j))
        pivots.append(pivot)
        inverse.append(1.0 / pivot)
        for i in range(j + 1, order):
            value = entry(j, i)
            for m in range(j):
                value = value - low[i, m] * (low[j, m] * pivots[m])
            low[i, j] = value * inverse[j]
    forward = []
    for i in range(order):
        value = right(i)
        for m in range(i):
            value = value - low[i, m] * forward[m]
        forward.append(value)
    answer = [None] * order
    for i in range(order - 1, -1, -1):
        value = forward[i] * inverse[i]
        for m in range(i + 1, order):
            value = value - low[m, i] * answer[m]
        answer[i] = value
    return answer, shares


def joint_kernel(
    n_tm,
    n_src,
    n_hi,
    src_ref,
    win_ref,
    cal_ref,
    w_ref,
    r_ref,
    vs_ref,
    mb_ref,
    cp_ref,
    po_ref,
    meta_ref,
    prior_ref,
    ridge_ref,
    update_ref,
    att_ref,
    calib_ref,
    resid_ref,
    trust_ref,
    vsr,
    mr,
    mown,
    halo,
    band,
    pb,
    br,
    basis,
    image,
    gs,
    g1,
    g2,
    gt,
    xm,
    xr,
    sub,
    cr,
    c2s,
    c2r,
    c3s,
    cf,
    inv,
    ra,
    vrow,
    kz,
    ky,
    kt,
    ks,
    send,
    recv,
):
    tm, sr = lax.axis_index("tm"), lax.axis_index("src")
    last_tm, last_sr = n_tm - 1, n_src - 1
    has_next, has_prev = tm < last_tm, tm > 0
    first, final = sr == 0, sr == last_sr
    ny = min(4, n_src)
    nz = n_src // ny
    yy, zz = sr % ny, sr // ny
    per_own = 24 // min(24, n_src)
    n_own = 24 // per_own
    share = 8 * per_own
    owner = sr < n_own
    lanes = prior_ref.shape[1] // n_tm

    def start(source, target, at, place):
        pltpu.make_async_remote_copy(
            src_ref=source,
            dst_ref=target,
            send_sem=send.at[at],
            recv_sem=recv.at[at],
            device_id=place,
            device_id_type=MESH,
        ).start()

    def arrived(part, at):
        pltpu.make_async_copy(part, part, recv.at[at]).wait()

    def left_us(part, at):
        pltpu.make_async_copy(part, part, send.at[at]).wait()

    def each(count, body):
        def run(d, carry):
            body(d)
            return carry

        lax.fori_loop(0, count, run, 0)

    def other_src(body):
        each(last_sr, lambda d: body((sr + 1 + d) % n_src))

    def other_tm(body):
        each(last_tm, lambda d: body((tm + 1 + d) % n_tm))

    halo[...] = jnp.zeros_like(halo)
    xr[...] = jnp.zeros_like(xr)

    barrier = pltpu.get_barrier_semaphore()

    def greet(a, b):
        pl.semaphore_signal(barrier, inc=1, device_id=(a, b), device_id_type=MESH)

    other_tm(lambda p: greet(p, sr))
    other_src(lambda p: greet(tm, p))
    next_tm, prev_tm = jnp.minimum(tm + 1, last_tm), jnp.maximum(tm - 1, 0)
    pl.when(has_next)(lambda: greet(next_tm, 0))
    pl.when(has_prev)(lambda: greet(prev_tm, last_sr))
    pl.when(has_prev & first)(lambda: each(n_src, lambda i: greet(prev_tm, i)))
    pl.when(has_next & final)(lambda: each(n_src, lambda i: greet(next_tm, i)))

    ids = jnp.broadcast_to(meta_ref[0:1, :].astype(F32), (128, 128)).T
    sources = (iota((lanes, 128), 0) + tm * lanes).astype(F32)
    wanted = jnp.concatenate([ids, sources], axis=0)
    knot = meta_ref[1:2, :]
    block, place = knot >> 7, knot & 127
    inside, past = place_lanes(place)
    blocks = iota((n_hi + 8, 128), 0)
    here, after = hot(blocks == block), hot(blocks == block + 1)
    spreads = jnp.concatenate([here, here, after, after], axis=1)
    unit_hot = hot(iota((NCU, 128), 0) == meta_ref[2:3, :])
    unit_hot_2 = jnp.concatenate([unit_hot, unit_hot], axis=1)
    flat_at, plane_at = iota((384, 384), 1), iota((384, 384), 0)
    mixed = hot(flat_at == 3 * (plane_at & 127) + (plane_at >> 7))
    flat_ridge = jnp.concatenate([ridge_ref[pl.ds(3 * sr + q, 1), :] for q in range(3)], axis=1)
    ridge_row = sum(dot_nt(jnp.broadcast_to(part, (16, 384)), mixed)[0:1] for part in pieces_3(flat_ridge))

    callers = last_tm + last_sr + jnp.where(has_next, 1, 0) + jnp.where(has_prev, 1, 0)
    callers = callers + jnp.where(has_prev & first, n_src, 0) + jnp.where(has_next & final, n_src, 0)
    pl.semaphore_wait(barrier, callers)

    def band_rows(j):
        return mb_ref.at[pl.ds(pl.multiple_of(j * MROWS, 8), MROWS)]

    other_tm(lambda p: start(vs_ref, vsr.at[tm], 0, (p, sr)))
    other_src(lambda p: start(band_rows(p), mr.at[sr], 1, (tm, p)))
    pl.when(has_next)(lambda: start(band_rows(n_src), mr.at[n_src + sr], 2, (next_tm, 0)))

    def cal_share(p):
        return cp_ref.at[pl.ds(pl.multiple_of(p * share, 8), share)]

    def send_cal(p):
        pl.when(p < n_own)(lambda: start(cal_share(p), cr.at[sr], 3, (tm, p)))

    other_src(send_cal)

    vsr[tm] = vs_ref[...]
    arrived(vsr.at[pl.ds(0, last_tm)], 0)
    normal = jnp.zeros((48, 128 + lanes), F32)
    for p in range(0, n_tm, 2):
        match = [hot(wanted == vsr[q, 20:21, :]) for q in (p, p + 1)]
        parts = [pieces_2(vsr[q]) for q in (p, p + 1)]
        left = jnp.concatenate([jnp.concatenate([part[i] for part in parts], axis=1) for i in range(2)], axis=0)
        normal = normal + dot_nt(left, jnp.concatenate(match, axis=1))
    normal = normal[:24] + normal[24:]
    trace = sum(vsr[p, 21:22, :] for p in range(n_tm))
    prior = jnp.concatenate([po_ref[...], prior_ref[:, pl.ds(pl.multiple_of(tm * lanes, 128), lanes)]], axis=1)

    def source_entry(k, l):
        row = SRC_AT[k, l]
        value = normal[row : row + 1]
        return value + prior[k : k + 1] if k == l else value

    update, _ = ldl_solve(source_entry, lambda k: normal[15 + k : 16 + k], 5)
    resid_a = r_ref[...]
    for k in range(5):
        resid_a = resid_a - src_ref[k].astype(F32) * update[k][:, :128]
    ra[...] = resid_a
    weighted = w_ref[...] * resid_a
    for j in range(21):
        vrow[j : j + 1, :] = jnp.sum(win_ref[j].astype(F32) * weighted, axis=0, keepdims=True)

    pb[...] = jnp.zeros_like(pb)
    rest = jnp.zeros((120, 128), F32)
    for c in range(3):
        spread = jnp.zeros((128, 128), F32)
        over = jnp.zeros((8, 128), F32)
        for m in range(7):
            row = vrow[3 * m + c : 3 * m + c + 1, :]
            spread = jnp.where(inside == m, row, spread)
            over = jnp.where(past == m, row, over)
        over = jnp.concatenate([over, rest], axis=0)
        right = jnp.concatenate(pieces_2(spread) + pieces_2(over), axis=1)
        pb[pl.ds(16 + c, n_hi, stride=8), :] = dot_nt(spreads, right)[:n_hi]
    pb[pl.ds(19, n_hi, stride=8), :] = jnp.where(iota((n_hi, 128), 0) < n_src, trace, 0.0)

    def right_rows(j):
        return pb.at[pl.ds(pl.multiple_of((j + 1) * 8, 8), 24)]

    other_src(lambda p: start(right_rows(p), br.at[sr], 4, (tm, p)))
    pl.when(has_next)(lambda: start(right_rows(n_src), br.at[n_src + sr], 5, (next_tm, 0)))
    pl.when(has_prev)(lambda: start(right_rows(-1), br.at[n_src + sr], 6, (prev_tm, last_sr)))

    for k in range(5):
        sub[tm, k : k + 1, :] = update[k][:, 128:]
    other_tm(lambda p: start(sub.at[tm], sub.at[tm], 7, (p, sr)))

    mr[sr] = mb_ref[pl.ds(pl.multiple_of(sr * MROWS, 8), MROWS), :]
    arrived(mr.at[pl.ds(0, last_sr)], 1)
    total = mr[0]
    for i in range(1, n_src):
        total = total + mr[i]
    mown[...] = total

    def add_carried():
        arrived(mr.at[pl.ds(n_src, n_src)], 2)
        total = mown[...]
        for i in range(n_src):
            total = total + mr[n_src + i]
        mown[...] = total

    pl.when(has_prev & first)(add_carried)
    for c in range(3):
        v = SLOT_AT[0, c, c]
        mown[v : v + 1, :] = mown[v : v + 1, :] + ridge_row[:, 128 * c : 128 * c + 128]
    lin = tm * n_src + sr
    lower, upper = jnp.maximum(lin - 1, 0), jnp.minimum(lin + 1, n_tm * n_src - 1)
    has_left, has_right = lin > 0, lin < n_tm * n_src - 1
    pl.when(has_left)(lambda: start(mown, halo.at[1], 8, (lower // n_src, lower % n_src)))
    pl.when(has_right)(lambda: start(mown, halo.at[0], 9, (upper // n_src, upper % n_src)))

    def sum_cal():
        cr[sr] = cp_ref[pl.ds(pl.multiple_of(sr * share, 8), share), :]
        arrived(cr.at[pl.ds(0, last_sr)], 3)
        total = cr[0]
        for i in range(1, n_src):
            total = total + cr[i]
        c2s[...] = total
        c2r[tm] = total
        other_tm(lambda p: start(c2s, c2r.at[tm], 10, (p, sr)))

    pl.when(owner)(sum_cal)

    pl.when(has_left)(lambda: arrived(halo.at[0], 9))
    pl.when(has_right)(lambda: arrived(halo.at[1], 8))
    full = jnp.concatenate([halo[0], mown[...], halo[1]], axis=1)
    band[...] = jnp.zeros_like(band)
    for d in range(3):
        for c in range(3):
            v = SLOT_AT[0, min(c, d), max(c, d)]
            band[9 + d, c : c + 1, :] = full[v : v + 1]
    for delta in range(1, 4):
        base = SLOT_AT[delta, 0, 0]
        moved = pltpu.roll(full, delta, 1)
        for d in range(3):
            for c in range(3):
                v = base + 3 * c + d
                band[3 * (3 + delta) + d, c : c + 1, :] = full[v : v + 1]
                v = base + 3 * d + c
                band[3 * (3 - delta) + d, c : c + 1, :] = moved[v : v + 1]

    def finish_cal():
        arrived(c2r.at[pl.ds(0, last_tm)], 10)
        total = c2r[0]
        for i in range(1, n_tm):
            total = total + c2r[i]
        c3s[...] = total
        cf[sr] = total
        other_src(lambda p: start(c3s, cf.at[sr], 11, (tm, p)))

    pl.when(owner)(finish_cal)

    br[sr] = pb[pl.ds(pl.multiple_of((sr + 1) * 8, 8), 24), :]
    arrived(br.at[pl.ds(0, last_sr)], 4)
    basis[0] = jnp.zeros((8, 384), F32)
    total = br[0]
    for i in range(1, n_src):
        total = total + br[i]
    gt[0:24, :] = total

    def add_other(at):
        arrived(br.at[pl.ds(n_src, n_src)], at)
        total = gt[0:24, :]
        for i in range(n_src):
            total = total + br[n_src + i]
        gt[0:24, :] = total

    trace_row = total[11:12]
    pl.when(has_prev & first)(lambda: add_other(5))
    pl.when(has_next & final)(lambda: add_other(6))
    right = jnp.concatenate([gt[0:8, :], gt[8:16, :], gt[16:24, :]], axis=1)
    basis[1] = jnp.where(iota((8, 384), 0) < 3, right, 0.0)
    mean = jnp.sum(trace_row, axis=1, keepdims=True) * (1.0 / (384 * n_src * n_tm))
    centre = jnp.broadcast_to(mean * 1.2, (8, 384))
    scale = jnp.broadcast_to(2.0 / (mean * 1.1), (8, 384))

    def grow(k, carry):
        x = basis[k + 1]
        y = jnp.zeros((8, 384), F32)
        for delta in range(-3, 4):
            moved = x if delta == 0 else pltpu.roll(x, (-delta) % 384, 1)
            for d in range(3):
                y = y + band[3 * (3 + delta) + d] * moved[d : d + 1]
        image[k] = y[:, 128:256]
        basis[k + 2] = scale * (y - centre * x) - basis[k]
        return carry

    lax.fori_loop(0, CG_ITERS, grow, 0)
    own = [basis[k + 1][:, 128:256] for k in range(CG_ITERS)]
    images = [image[k] for k in range(CG_ITERS)]
    rows = [jnp.sum(own[i] * images[j], axis=0, keepdims=True) for i, j in GRAM_PAIRS]
    rows += [jnp.sum(own[0] * own[i], axis=0, keepdims=True) for i in range(CG_ITERS)]
    for e, row in enumerate(rows):
        gt[e : e + 1, :] = row
    n_gram = len(rows)
    in_gram = iota((32, 128), 0) < n_gram
    same = iota((32, 128), 0) == iota((32, 128), 1)
    sums = jnp.sum(jnp.where(in_gram, gt[...], 0.0), axis=1, keepdims=True)
    gs[0] = jnp.broadcast_to(jnp.sum(jnp.where(same, sums, 0.0), axis=0, keepdims=True), (8, 128))
    g1[sr] = gs[0]
    other_src(lambda p: start(gs.at[0], g1.at[sr], 12, (tm, p)))

    pl.when(owner)(lambda: arrived(cf.at[pl.ds(0, n_own - 1)], 11))
    pl.when(jnp.logical_not(owner))(lambda: arrived(cf, 11))
    packed = jnp.concatenate([cf[i] for i in range(n_own)], axis=0)
    other_half = pltpu.roll(packed, 64, 1)
    for k in range(24):
        size = 24 - 8 * (k // 8)
        at = cal_row(k, 8 * (k // 8))
        part = packed[at : at + size] if k < 8 else other_half[at - 192 : at - 192 + size]
        inv[24 * k + 8 * (k // 8) : 24 * k + 24, :] = part
    for k in range(8, 24):
        size = 8 * (k // 8)
        inv[24 * k : 24 * k + size, :] = inv[pl.ds(k, size, stride=24), :]

    def sweep(j, carry):
        row_of = iota((24, 128), 0)
        column = inv[pl.ds(pl.multiple_of(24 * j, 8), 24), :]
        pivot = jnp.sum(jnp.where(row_of == j, column, 0.0), axis=0, keepdims=True)
        over = 1.0 / pivot
        scaled = column * over
        for k in range(24):
            at = inv[24 * k : 24 * k + 24, :]
            factor = scaled[k : k + 1]
            inv[24 * k : 24 * k + 24, :] = jnp.where(row_of == j, factor, at - factor * column)
        inv[pl.ds(pl.multiple_of(24 * j, 8), 24), :] = jnp.where(row_of == j, -over, scaled)
        return carry

    lax.fori_loop(0, 12, sweep, 0)

    arrived(g1.at[pl.ds(0, last_sr)], 12)
    total = g1[0]
    for i in range(1, n_src):
        total = total + g1[i]
    gs[1] = total
    g2[tm] = total
    other_tm(lambda p: start(gs.at[1], g2.at[tm], 13, (p, sr)))
    lax.fori_loop(12, 24, sweep, 0)
    arrived(g2.at[pl.ds(0, last_tm)], 13)
    total = g2[0]
    for i in range(1, n_tm):
        total = total + g2[i]
    sums = jnp.sum(jnp.where(same, total[0:1], 0.0), axis=1, keepdims=True)
    gt[...] = jnp.broadcast_to(sums, (32, 128))
    gram_at = {pair: e for e, pair in enumerate(GRAM_PAIRS)}
    n_pairs = len(GRAM_PAIRS)

    def gram(i, j):
        e = gram_at[i, j]
        return gt[e : e + 1, :]

    weights, shares = ldl_solve(gram, lambda i: gt[n_pairs + i : n_pairs + i + 1, :], CG_ITERS)
    least = shares[0]
    for value in shares[1:]:
        least = jnp.where(value >= least, least, value)
    trust_ref[...] = jnp.broadcast_to(jnp.where(least > TRUST, 1.0, 0.0), (8, 128))
    answer = weights[0] * own[0]
    for k in range(1, CG_ITERS):
        answer = answer + weights[k] * own[k]
    row = jnp.concatenate([answer[c : c + 1] for c in range(3)], axis=1)
    flat = sum(dot_nn(jnp.broadcast_to(part, (16, 384)), mixed)[0:1] for part in pieces_3(row))
    xm[...] = answer
    for q in range(3):
        xm[3 + q : 4 + q, :] = flat[:, 128 * q : 128 * q + 128]

    def slab_rows(i):
        return xr.at[pl.ds(pl.multiple_of(i * 8, 8), 8)]

    other_src(lambda p: start(xm, slab_rows(sr), 14, (tm, p)))
    pl.when(has_prev & first)(
        lambda: each(n_src, lambda i: start(xm, slab_rows(n_src), 15, (prev_tm, i)))
    )
    xr[pl.ds(pl.multiple_of(sr * 8, 8), 8), :] = xm[...]

    arrived(sub.at[pl.ds(0, last_tm)], 7)
    for p in range(n_tm):
        update_ref[:, lanes * p : lanes * p + lanes] = sub[p, 0:5, :]

    here_3 = jnp.concatenate([here[:n_hi].astype(F32)] * 3 + [jnp.zeros((128 - 3 * n_hi, 128), F32)], axis=0).astype(BF16)
    after_3 = jnp.concatenate([after[:n_hi].astype(F32)] * 3 + [jnp.zeros((128 - 3 * n_hi, 128), F32)], axis=0).astype(BF16)
    arrived(xr.at[pl.ds(0, 8 * last_sr)], 14)
    pl.when(has_next)(lambda: arrived(slab_rows(n_src), 15))
    for q in range(3):
        att_ref[pl.ds(q, n_src, stride=3), :] = xr[pl.ds(3 + q, n_src, stride=8), :]
    resid_b = ra[...]
    for c in range(3):
        parts = [part.astype(F32) for part in pieces_3(xr[pl.ds(c, n_hi, stride=8), :])]
        parts.append(jnp.zeros((128 - 3 * n_hi, 128), F32))
        turned = jnp.concatenate(parts, axis=0).T.astype(BF16)
        at_place = dot_nn(turned, here_3)
        past_place = dot_nn(turned[:16], after_3)[:8]
        for m in range(7):
            value = jnp.sum(jnp.where(inside == m, at_place, 0.0), axis=0, keepdims=True)
            value = value + jnp.sum(jnp.where(past == m, past_place, 0.0), axis=0, keepdims=True)
            resid_b = resid_b - win_ref[3 * m + c].astype(F32) * value

    weighted = w_ref[...] * resid_b
    for k in range(24):
        vrow[k : k + 1, :] = jnp.sum(cal_ref[k].astype(F32) * weighted, axis=0, keepdims=True)
    units = dot_nt(jnp.concatenate(pieces_2(vrow[...]), axis=1), unit_hot_2)
    ks[0, 0:8, :] = jnp.concatenate([units[0:8], units[8:16]], axis=1)
    ks[0, 8:16, :] = jnp.concatenate([units[16:24], jnp.zeros((8, NCU), F32)], axis=1)

    def exchange(buffer, count, me, at, place):
        buffer[me] = ks[at]
        each(
            count - 1,
            lambda d: start(ks.at[at], buffer.at[me], 16 + at, place((me + 1 + d) % count)),
        )
        arrived(buffer.at[pl.ds(0, count - 1)], 16 + at)
        total = buffer[0]
        for i in range(1, count):
            total = total + buffer[i]
        ks[at + 1] = total

    exchange(kz, nz, zz, 0, lambda p: (tm, p * ny + yy))
    exchange(ky, ny, yy, 1, lambda p: (tm, zz * ny + p))
    exchange(kt, n_tm, tm, 2, lambda p: (p, sr))
    total = ks[3]
    right = jnp.concatenate([total[0:8, :NCU], total[0:8, NCU:], total[8:16, :NCU]], axis=0)
    calib = jnp.zeros((24, NCU), F32)
    for j in range(24):
        calib = calib - inv[24 * j : 24 * j + 24, :NCU] * right[j : j + 1]
    calib_ref[...] = calib
    spread = dot_nn(jnp.concatenate(pieces_3(calib), axis=0), unit_hot)
    spread = spread[0:24] + spread[24:48] + spread[48:72]
    out = resid_b
    for k in range(24):
        out = out - cal_ref[k].astype(F32) * spread[k : k + 1]
    resid_ref[...] = out.T

    left_us(vsr.at[pl.ds(0, last_tm)], 0)
    left_us(mr.at[pl.ds(0, last_sr)], 1)
    pl.when(has_next)(lambda: left_us(mr.at[0], 2))
    pl.when(owner)(lambda: left_us(cr.at[pl.ds(0, n_own - 1)], 3))
    pl.when(jnp.logical_not(owner))(lambda: left_us(cr.at[pl.ds(0, n_own)], 3))
    left_us(br.at[pl.ds(0, last_sr)], 4)
    pl.when(has_next)(lambda: left_us(br.at[0], 5))
    pl.when(has_prev)(lambda: left_us(br.at[0], 6))
    left_us(sub.at[pl.ds(0, last_tm)], 7)
    pl.when(has_left)(lambda: left_us(mown, 8))
    pl.when(has_right)(lambda: left_us(mown, 9))
    pl.when(owner)(lambda: left_us(c2r.at[pl.ds(0, last_tm)], 10))
    pl.when(owner)(lambda: left_us(cr.at[pl.ds(0, last_sr)], 11))
    left_us(g1.at[pl.ds(0, last_sr)], 12)
    left_us(g2.at[pl.ds(0, last_tm)], 13)
    left_us(xr.at[pl.ds(0, 8 * last_sr)], 14)
    pl.when(has_prev & first)(lambda: left_us(xr.at[pl.ds(0, 8 * n_src)], 15))
    left_us(kz.at[pl.ds(0, nz - 1)], 16)
    left_us(ky.at[pl.ds(0, ny - 1)], 17)
    left_us(kt.at[pl.ds(0, last_tm)], 18)


def fast_shards(
    n_tm,
    n_src,
    src_deriv,
    att_deriv,
    cal_deriv,
    obs_resid,
    obs_weight,
    src_id,
    tile_knot,
    row_offset,
    cal_unit,
    src_prior,
    att_ridge,
):
    n_hi = (n_src + 1 + 7) // 8 * 8
    groups = src_prior.shape[1]
    lanes = groups // n_tm
    per_own = 24 // min(24, n_src)
    n_own, share = 24 // per_own, 8 * (24 // min(24, n_src))
    ny = min(4, n_src)
    nz = n_src // ny
    src_planes = jnp.transpose(src_deriv, (1, 2, 0))
    att_planes = jnp.transpose(att_deriv, (1, 2, 0))
    cal_planes = jnp.transpose(cal_deriv, (1, 2, 0))
    local_knot = tile_knot - lax.axis_index("tm") * (128 * n_src)
    meta = jnp.stack([src_id, local_knot, cal_unit] + [jnp.zeros_like(src_id)] * 5)
    ridge = att_ridge.reshape(3 * n_src, 128)
    prior = jnp.concatenate([src_prior, jnp.ones((3, groups), F32)], axis=0)

    def f32(*shape):
        return jax.ShapeDtypeStruct(shape, F32)

    def vmem(*shape):
        return pltpu.VMEM(shape, F32)

    whole = pl.BlockSpec(memory_space=pltpu.VMEM)
    win, w, r, vs, mb, cp, po = pl.pallas_call(
        functools.partial(local_kernel, n_src, n_hi),
        out_shape=[
            jax.ShapeDtypeStruct((21, 128, 128), BF16),
            f32(128, 128),
            f32(128, 128),
            f32(24, 128),
            f32(n_hi * MROWS, 128),
            f32(192, 128),
            f32(8, 128),
        ],
        in_specs=[whole] * 9,
        out_specs=[whole] * 7,
        scratch_shapes=[
            vmem(21, 128, 128),
            vmem(5, 128, 128),
            vmem(24, 128, 128),
            pltpu.VMEM((128, 128), jnp.int32),
            vmem(7, MROWS, 128),
            vmem(384, 128),
        ],
        compiler_params=pltpu.CompilerParams(vmem_limit_bytes=48 << 20),
        name="local_normals",
    )(src_planes, att_planes, cal_planes, obs_resid, obs_weight, row_offset, meta, prior, ridge)

    return pl.pallas_call(
        functools.partial(joint_kernel, n_tm, n_src, n_hi),
        out_shape=[f32(5, groups), f32(3 * n_src, 128), f32(24, NCU), f32(128, 128), f32(8, 128)],
        in_specs=[whole] * 12,
        out_specs=[whole] * 5,
        scratch_shapes=[
            vmem(n_tm, 24, 128),
            vmem(2 * n_src, MROWS, 128),
            vmem(MROWS, 128),
            vmem(2, MROWS, 128),
            vmem(21, 8, 384),
            vmem((n_hi + 2) * 8, 128),
            vmem(2 * n_src, 24, 128),
            vmem(CG_ITERS + 2, 8, 384),
            vmem(CG_ITERS, 8, 128),
            vmem(2, 8, 128),
            vmem(n_src, 8, 128),
            vmem(n_tm, 8, 128),
            vmem(32, 128),
            vmem(8, 128),
            vmem(n_hi * 8, 128),
            vmem(n_tm, 8, lanes),
            vmem(n_src, share, 128),
            vmem(share, 128),
            vmem(n_tm, share, 128),
            vmem(share, 128),
            vmem(n_own, share, 128),
            vmem(576, 128),
            vmem(128, 128),
            vmem(24, 128),
            vmem(nz, 16, 128),
            vmem(ny, 16, 128),
            vmem(n_tm, 16, 128),
            vmem(4, 16, 128),
            pltpu.SemaphoreType.DMA((19,)),
            pltpu.SemaphoreType.DMA((19,)),
        ],
        compiler_params=pltpu.CompilerParams(
            collective_id=0, has_side_effects=True, vmem_limit_bytes=48 << 20
        ),
        name="joint_solve",
    )(src_planes, win, cal_planes, w, r, vs, mb, cp, po, meta, prior, ridge)


def guarded_shards(n_tm, n_src, *arrays):
    update, attitude, calib, resid, trust = fast_shards(n_tm, n_src, *arrays)
    fast = (update, attitude.reshape(-1), calib, resid)
    return lax.cond(trust[0, 0] > 0.5, lambda: fast, lambda: shards(*arrays))


def solution(mesh):
    placed = (
        P(("tm", "src"), None, None),
        P(("tm", "src"), None, None),
        P(("tm", "src"), None, None),
        P(("tm", "src"), None),
        P(("tm", "src"), None),
        P(("tm", "src")),
        P(("tm", "src")),
        P(("tm", "src"), None),
        P(("tm", "src")),
        P(None, "src"),
        P("tm"),
    )
    return jax.shard_map(
        functools.partial(guarded_shards, mesh.shape["tm"], mesh.shape["src"]),
        mesh=mesh,
        in_specs=placed,
        out_specs=(P(None, "src"), P("tm"), P(), P(("tm", "src"), None)),
        check_vma=False,
    )
```

```python
import functools

import jax
import jax.numpy as jnp
import numpy as np
from jax import lax
from jax.experimental import pallas as pl
from jax.experimental.pallas import tpu as pltpu
from jax.sharding import PartitionSpec as P

NCU = 64
CG_ITERS = 6


HIGH = lax.Precision.HIGHEST


def padded_2(cells, sides, width):
    for axis, dim in sides:
        count = lax.axis_size(axis)
        ends = count - 1
        head = lax.slice_in_dim(cells, 0, width, axis=dim)
        tail = lax.slice_in_dim(cells, cells.shape[dim] - width, cells.shape[dim], axis=dim)
        cells = jnp.concatenate(
            [
                lax.ppermute(tail, axis, [(i, (i + 1) % count) for i in range(ends)]),
                cells,
                lax.ppermute(head, axis, [((i + 1) % count, i) for i in range(ends)]),
            ],
            axis=dim,
        )
    return cells


def all_sum(array, axis):
    devices, step = lax.axis_size(axis), 1
    while step < devices:
        array = array + lax.ppermute(array, axis, [(i, i ^ step) for i in range(devices)])
        step *= 2
    return array


def from_behind(array, axis, by):
    devices = lax.axis_size(axis)
    pairs = [(i, i + by) for i in range(devices) if 0 <= i + by < devices]
    return lax.ppermute(array, axis, pairs)


def lag_table():
    first_index = np.arange(21)[None, :]
    lag_rows = np.arange(12)[:, None]
    second = first_index + lag_rows
    flat_index = first_index * 21 + np.minimum(second, 20)
    return (flat_index, (second < 21).astype(np.float32))


def solve_spd(matrix, right):
    order = right.shape[0]
    rows = jnp.arange(order)[:, None]

    def column(j, state):
        rest, factor = state
        col = jnp.where(rows >= j, rest[:, j] / jnp.sqrt(rest[j, j]), 0.0)
        return rest - col[:, None, :] * col[None, :, :], factor.at[:, j].set(col)

    factor = lax.fori_loop(0, order, column, (matrix, jnp.zeros_like(matrix)))[1]

    def forward(i, answer):
        value = right[i] - jnp.sum(jnp.where(rows < i, factor[i] * answer, 0.0), axis=0)
        return answer.at[i].set(value / factor[i, i])

    halfway = lax.fori_loop(0, order, forward, jnp.zeros_like(right))

    def backward(step, answer):
        i = order - 1 - step
        value = halfway[i] - jnp.sum(jnp.where(rows > i, factor[:, i] * answer, 0.0), axis=0)
        return answer.at[i].set(value / factor[i, i])

    return lax.fori_loop(0, order, backward, jnp.zeros_like(right))


def tile_normals(deriv, weight, resid):
    values = deriv.astype(jnp.float32)
    weighted = values * weight[:, None, :]
    normal = jnp.einsum("tkr,tlr->tkl", weighted, values, precision=HIGH)
    right = jnp.einsum("tkr,tr->tk", weighted, resid, precision=HIGH)
    return jnp.concatenate([normal.reshape(normal.shape[0], -1), right], axis=1)


def small_solve(sums, prior, order):
    count = sums.shape[1]
    matrix = sums[: order * order].reshape(order, order, count)
    if prior is not None:
        matrix = matrix + jnp.eye(order, dtype=jnp.float32)[:, :, None] * prior[:, None, :]
    return solve_spd(matrix, sums[order * order :])


def window_rows(att_deriv, row_offset):
    values = att_deriv.astype(jnp.float32)
    window = jnp.zeros((values.shape[0], 21, values.shape[2]), jnp.float32)
    for knot_step in range(4):
        placed = jnp.pad(values, ((0, 0), (3 * knot_step, 9 - 3 * knot_step), (0, 0)))
        window = window + jnp.where((row_offset == knot_step)[:, None, :], placed, 0.0)
    return window


def attitude_terms(window, weight, resid):
    weighted = window * weight[:, None, :]
    normal = jnp.einsum("tjr,tlr->tjl", weighted, window, precision=HIGH)
    right = jnp.einsum("tjr,tr->tj", weighted, resid, precision=HIGH)
    flat_index, valid_lag = lag_table()
    banded = normal.reshape(normal.shape[0], 441)[:, flat_index] * valid_lag
    return jnp.concatenate([banded, right[:, None, :]], axis=1)


def conjugate(band_rows, right, ridge_part, band_edge, extend, inner_sum):
    count = right.shape[0]
    lagged = jnp.concatenate([band_edge, band_rows[1:]], axis=1)
    solution = jnp.zeros_like(right)
    residual = right
    direction = right
    norm_now = inner_sum(residual, residual)
    for iteration in range(CG_ITERS):
        padded = extend(direction)
        result = ridge_part * direction
        for d in range(12):
            result = result + band_rows[d] * padded[11 + d : 11 + d + count]
        for d in range(1, 12):
            result = (
                result + lagged[d - 1, 11 - d : 11 - d + count] * padded[11 - d : 11 - d + count]
            )
        step_size = norm_now / inner_sum(direction, result)
        solution = solution + step_size * direction
        residual = residual - step_size * result
        norm_next = inner_sum(residual, residual)
        direction = residual + norm_next / norm_now * direction
        norm_now = norm_next
    return solution


def slab_extend(vector):
    return padded_2(vector, (("tm", 0),), 11)


def slab_dot(first_vec, second_vec):
    return all_sum(jnp.sum(first_vec * second_vec), "tm")


def shards(
    src_deriv,
    att_deriv,
    cal_deriv,
    obs_resid,
    obs_weight,
    src_id,
    tile_knot,
    row_offset,
    cal_unit,
    src_prior,
    att_ridge,
):
    slab_pos = lax.axis_index("tm")
    groups = src_prior.shape[1]
    normal_sums = jax.ops.segment_sum(
        tile_normals(src_deriv, obs_weight, obs_resid), src_id, num_segments=groups
    ).T
    summed = all_sum(normal_sums, "tm")
    source_update = small_solve(summed, src_prior, 5)
    resid_a = obs_resid - jnp.einsum(
        "tkr,kt->tr", src_deriv.astype(jnp.float32), source_update[:, src_id], precision=HIGH
    )
    slab_params = att_ridge.shape[0]
    window = window_rows(att_deriv, row_offset)
    local_knot = tile_knot - slab_pos * (slab_params // 3)
    columns = 3 * local_knot[:, None] + jnp.arange(21, dtype=jnp.int32)[None, :]
    values = attitude_terms(window, obs_weight, resid_a)
    slab_sums = jax.ops.segment_sum(
        values.transpose(0, 2, 1).reshape(-1, 13),
        columns.reshape(-1),
        num_segments=slab_params + 21,
    ).T
    carried = from_behind(slab_sums[:, slab_params:], "tm", 1)
    head_sums = slab_sums[:, :slab_params].at[:, :21].add(carried)
    summed_band = all_sum(head_sums, "src")
    band_edge = from_behind(summed_band[1:12, -11:], "tm", 1)
    attitude_update = conjugate(
        summed_band[:12], summed_band[12], att_ridge, band_edge, slab_extend, slab_dot
    )
    next_params = from_behind(attitude_update[:21], "tm", -1)
    extended = jnp.concatenate([attitude_update, next_params])
    resid_b = resid_a - jnp.einsum("tjr,tj->tr", window, extended[columns], precision=HIGH)
    calib_sums = jax.ops.segment_sum(
        tile_normals(cal_deriv, obs_weight, resid_b), cal_unit, num_segments=NCU
    ).T
    calib_total = all_sum(all_sum(calib_sums, "tm"), "src")
    calib_update = small_solve(calib_total, None, 24)
    residual_out = resid_b - jnp.einsum(
        "tkr,kt->tr", cal_deriv.astype(jnp.float32), calib_update[:, cal_unit], precision=HIGH
    )
    return (source_update, attitude_update, calib_update, residual_out)


F32 = jnp.float32
BF16 = jnp.bfloat16
MESH = pl.DeviceIdType.MESH
MROWS = 32
XROWS = 24
TRUST = 0.01


def pieces_2(x):
    high = x.astype(BF16)
    return high, (x - high.astype(F32)).astype(BF16)


def pieces_3(x):
    high = x.astype(BF16)
    rest = x - high.astype(F32)
    mid = rest.astype(BF16)
    return high, mid, (rest - mid.astype(F32)).astype(BF16)


def dot_nn(a, b):
    return lax.dot_general(a, b, (((1,), (0,)), ((), ())), preferred_element_type=F32)


def dot_nt(a, b):
    return lax.dot_general(a, b, (((1,), (1,)), ((), ())), preferred_element_type=F32)


def iota(shape, dim):
    return lax.broadcasted_iota(jnp.int32, shape, dim)


def hot(match):
    return jnp.where(match, 1.0, 0.0).astype(BF16)


def band_slots():
    slots = [(0, c, d) for c in range(3) for d in range(c, 3)]
    for delta in range(1, 4):
        slots += [(delta, c, d) for c in range(3) for d in range(3)]
    return slots


SLOTS = band_slots()
SLOT_AT = {slot: v for v, slot in enumerate(SLOTS)}
SRC_PAIRS = [(k, l) for k in range(5) for l in range(k, 5)]
SRC_AT = {pair: e for e, pair in enumerate(SRC_PAIRS)}
GRAM_PAIRS = [(i, j) for i in range(CG_ITERS) for j in range(i, CG_ITERS)]


def cal_row(k, l):
    if k < 8:
        return 24 * k + l
    if k < 16:
        return 192 + 16 * (k - 8) + l - 8
    return 320 + 8 * (k - 16) + l - 16


def place_lanes(lo_row):
    inside = iota((128, 128), 0) - lo_row
    return inside, iota((8, 128), 0) + 128 - lo_row


def ldl_solve(entry, right, order):
    low = {}
    pivots, inverse, shares = [], [], []
    for j in range(order):
        pivot = entry(j, j)
        for m in range(j):
            pivot = pivot - low[j, m] * low[j, m] * pivots[m]
        shares.append(pivot / entry(j, j))
        pivots.append(pivot)
        inverse.append(1.0 / pivot)
        for i in range(j + 1, order):
            value = entry(j, i)
            for m in range(j):
                value = value - low[i, m] * (low[j, m] * pivots[m])
            low[i, j] = value * inverse[j]
    forward = []
    for i in range(order):
        value = right(i)
        for m in range(i):
            value = value - low[i, m] * forward[m]
        forward.append(value)
    answer = [None] * order
    for i in range(order - 1, -1, -1):
        value = forward[i] * inverse[i]
        for m in range(i + 1, order):
            value = value - low[m, i] * answer[m]
        answer[i] = value
    return answer, shares


def joint_kernel(
    n_tm,
    n_src,
    n_hi,
    src_ref,
    att_in_ref,
    cal_ref,
    resid_in_ref,
    weight_ref,
    offset_ref,
    meta_ref,
    prior_ref,
    ridge_ref,
    update_ref,
    att_ref,
    calib_ref,
    resid_ref,
    trust_ref,
    winp,
    srcp,
    calp,
    offp,
    w_ref,
    r_ref,
    vm,
    vc,
    vs,
    mb,
    ex,
    cp,
    vsr,
    mr,
    mown,
    halo,
    band,
    pb,
    br,
    basis,
    image,
    gs,
    g1,
    g2,
    gt,
    xm,
    xr,
    sub,
    cr,
    c2s,
    c2r,
    c3s,
    cf,
    inv,
    ra,
    vrow,
    kz,
    ky,
    kt,
    ks,
    send,
    recv,
):
    tm, sr = lax.axis_index("tm"), lax.axis_index("src")
    last_tm, last_sr = n_tm - 1, n_src - 1
    has_next, has_prev = tm < last_tm, tm > 0
    first, final = sr == 0, sr == last_sr
    ny = min(4, n_src)
    nz = n_src // ny
    yy, zz = sr % ny, sr // ny
    per_own = 24 // min(24, n_src)
    n_own = 24 // per_own
    share = 8 * per_own
    owner = sr < n_own
    lanes = prior_ref.shape[1] // n_tm

    def start(source, target, at, place):
        pltpu.make_async_remote_copy(
            src_ref=source,
            dst_ref=target,
            send_sem=send.at[at],
            recv_sem=recv.at[at],
            device_id=place,
            device_id_type=MESH,
        ).start()

    def arrived(part, at):
        pltpu.make_async_copy(part, part, recv.at[at]).wait()

    def left_us(part, at):
        pltpu.make_async_copy(part, part, send.at[at]).wait()

    def each(count, body):
        def run(d, carry):
            body(d)
            return carry

        lax.fori_loop(0, count, run, 0)

    def other_src(body):
        each(last_sr, lambda d: body((sr + 1 + d) % n_src))

    def other_tm(body):
        each(last_tm, lambda d: body((tm + 1 + d) % n_tm))

    halo[...] = jnp.zeros_like(halo)
    xr[...] = jnp.zeros_like(xr)

    barrier = pltpu.get_barrier_semaphore()

    def greet(a, b):
        pl.semaphore_signal(barrier, inc=1, device_id=(a, b), device_id_type=MESH)

    other_tm(lambda p: greet(p, sr))
    other_src(lambda p: greet(tm, p))
    next_tm, prev_tm = jnp.minimum(tm + 1, last_tm), jnp.maximum(tm - 1, 0)
    pl.when(has_next)(lambda: greet(next_tm, 0))
    pl.when(has_prev)(lambda: greet(prev_tm, last_sr))
    pl.when(has_prev & first)(lambda: each(n_src, lambda i: greet(prev_tm, i)))
    pl.when(has_next & final)(lambda: each(n_src, lambda i: greet(next_tm, i)))

    w_ref[...] = weight_ref[...].T
    r_ref[...] = resid_in_ref[...].T
    offp[...] = offset_ref[...].astype(F32).T.astype(jnp.int32)
    vm[...] = jnp.zeros_like(vm)
    pb[...] = jnp.zeros_like(pb)

    def windows(i, carry):
        rows = pl.ds(pl.multiple_of(i * 16, 16), 16)
        values = [att_in_ref[k, rows, :].astype(F32) for k in range(12)]
        step = offp[rows, :]
        for j in range(21):
            placed = jnp.zeros((16, 128), F32)
            for o in range(4):
                if 0 <= j - 3 * o < 12:
                    placed = jnp.where(step == o, values[j - 3 * o], placed)
            winp[j, rows, :] = placed
        for k in range(5):
            srcp[k, rows, :] = src_ref[k, rows, :].astype(F32)
        return carry

    lax.fori_loop(0, 8, windows, 0)

    def summed(count, terms):
        def body(i, sums):
            rows = pl.ds(pl.multiple_of(i * 8, 8), 8)
            return tuple(s + t for s, t in zip(sums, terms(rows)))

        sums = lax.fori_loop(0, 16, body, tuple(jnp.zeros((8, 128), F32) for _ in range(count)))
        return [jnp.sum(s, axis=0, keepdims=True) for s in sums]

    def src_terms(rows):
        x = [srcp[k, rows, :] for k in range(5)]
        w = w_ref[rows, :]
        y = [w * v for v in x]
        r = r_ref[rows, :]
        return [y[k] * x[l] for k, l in SRC_PAIRS] + [v * r for v in y]

    vs[...] = jnp.zeros_like(vs)
    for e, row in enumerate(summed(20, src_terms)):
        vs[e : e + 1, :] = row
    vs[20:21, :] = meta_ref[0:1, :].astype(F32)

    trace = jnp.sum(ridge_ref[...], axis=0, keepdims=True) * (1.0 / n_src)
    for m in range(7):
        slots = [s for s in SLOTS if m + s[0] < 7]

        def att_terms(rows, m=m, slots=slots):
            x = [winp[j, rows, :] for j in range(3 * m, min(3 * m + 12, 21))]
            w = w_ref[rows, :]
            y = [w * x[c] for c in range(3)]
            return [y[c] * x[3 * delta + d] for delta, c, d in slots]

        for slot, row in zip(slots, summed(len(slots), att_terms)):
            vm[m, SLOT_AT[slot] : SLOT_AT[slot] + 1, :] = row
            if slot[0] == 0 and slot[1] == slot[2]:
                trace = trace + row
    vs[21:22, :] = trace

    knot = meta_ref[1:2, :]
    block, place = knot >> 7, knot & 127
    inside, past = place_lanes(place)
    blocks = iota((n_hi + 8, 128), 0)
    here, after = hot(blocks == block), hot(blocks == block + 1)
    spreads = jnp.concatenate([here, here, after, after], axis=1)
    rest = jnp.zeros((120, 128), F32)

    def spread_rows(row_of, count):
        spread = jnp.zeros((128, 128), F32)
        over = jnp.zeros((8, 128), F32)
        for m in range(count):
            row = row_of(m)
            spread = jnp.where(inside == m, row, spread)
            over = jnp.where(past == m, row, over)
        over = jnp.concatenate([over, rest], axis=0)
        right = jnp.concatenate(pieces_2(spread) + pieces_2(over), axis=1)
        return dot_nt(spreads, right)[:n_hi]

    callers = last_tm + last_sr + jnp.where(has_next, 1, 0) + jnp.where(has_prev, 1, 0)
    callers = callers + jnp.where(has_prev & first, n_src, 0) + jnp.where(has_next & final, n_src, 0)
    pl.semaphore_wait(barrier, callers)

    other_tm(lambda p: start(vs, vsr.at[tm], 0, (p, sr)))

    for v, (delta, c, d) in enumerate(SLOTS):
        rows = spread_rows(lambda m, v=v: vm[m, v : v + 1, :], 7 - delta)
        if v < MROWS:
            mb[pl.ds(v, n_hi, stride=MROWS), :] = rows
        else:
            ex[...] = rows

    def band_rows(j):
        return mb.at[pl.ds(pl.multiple_of(j * MROWS, 8), MROWS)]

    other_src(lambda p: start(band_rows(p), mr.at[sr], 1, (tm, p)))
    pl.when(has_next)(lambda: start(band_rows(n_src), mr.at[n_src + sr], 2, (next_tm, 0)))

    def widen(i, carry):
        rows = pl.ds(pl.multiple_of(i * 16, 16), 16)
        for k in range(24):
            calp[k, rows, :] = cal_ref[k, rows, :].astype(F32)
        return carry

    lax.fori_loop(0, 8, widen, 0)
    for kg in range(6):
        for lg in range(kg // 2, 3):

            def cal_terms(rows, kg=kg, lg=lg):
                w = w_ref[rows, :]
                y = [w * calp[4 * kg + k, rows, :] for k in range(4)]
                x = [calp[8 * lg + l, rows, :] for l in range(8)]
                return [y[k] * x[l] for k in range(4) for l in range(8)]

            sums = summed(32, cal_terms)
            for k in range(4):
                at = cal_row(4 * kg + k, 8 * lg)
                vc[at : at + 8, :] = jnp.concatenate(sums[8 * k : 8 * k + 8], axis=0)
    unit_hot = hot(iota((NCU, 128), 0) == meta_ref[2:3, :])
    unit_hot_2 = jnp.concatenate([unit_hot, unit_hot], axis=1)
    units = dot_nt(jnp.concatenate(pieces_2(vc[...]), axis=1), unit_hot_2)
    cp[...] = jnp.concatenate([units[:192], units[192:]], axis=1)

    def cal_share(p):
        return cp.at[pl.ds(pl.multiple_of(p * share, 8), share)]

    def send_cal(p):
        pl.when(p < n_own)(lambda: start(cal_share(p), cr.at[sr], 3, (tm, p)))

    other_src(send_cal)

    ids = jnp.broadcast_to(meta_ref[0:1, :].astype(F32), (128, 128)).T
    sources = (iota((lanes, 128), 0) + tm * lanes).astype(F32)
    wanted = jnp.concatenate([ids, sources], axis=0)
    flat_at, plane_at = iota((384, 384), 1), iota((384, 384), 0)
    mixed = hot(flat_at == 3 * (plane_at & 127) + (plane_at >> 7))
    flat_ridge = jnp.concatenate([ridge_ref[pl.ds(3 * sr + q, 1), :] for q in range(3)], axis=1)
    ridge_row = sum(dot_nt(jnp.broadcast_to(part, (16, 384)), mixed)[0:1] for part in pieces_3(flat_ridge))
    groups = prior_ref.shape[1]
    source_hot = hot(iota((groups, 128), 0) == meta_ref[0:1, :])
    owned = dot_nn(jnp.concatenate(pieces_3(prior_ref[...]), axis=0), source_hot)
    owned = owned[0:8] + owned[8:16] + owned[16:24]

    vsr[tm] = vs[...]
    arrived(vsr.at[pl.ds(0, last_tm)], 0)
    normal = jnp.zeros((48, 128 + lanes), F32)
    for p in range(0, n_tm, 2):
        match = [hot(wanted == vsr[q, 20:21, :]) for q in (p, p + 1)]
        parts = [pieces_2(vsr[q]) for q in (p, p + 1)]
        left = jnp.concatenate([jnp.concatenate([part[i] for part in parts], axis=1) for i in range(2)], axis=0)
        normal = normal + dot_nt(left, jnp.concatenate(match, axis=1))
    normal = normal[:24] + normal[24:]
    trace = sum(vsr[p, 21:22, :] for p in range(n_tm))
    prior = jnp.concatenate([owned, prior_ref[:, pl.ds(pl.multiple_of(tm * lanes, 128), lanes)]], axis=1)

    def source_entry(k, l):
        row = SRC_AT[k, l]
        value = normal[row : row + 1]
        return value + prior[k : k + 1] if k == l else value

    update, _ = ldl_solve(source_entry, lambda k: normal[15 + k : 16 + k], 5)
    resid_a = r_ref[...]
    for k in range(5):
        resid_a = resid_a - srcp[k] * update[k][:, :128]
    ra[...] = resid_a
    weighted = w_ref[...] * resid_a
    for j in range(21):
        vrow[j : j + 1, :] = jnp.sum(winp[j] * weighted, axis=0, keepdims=True)

    lane = iota((n_hi, 128), 1)

    def put_blocks(rows, centre_at, edge_at, extra=None):
        edges = jnp.where(lane < 64, pltpu.roll(rows, n_hi - 1, 0), pltpu.roll(rows, 1, 0))
        if extra is not None:
            edges = jnp.where((lane == 64) & (iota((n_hi, 128), 0) < n_src), extra, edges)
        pb[pl.ds(centre_at, n_hi, stride=8), :] = rows
        pb[pl.ds(edge_at, n_hi, stride=8), :] = edges

    trace = jnp.sum(trace, axis=1, keepdims=True)
    for c in range(3):
        rows = spread_rows(lambda m, c=c: vrow[3 * m + c : 3 * m + c + 1, :], 7)
        put_blocks(rows, c, 3 + c, trace if c == 0 else None)
    put_blocks(ex[...], 6, 7)

    def right_rows(j):
        return pb.at[pl.ds(pl.multiple_of(j * 8, 8), 8)]

    other_src(lambda p: start(right_rows(p), br.at[sr], 4, (tm, p)))
    pl.when(has_next)(lambda: start(right_rows(n_src), br.at[n_src + sr], 5, (next_tm, 0)))
    pl.when(has_prev)(lambda: start(right_rows(n_hi - 1), br.at[n_src + sr], 6, (prev_tm, last_sr)))

    for k in range(5):
        sub[tm, k : k + 1, :] = update[k][:, 128:]
    other_tm(lambda p: start(sub.at[tm], sub.at[tm], 7, (p, sr)))

    mr[sr] = mb[pl.ds(pl.multiple_of(sr * MROWS, 8), MROWS), :]
    arrived(mr.at[pl.ds(0, last_sr)], 1)
    total = mr[0]
    for i in range(1, n_src):
        total = total + mr[i]
    mown[...] = total

    def add_carried():
        arrived(mr.at[pl.ds(n_src, n_src)], 2)
        total = mown[...]
        for i in range(n_src):
            total = total + mr[n_src + i]
        mown[...] = total

    pl.when(has_prev & first)(add_carried)
    for c in range(3):
        v = SLOT_AT[0, c, c]
        mown[v : v + 1, :] = mown[v : v + 1, :] + ridge_row[:, 128 * c : 128 * c + 128]
    lin = tm * n_src + sr
    lower, upper = jnp.maximum(lin - 1, 0), jnp.minimum(lin + 1, n_tm * n_src - 1)
    has_left, has_right = lin > 0, lin < n_tm * n_src - 1
    pl.when(has_left)(lambda: start(mown, halo.at[1], 8, (lower // n_src, lower % n_src)))
    pl.when(has_right)(lambda: start(mown, halo.at[0], 9, (upper // n_src, upper % n_src)))

    def sum_cal():
        cr[sr] = cp[pl.ds(pl.multiple_of(sr * share, 8), share), :]
        arrived(cr.at[pl.ds(0, last_sr)], 3)
        total = cr[0]
        for i in range(1, n_src):
            total = total + cr[i]
        c2s[...] = total
        c2r[tm] = total
        other_tm(lambda p: start(c2s, c2r.at[tm], 10, (p, sr)))

    pl.when(owner)(sum_cal)

    pl.when(has_left)(lambda: arrived(halo.at[0], 9))
    pl.when(has_right)(lambda: arrived(halo.at[1], 8))
    def finish_cal():
        arrived(c2r.at[pl.ds(0, last_tm)], 10)
        total = c2r[0]
        for i in range(1, n_tm):
            total = total + c2r[i]
        c3s[...] = total
        cf[sr] = total
        other_src(lambda p: start(c3s, cf.at[sr], 11, (tm, p)))

    pl.when(owner)(finish_cal)

    br[sr] = pb[pl.ds(pl.multiple_of(sr * 8, 8), 8), :]
    arrived(br.at[pl.ds(0, last_sr)], 4)
    basis[0] = jnp.zeros((8, 384), F32)
    total = br[0]
    for i in range(1, n_src):
        total = total + br[i]
    gt[0:8, :] = total
    trace = total[3:4, 64:65]

    def add_other(at):
        arrived(br.at[pl.ds(n_src, n_src)], at)
        total = gt[0:8, :]
        for i in range(n_src):
            total = total + br[n_src + i]
        gt[0:8, :] = total

    pl.when(has_prev & first)(lambda: add_other(5))
    pl.when(has_next & final)(lambda: add_other(6))
    lane = iota((8, 128), 1)

    def widened(centre, edge):
        return jnp.concatenate([jnp.where(lane >= 110, edge, 0.0), centre, jnp.where(lane < 18, edge, 0.0)], axis=1)

    total = gt[0:8, :]
    edge = jnp.concatenate([total[3:8], total[0:3]], axis=0)
    basis[1] = jnp.where(iota((8, 384), 0) < 3, widened(total, edge), 0.0)
    last = widened(total[6:7] + jnp.zeros((8, 128), F32), total[7:8] + jnp.zeros((8, 128), F32))[0:1]
    full = jnp.concatenate([halo[0], mown[...], halo[1]], axis=1)
    full = jnp.concatenate([full, jnp.broadcast_to(last, (8, 384))], axis=0)
    band[...] = jnp.zeros_like(band)
    for d in range(3):
        for c in range(3):
            v = SLOT_AT[0, min(c, d), max(c, d)]
            band[9 + d, c : c + 1, :] = full[v : v + 1]
    for delta in range(1, 4):
        base = SLOT_AT[delta, 0, 0]
        moved = pltpu.roll(full, delta, 1)
        for d in range(3):
            for c in range(3):
                v = base + 3 * c + d
                band[3 * (3 + delta) + d, c : c + 1, :] = full[v : v + 1]
                v = base + 3 * d + c
                band[3 * (3 - delta) + d, c : c + 1, :] = moved[v : v + 1]

    mean = trace * (1.0 / (384 * n_src * n_tm))
    centre = jnp.broadcast_to(mean * 1.2, (8, 384))
    scale = jnp.broadcast_to(2.0 / (mean * 1.1), (8, 384))

    def grow(k, carry):
        x = basis[k + 1]
        y = jnp.zeros((8, 384), F32)
        for delta in range(-3, 4):
            moved = x if delta == 0 else pltpu.roll(x, (-delta) % 384, 1)
            for d in range(3):
                y = y + band[3 * (3 + delta) + d] * moved[d : d + 1]
        image[k] = y[:, 128:256]
        basis[k + 2] = scale * (y - centre * x) - basis[k]
        return carry

    lax.fori_loop(0, CG_ITERS, grow, 0)
    own = [basis[k + 1][:, 128:256] for k in range(CG_ITERS)]
    images = [image[k] for k in range(CG_ITERS)]
    rows = [jnp.sum(own[i] * images[j], axis=0, keepdims=True) for i, j in GRAM_PAIRS]
    rows += [jnp.sum(own[0] * own[i], axis=0, keepdims=True) for i in range(CG_ITERS)]
    for e, row in enumerate(rows):
        gt[e : e + 1, :] = row
    n_gram = len(rows)
    in_gram = iota((32, 128), 0) < n_gram
    same = iota((32, 128), 0) == iota((32, 128), 1)
    sums = jnp.sum(jnp.where(in_gram, gt[...], 0.0), axis=1, keepdims=True)
    gs[0] = jnp.broadcast_to(jnp.sum(jnp.where(same, sums, 0.0), axis=0, keepdims=True), (8, 128))
    g1[sr] = gs[0]
    other_src(lambda p: start(gs.at[0], g1.at[sr], 12, (tm, p)))
    for k in range(CG_ITERS):
        xm[3 * k : 3 * k + 3, :] = own[k][0:3]

    def slab_rows(i):
        return xr.at[pl.ds(pl.multiple_of(i * XROWS, 8), XROWS)]

    other_src(lambda p: start(xm, slab_rows(sr), 14, (tm, p)))
    pl.when(has_prev & first)(
        lambda: each(n_src, lambda i: start(xm, slab_rows(n_src), 15, (prev_tm, i)))
    )
    xr[pl.ds(pl.multiple_of(sr * XROWS, 8), XROWS), :] = xm[...]

    pl.when(owner)(lambda: arrived(cf.at[pl.ds(0, n_own - 1)], 11))
    pl.when(jnp.logical_not(owner))(lambda: arrived(cf, 11))
    packed = jnp.concatenate([cf[i] for i in range(n_own)], axis=0)
    other_half = pltpu.roll(packed, 64, 1)
    for k in range(24):
        size = 24 - 8 * (k // 8)
        at = cal_row(k, 8 * (k // 8))
        part = packed[at : at + size] if k < 8 else other_half[at - 192 : at - 192 + size]
        inv[24 * k + 8 * (k // 8) : 24 * k + 24, :] = part
    for k in range(8, 24):
        size = 8 * (k // 8)
        inv[24 * k : 24 * k + size, :] = inv[pl.ds(k, size, stride=24), :]

    def sweep(j, carry):
        row_of = iota((24, 128), 0)
        column = inv[pl.ds(pl.multiple_of(24 * j, 8), 24), :]
        pivot = jnp.sum(jnp.where(row_of == j, column, 0.0), axis=0, keepdims=True)
        over = 1.0 / pivot
        scaled = column * over
        for k in range(24):
            at = inv[24 * k : 24 * k + 24, :]
            factor = scaled[k : k + 1]
            inv[24 * k : 24 * k + 24, :] = jnp.where(row_of == j, factor, at - factor * column)
        inv[pl.ds(pl.multiple_of(24 * j, 8), 24), :] = jnp.where(row_of == j, -over, scaled)
        return carry

    lax.fori_loop(0, 12, sweep, 0)

    arrived(g1.at[pl.ds(0, last_sr)], 12)
    total = g1[0]
    for i in range(1, n_src):
        total = total + g1[i]
    gs[1] = total
    g2[tm] = total
    other_tm(lambda p: start(gs.at[1], g2.at[tm], 13, (p, sr)))
    lax.fori_loop(12, 24, sweep, 0)
    arrived(g2.at[pl.ds(0, last_tm)], 13)
    total = g2[0]
    for i in range(1, n_tm):
        total = total + g2[i]
    sums = jnp.sum(jnp.where(same, total[0:1], 0.0), axis=1, keepdims=True)
    gt[...] = jnp.broadcast_to(sums, (32, 128))
    gram_at = {pair: e for e, pair in enumerate(GRAM_PAIRS)}
    n_pairs = len(GRAM_PAIRS)

    def gram(i, j):
        e = gram_at[i, j]
        return gt[e : e + 1, :]

    weights, shares = ldl_solve(gram, lambda i: gt[n_pairs + i : n_pairs + i + 1, :], CG_ITERS)
    least = shares[0]
    for value in shares[1:]:
        least = jnp.where(value >= least, least, value)
    trust_ref[...] = jnp.broadcast_to(jnp.where(least > TRUST, 1.0, 0.0), (8, 128))
    arrived(sub.at[pl.ds(0, last_tm)], 7)
    for p in range(n_tm):
        update_ref[:, lanes * p : lanes * p + lanes] = sub[p, 0:5, :]

    here_3 = jnp.concatenate([here[:n_hi].astype(F32)] * 3 + [jnp.zeros((128 - 3 * n_hi, 128), F32)], axis=0).astype(BF16)
    after_3 = jnp.concatenate([after[:n_hi].astype(F32)] * 3 + [jnp.zeros((128 - 3 * n_hi, 128), F32)], axis=0).astype(BF16)
    arrived(xr.at[pl.ds(0, XROWS * last_sr)], 14)
    pl.when(has_next)(lambda: arrived(slab_rows(n_src), 15))
    resid_b = ra[...]
    planes = []
    for c in range(3):
        plane = weights[0] * xr[pl.ds(c, n_hi, stride=XROWS), :]
        for k in range(1, CG_ITERS):
            plane = plane + weights[k] * xr[pl.ds(3 * k + c, n_hi, stride=XROWS), :]
        planes.append(plane)
        parts = [part.astype(F32) for part in pieces_3(plane)]
        parts.append(jnp.zeros((128 - 3 * n_hi, 128), F32))
        turned = jnp.concatenate(parts, axis=0).T.astype(BF16)
        at_place = dot_nn(turned, here_3)
        past_place = dot_nn(turned[:16], after_3)[:8]
        for m in range(7):
            value = jnp.sum(jnp.where(inside == m, at_place, 0.0), axis=0, keepdims=True)
            value = value + jnp.sum(jnp.where(past == m, past_place, 0.0), axis=0, keepdims=True)
            resid_b = resid_b - winp[3 * m + c] * value

    weighted = w_ref[...] * resid_b
    for k in range(24):
        vrow[k : k + 1, :] = jnp.sum(calp[k] * weighted, axis=0, keepdims=True)
    units = dot_nt(jnp.concatenate(pieces_2(vrow[...]), axis=1), unit_hot_2)
    ks[0, 0:8, :] = jnp.concatenate([units[0:8], units[8:16]], axis=1)
    ks[0, 8:16, :] = jnp.concatenate([units[16:24], jnp.zeros((8, NCU), F32)], axis=1)

    def exchange(buffer, count, me, at, place, beside=None):
        buffer[me] = ks[at]
        each(
            count - 1,
            lambda d: start(ks.at[at], buffer.at[me], 16 + at, place((me + 1 + d) % count)),
        )
        if beside is not None:
            beside()
        arrived(buffer.at[pl.ds(0, count - 1)], 16 + at)
        total = buffer[0]
        for i in range(1, count):
            total = total + buffer[i]
        ks[at + 1] = total

    def write_attitude():
        slab = jnp.concatenate(planes, axis=1)
        flat = dot_nn(jnp.concatenate(pieces_3(slab), axis=0), mixed)
        flat = flat[:n_hi] + flat[n_hi : 2 * n_hi] + flat[2 * n_hi :]
        for q in range(3):
            att_ref[pl.ds(q, n_src, stride=3), :] = flat[:n_src, 128 * q : 128 * q + 128]

    exchange(kz, nz, zz, 0, lambda p: (tm, p * ny + yy), write_attitude)
    exchange(ky, ny, yy, 1, lambda p: (tm, zz * ny + p))
    exchange(kt, n_tm, tm, 2, lambda p: (p, sr))
    total = ks[3]
    right = jnp.concatenate([total[0:8, :NCU], total[0:8, NCU:], total[8:16, :NCU]], axis=0)
    calib = jnp.zeros((24, NCU), F32)
    for j in range(24):
        calib = calib - inv[24 * j : 24 * j + 24, :NCU] * right[j : j + 1]
    calib_ref[...] = calib
    spread = dot_nn(jnp.concatenate(pieces_3(calib), axis=0), unit_hot)
    spread = spread[0:24] + spread[24:48] + spread[48:72]
    out = resid_b
    for k in range(24):
        out = out - calp[k] * spread[k : k + 1]
    resid_ref[...] = out.T

    left_us(vsr.at[pl.ds(0, last_tm)], 0)
    left_us(mr.at[pl.ds(0, last_sr)], 1)
    pl.when(has_next)(lambda: left_us(mr.at[0], 2))
    pl.when(owner)(lambda: left_us(cr.at[pl.ds(0, n_own - 1)], 3))
    pl.when(jnp.logical_not(owner))(lambda: left_us(cr.at[pl.ds(0, n_own)], 3))
    left_us(br.at[pl.ds(0, last_sr)], 4)
    pl.when(has_next)(lambda: left_us(br.at[0], 5))
    pl.when(has_prev)(lambda: left_us(br.at[0], 6))
    left_us(sub.at[pl.ds(0, last_tm)], 7)
    pl.when(has_left)(lambda: left_us(mown, 8))
    pl.when(has_right)(lambda: left_us(mown, 9))
    pl.when(owner)(lambda: left_us(c2r.at[pl.ds(0, last_tm)], 10))
    pl.when(owner)(lambda: left_us(cr.at[pl.ds(0, last_sr)], 11))
    left_us(g1.at[pl.ds(0, last_sr)], 12)
    left_us(g2.at[pl.ds(0, last_tm)], 13)
    left_us(xr.at[pl.ds(0, XROWS * last_sr)], 14)
    pl.when(has_prev & first)(lambda: left_us(xr.at[pl.ds(0, XROWS * n_src)], 15))
    left_us(kz.at[pl.ds(0, nz - 1)], 16)
    left_us(ky.at[pl.ds(0, ny - 1)], 17)
    left_us(kt.at[pl.ds(0, last_tm)], 18)


def fast_shards(
    n_tm,
    n_src,
    src_deriv,
    att_deriv,
    cal_deriv,
    obs_resid,
    obs_weight,
    src_id,
    tile_knot,
    row_offset,
    cal_unit,
    src_prior,
    att_ridge,
):
    n_hi = (n_src + 1 + 7) // 8 * 8
    groups = src_prior.shape[1]
    lanes = groups // n_tm
    per_own = 24 // min(24, n_src)
    n_own, share = 24 // per_own, 8 * (24 // min(24, n_src))
    ny = min(4, n_src)
    nz = n_src // ny
    src_planes = jnp.transpose(src_deriv, (1, 2, 0))
    att_planes = jnp.transpose(att_deriv, (1, 2, 0))
    cal_planes = jnp.transpose(cal_deriv, (1, 2, 0))
    local_knot = tile_knot - lax.axis_index("tm") * (128 * n_src)
    meta = jnp.stack([src_id, local_knot, cal_unit] + [jnp.zeros_like(src_id)] * 5)
    ridge = att_ridge.reshape(3 * n_src, 128)
    prior = jnp.concatenate([src_prior, jnp.ones((3, groups), F32)], axis=0)

    def f32(*shape):
        return jax.ShapeDtypeStruct(shape, F32)

    def vmem(*shape):
        return pltpu.VMEM(shape, F32)

    whole = pl.BlockSpec(memory_space=pltpu.VMEM)
    return pl.pallas_call(
        functools.partial(joint_kernel, n_tm, n_src, n_hi),
        out_shape=[f32(5, groups), f32(3 * n_src, 128), f32(24, NCU), f32(128, 128), f32(8, 128)],
        in_specs=[whole] * 9,
        out_specs=[whole] * 5,
        scratch_shapes=[
            vmem(21, 128, 128),
            vmem(5, 128, 128),
            vmem(24, 128, 128),
            pltpu.VMEM((128, 128), jnp.int32),
            vmem(128, 128),
            vmem(128, 128),
            vmem(7, MROWS + 8, 128),
            vmem(384, 128),
            vmem(24, 128),
            vmem(n_hi * MROWS, 128),
            vmem(n_hi, 128),
            vmem(192, 128),
            vmem(n_tm, 24, 128),
            vmem(2 * n_src, MROWS, 128),
            vmem(MROWS, 128),
            vmem(2, MROWS, 128),
            vmem(21, 8, 384),
            vmem(n_hi * 8, 128),
            vmem(2 * n_src, 8, 128),
            vmem(CG_ITERS + 2, 8, 384),
            vmem(CG_ITERS, 8, 128),
            vmem(2, 8, 128),
            vmem(n_src, 8, 128),
            vmem(n_tm, 8, 128),
            vmem(32, 128),
            vmem(XROWS, 128),
            vmem(n_hi * XROWS, 128),
            vmem(n_tm, 8, lanes),
            vmem(n_src, share, 128),
            vmem(share, 128),
            vmem(n_tm, share, 128),
            vmem(share, 128),
            vmem(n_own, share, 128),
            vmem(576, 128),
            vmem(128, 128),
            vmem(24, 128),
            vmem(nz, 16, 128),
            vmem(ny, 16, 128),
            vmem(n_tm, 16, 128),
            vmem(4, 16, 128),
            pltpu.SemaphoreType.DMA((19,)),
            pltpu.SemaphoreType.DMA((19,)),
        ],
        compiler_params=pltpu.CompilerParams(
            collective_id=0, has_side_effects=True, vmem_limit_bytes=48 << 20
        ),
        name="joint_solve",
    )(src_planes, att_planes, cal_planes, obs_resid, obs_weight, row_offset, meta, prior, ridge)


def guarded_shards(n_tm, n_src, *arrays):
    update, attitude, calib, resid, trust = fast_shards(n_tm, n_src, *arrays)
    fast = (update, attitude.reshape(-1), calib, resid)
    return lax.cond(trust[0, 0] > 0.5, lambda: fast, lambda: shards(*arrays))


def solution(mesh):
    placed = (
        P(("tm", "src"), None, None),
        P(("tm", "src"), None, None),
        P(("tm", "src"), None, None),
        P(("tm", "src"), None),
        P(("tm", "src"), None),
        P(("tm", "src")),
        P(("tm", "src")),
        P(("tm", "src"), None),
        P(("tm", "src")),
        P(None, "src"),
        P("tm"),
    )
    return jax.shard_map(
        functools.partial(guarded_shards, mesh.shape["tm"], mesh.shape["src"]),
        mesh=mesh,
        in_specs=placed,
        out_specs=(P(None, "src"), P("tm"), P(), P(("tm", "src"), None)),
        check_vma=False,
    )
```

```python
import functools

import jax
import jax.numpy as jnp
import numpy as np
from jax import lax
from jax.experimental import pallas as pl
from jax.experimental.pallas import tpu as pltpu
from jax.sharding import PartitionSpec as P

NCU = 64
CG_ITERS = 6


HIGH = lax.Precision.HIGHEST


def padded_2(cells, sides, width):
    for axis, dim in sides:
        count = lax.axis_size(axis)
        ends = count - 1
        head = lax.slice_in_dim(cells, 0, width, axis=dim)
        tail = lax.slice_in_dim(cells, cells.shape[dim] - width, cells.shape[dim], axis=dim)
        cells = jnp.concatenate(
            [
                lax.ppermute(tail, axis, [(i, (i + 1) % count) for i in range(ends)]),
                cells,
                lax.ppermute(head, axis, [((i + 1) % count, i) for i in range(ends)]),
            ],
            axis=dim,
        )
    return cells


def all_sum(array, axis):
    devices, step = lax.axis_size(axis), 1
    while step < devices:
        array = array + lax.ppermute(array, axis, [(i, i ^ step) for i in range(devices)])
        step *= 2
    return array


def from_behind(array, axis, by):
    devices = lax.axis_size(axis)
    pairs = [(i, i + by) for i in range(devices) if 0 <= i + by < devices]
    return lax.ppermute(array, axis, pairs)


def lag_table():
    first_index = np.arange(21)[None, :]
    lag_rows = np.arange(12)[:, None]
    second = first_index + lag_rows
    flat_index = first_index * 21 + np.minimum(second, 20)
    return (flat_index, (second < 21).astype(np.float32))


def solve_spd(matrix, right):
    order = right.shape[0]
    rows = jnp.arange(order)[:, None]

    def column(j, state):
        rest, factor = state
        col = jnp.where(rows >= j, rest[:, j] / jnp.sqrt(rest[j, j]), 0.0)
        return rest - col[:, None, :] * col[None, :, :], factor.at[:, j].set(col)

    factor = lax.fori_loop(0, order, column, (matrix, jnp.zeros_like(matrix)))[1]

    def forward(i, answer):
        value = right[i] - jnp.sum(jnp.where(rows < i, factor[i] * answer, 0.0), axis=0)
        return answer.at[i].set(value / factor[i, i])

    halfway = lax.fori_loop(0, order, forward, jnp.zeros_like(right))

    def backward(step, answer):
        i = order - 1 - step
        value = halfway[i] - jnp.sum(jnp.where(rows > i, factor[:, i] * answer, 0.0), axis=0)
        return answer.at[i].set(value / factor[i, i])

    return lax.fori_loop(0, order, backward, jnp.zeros_like(right))


def tile_normals(deriv, weight, resid):
    values = deriv.astype(jnp.float32)
    weighted = values * weight[:, None, :]
    normal = jnp.einsum("tkr,tlr->tkl", weighted, values, precision=HIGH)
    right = jnp.einsum("tkr,tr->tk", weighted, resid, precision=HIGH)
    return jnp.concatenate([normal.reshape(normal.shape[0], -1), right], axis=1)


def small_solve(sums, prior, order):
    count = sums.shape[1]
    matrix = sums[: order * order].reshape(order, order, count)
    if prior is not None:
        matrix = matrix + jnp.eye(order, dtype=jnp.float32)[:, :, None] * prior[:, None, :]
    return solve_spd(matrix, sums[order * order :])


def window_rows(att_deriv, row_offset):
    values = att_deriv.astype(jnp.float32)
    window = jnp.zeros((values.shape[0], 21, values.shape[2]), jnp.float32)
    for knot_step in range(4):
        placed = jnp.pad(values, ((0, 0), (3 * knot_step, 9 - 3 * knot_step), (0, 0)))
        window = window + jnp.where((row_offset == knot_step)[:, None, :], placed, 0.0)
    return window


def attitude_terms(window, weight, resid):
    weighted = window * weight[:, None, :]
    normal = jnp.einsum("tjr,tlr->tjl", weighted, window, precision=HIGH)
    right = jnp.einsum("tjr,tr->tj", weighted, resid, precision=HIGH)
    flat_index, valid_lag = lag_table()
    banded = normal.reshape(normal.shape[0], 441)[:, flat_index] * valid_lag
    return jnp.concatenate([banded, right[:, None, :]], axis=1)


def conjugate(band_rows, right, ridge_part, band_edge, extend, inner_sum):
    count = right.shape[0]
    lagged = jnp.concatenate([band_edge, band_rows[1:]], axis=1)
    solution = jnp.zeros_like(right)
    residual = right
    direction = right
    norm_now = inner_sum(residual, residual)
    for iteration in range(CG_ITERS):
        padded = extend(direction)
        result = ridge_part * direction
        for d in range(12):
            result = result + band_rows[d] * padded[11 + d : 11 + d + count]
        for d in range(1, 12):
            result = (
                result + lagged[d - 1, 11 - d : 11 - d + count] * padded[11 - d : 11 - d + count]
            )
        step_size = norm_now / inner_sum(direction, result)
        solution = solution + step_size * direction
        residual = residual - step_size * result
        norm_next = inner_sum(residual, residual)
        direction = residual + norm_next / norm_now * direction
        norm_now = norm_next
    return solution


def slab_extend(vector):
    return padded_2(vector, (("tm", 0),), 11)


def slab_dot(first_vec, second_vec):
    return all_sum(jnp.sum(first_vec * second_vec), "tm")


def shards(
    src_deriv,
    att_deriv,
    cal_deriv,
    obs_resid,
    obs_weight,
    src_id,
    tile_knot,
    row_offset,
    cal_unit,
    src_prior,
    att_ridge,
):
    slab_pos = lax.axis_index("tm")
    groups = src_prior.shape[1]
    normal_sums = jax.ops.segment_sum(
        tile_normals(src_deriv, obs_weight, obs_resid), src_id, num_segments=groups
    ).T
    summed = all_sum(normal_sums, "tm")
    source_update = small_solve(summed, src_prior, 5)
    resid_a = obs_resid - jnp.einsum(
        "tkr,kt->tr", src_deriv.astype(jnp.float32), source_update[:, src_id], precision=HIGH
    )
    slab_params = att_ridge.shape[0]
    window = window_rows(att_deriv, row_offset)
    local_knot = tile_knot - slab_pos * (slab_params // 3)
    columns = 3 * local_knot[:, None] + jnp.arange(21, dtype=jnp.int32)[None, :]
    values = attitude_terms(window, obs_weight, resid_a)
    slab_sums = jax.ops.segment_sum(
        values.transpose(0, 2, 1).reshape(-1, 13),
        columns.reshape(-1),
        num_segments=slab_params + 21,
    ).T
    carried = from_behind(slab_sums[:, slab_params:], "tm", 1)
    head_sums = slab_sums[:, :slab_params].at[:, :21].add(carried)
    summed_band = all_sum(head_sums, "src")
    band_edge = from_behind(summed_band[1:12, -11:], "tm", 1)
    attitude_update = conjugate(
        summed_band[:12], summed_band[12], att_ridge, band_edge, slab_extend, slab_dot
    )
    next_params = from_behind(attitude_update[:21], "tm", -1)
    extended = jnp.concatenate([attitude_update, next_params])
    resid_b = resid_a - jnp.einsum("tjr,tj->tr", window, extended[columns], precision=HIGH)
    calib_sums = jax.ops.segment_sum(
        tile_normals(cal_deriv, obs_weight, resid_b), cal_unit, num_segments=NCU
    ).T
    calib_total = all_sum(all_sum(calib_sums, "tm"), "src")
    calib_update = small_solve(calib_total, None, 24)
    residual_out = resid_b - jnp.einsum(
        "tkr,kt->tr", cal_deriv.astype(jnp.float32), calib_update[:, cal_unit], precision=HIGH
    )
    return (source_update, attitude_update, calib_update, residual_out)


F32 = jnp.float32
BF16 = jnp.bfloat16
MESH = pl.DeviceIdType.MESH
MROWS = 32
XROWS = 24
TRUST = 0.01


def pieces_2(x):
    high = x.astype(BF16)
    return high, (x - high.astype(F32)).astype(BF16)


def pieces_3(x):
    high = x.astype(BF16)
    rest = x - high.astype(F32)
    mid = rest.astype(BF16)
    return high, mid, (rest - mid.astype(F32)).astype(BF16)


def dot_nn(a, b):
    return lax.dot_general(a, b, (((1,), (0,)), ((), ())), preferred_element_type=F32)


def dot_nt(a, b):
    return lax.dot_general(a, b, (((1,), (1,)), ((), ())), preferred_element_type=F32)


def iota(shape, dim):
    return lax.broadcasted_iota(jnp.int32, shape, dim)


def hot(match):
    return jnp.where(match, 1.0, 0.0).astype(BF16)


def band_slots():
    slots = [(0, c, d) for c in range(3) for d in range(c, 3)]
    for delta in range(1, 4):
        slots += [(delta, c, d) for c in range(3) for d in range(3)]
    return slots


SLOTS = band_slots()
SLOT_AT = {slot: v for v, slot in enumerate(SLOTS)}
SRC_PAIRS = [(k, l) for k in range(5) for l in range(k, 5)]
SRC_AT = {pair: e for e, pair in enumerate(SRC_PAIRS)}
GRAM_PAIRS = [(i, j) for i in range(CG_ITERS) for j in range(i, CG_ITERS)]


def cal_row(k, l):
    if k < 8:
        return 24 * k + l
    if k < 16:
        return 192 + 16 * (k - 8) + l - 8
    return 320 + 8 * (k - 16) + l - 16


def place_lanes(lo_row):
    inside = iota((128, 128), 0) - lo_row
    return inside, iota((8, 128), 0) + 128 - lo_row


def ldl_solve(entry, right, order):
    low = {}
    pivots, inverse, shares = [], [], []
    for j in range(order):
        pivot = entry(j, j)
        for m in range(j):
            pivot = pivot - low[j, m] * low[j, m] * pivots[m]
        shares.append(pivot / entry(j, j))
        pivots.append(pivot)
        inverse.append(1.0 / pivot)
        for i in range(j + 1, order):
            value = entry(j, i)
            for m in range(j):
                value = value - low[i, m] * (low[j, m] * pivots[m])
            low[i, j] = value * inverse[j]
    forward = []
    for i in range(order):
        value = right(i)
        for m in range(i):
            value = value - low[i, m] * forward[m]
        forward.append(value)
    answer = [None] * order
    for i in range(order - 1, -1, -1):
        value = forward[i] * inverse[i]
        for m in range(i + 1, order):
            value = value - low[m, i] * answer[m]
        answer[i] = value
    return answer, shares


def joint_kernel(
    n_tm,
    n_src,
    n_hi,
    src_ref,
    att_in_ref,
    cal_ref,
    resid_in_ref,
    weight_ref,
    offset_ref,
    id_ref,
    knot_ref,
    unit_ref,
    raw_prior_ref,
    ridge_ref,
    update_ref,
    att_ref,
    calib_ref,
    resid_ref,
    trust_ref,
    prior_ref,
    winp,
    srcp,
    attp,
    calp,
    calf,
    offp,
    w_ref,
    r_ref,
    vm,
    vc,
    vs,
    mb,
    ex,
    cp,
    vsr,
    mr,
    mown,
    halo,
    band,
    pb,
    br,
    basis,
    image,
    gs,
    g1,
    g2,
    gt,
    xm,
    xr,
    sub,
    cr,
    c2s,
    c2r,
    c3s,
    cf,
    inv,
    ra,
    vrow,
    kz,
    ky,
    kt,
    ks,
    send,
    recv,
):
    tm, sr = lax.axis_index("tm"), lax.axis_index("src")
    last_tm, last_sr = n_tm - 1, n_src - 1
    has_next, has_prev = tm < last_tm, tm > 0
    first, final = sr == 0, sr == last_sr
    ny = min(4, n_src)
    nz = n_src // ny
    yy, zz = sr % ny, sr // ny
    per_own = 24 // min(24, n_src)
    n_own = 24 // per_own
    share = 8 * per_own
    owner = sr < n_own
    lanes = prior_ref.shape[1] // n_tm

    def start(source, target, at, place):
        pltpu.make_async_remote_copy(
            src_ref=source,
            dst_ref=target,
            send_sem=send.at[at],
            recv_sem=recv.at[at],
            device_id=place,
            device_id_type=MESH,
        ).start()

    def arrived(part, at):
        pltpu.make_async_copy(part, part, recv.at[at]).wait()

    def left_us(part, at):
        pltpu.make_async_copy(part, part, send.at[at]).wait()

    def each(count, body):
        def run(d, carry):
            body(d)
            return carry

        lax.fori_loop(0, count, run, 0)

    def other_src(body):
        each(last_sr, lambda d: body((sr + 1 + d) % n_src))

    def other_tm(body):
        each(last_tm, lambda d: body((tm + 1 + d) % n_tm))

    next_tm, prev_tm = jnp.minimum(tm + 1, last_tm), jnp.maximum(tm - 1, 0)
    halo[...] = jnp.zeros_like(halo)
    xr[XROWS * n_src :, :] = jnp.zeros((XROWS * (n_hi - n_src), 128), F32)

    barrier = pltpu.get_barrier_semaphore()

    def greet(a, b):
        pl.semaphore_signal(barrier, inc=1, device_id=(a, b), device_id_type=MESH)

    other_tm(lambda p: greet(p, sr))
    other_src(lambda p: greet(tm, p))

    w_ref[...] = weight_ref[...].T
    r_ref[...] = resid_in_ref[...].T
    offp[...] = offset_ref[...].astype(F32).T.astype(jnp.int32)
    for k in range(5):
        srcp[k] = src_ref[k].astype(F32)
    for k in range(12):
        attp[k] = att_in_ref[k].astype(F32)
    vm[...] = jnp.zeros_like(vm)
    prior_ref[...] = jnp.ones_like(prior_ref)
    prior_ref[0:5, :] = raw_prior_ref[...]
    pb[...] = jnp.zeros_like(pb)

    def windows(i, carry):
        rows = pl.ds(pl.multiple_of(i * 16, 16), 16)
        values = [attp[k, rows, :] for k in range(12)]
        step = offp[rows, :]
        for j in range(21):
            placed = jnp.zeros((16, 128), F32)
            for o in range(4):
                if 0 <= j - 3 * o < 12:
                    placed = jnp.where(step == o, values[j - 3 * o], placed)
            winp[j, rows, :] = placed
        return carry

    lax.fori_loop(0, 8, windows, 0)

    def summed(count, terms):
        def body(i, sums):
            rows = pl.ds(pl.multiple_of(i * 8, 8), 8)
            return tuple(s + t for s, t in zip(sums, terms(rows)))

        sums = lax.fori_loop(0, 16, body, tuple(jnp.zeros((8, 128), F32) for _ in range(count)))
        return [jnp.sum(s, axis=0, keepdims=True) for s in sums]

    def src_terms(rows):
        x = [srcp[k, rows, :] for k in range(5)]
        w = w_ref[rows, :]
        y = [w * v for v in x]
        r = r_ref[rows, :]
        return [y[k] * x[l] for k, l in SRC_PAIRS] + [v * r for v in y]

    vs[...] = jnp.zeros_like(vs)
    for e, row in enumerate(summed(20, src_terms)):
        vs[e : e + 1, :] = row
    vs[20:21, :] = id_ref[...].astype(F32)

    trace = jnp.sum(ridge_ref[...], axis=0, keepdims=True) * (1.0 / n_src)
    for m in range(7):
        slots = [s for s in SLOTS if m + s[0] < 7]

        def att_terms(rows, m=m, slots=slots):
            x = [winp[j, rows, :] for j in range(3 * m, min(3 * m + 12, 21))]
            w = w_ref[rows, :]
            y = [w * x[c] for c in range(3)]
            return [y[c] * x[3 * delta + d] for delta, c, d in slots]

        for slot, row in zip(slots, summed(len(slots), att_terms)):
            vm[m, SLOT_AT[slot] : SLOT_AT[slot] + 1, :] = row
            if slot[0] == 0 and slot[1] == slot[2]:
                trace = trace + row
    vs[21:22, :] = trace

    knot = knot_ref[...] - tm * (128 * n_src)
    block, place = knot >> 7, knot & 127
    inside, past = place_lanes(place)
    blocks = iota((n_hi + 8, 128), 0)
    here, after = hot(blocks == block), hot(blocks == block + 1)
    spreads = jnp.concatenate([here, here, after, after], axis=1)
    rest = jnp.zeros((120, 128), F32)

    def spread_rows(row_of, count):
        spread = jnp.zeros((128, 128), F32)
        over = jnp.zeros((8, 128), F32)
        for m in range(count):
            row = row_of(m)
            spread = jnp.where(inside == m, row, spread)
            over = jnp.where(past == m, row, over)
        over = jnp.concatenate([over, rest], axis=0)
        right = jnp.concatenate(pieces_2(spread) + pieces_2(over), axis=1)
        return dot_nt(spreads, right)[:n_hi]

    for v, (delta, c, d) in enumerate(SLOTS):
        rows = spread_rows(lambda m, v=v: vm[m, v : v + 1, :], 7 - delta)
        if v < MROWS:
            mb[pl.ds(v, n_hi, stride=MROWS), :] = rows
        else:
            ex[...] = rows

    def band_rows(j):
        return mb.at[pl.ds(pl.multiple_of(j * MROWS, 8), MROWS)]

    ids = jnp.broadcast_to(id_ref[...].astype(F32), (128, 128)).T
    sources = (iota((lanes, 128), 0) + tm * lanes).astype(F32)
    wanted = jnp.concatenate([ids, sources], axis=0)
    groups = prior_ref.shape[1]
    source_hot = hot(iota((groups, 128), 0) == id_ref[...])
    owned = dot_nn(jnp.concatenate(pieces_3(prior_ref[...]), axis=0), source_hot)
    owned = owned[0:8] + owned[8:16] + owned[16:24]

    pl.semaphore_wait(barrier, last_tm + last_sr)
    other_tm(lambda p: start(vs, vsr.at[tm], 0, (p, sr)))
    other_src(lambda p: start(band_rows(p), mr.at[sr], 1, (tm, p)))

    vsr[tm] = vs[...]
    arrived(vsr.at[pl.ds(0, last_tm)], 0)
    pl.when(has_next)(lambda: start(band_rows(n_src), mr.at[n_src + sr], 2, (next_tm, 0)))
    normal = jnp.zeros((48, 128 + lanes), F32)
    for p in range(0, n_tm, 2):
        match = [hot(wanted == vsr[q, 20:21, :]) for q in (p, p + 1)]
        parts = [pieces_2(vsr[q]) for q in (p, p + 1)]
        left = jnp.concatenate([jnp.concatenate([part[i] for part in parts], axis=1) for i in range(2)], axis=0)
        normal = normal + dot_nt(left, jnp.concatenate(match, axis=1))
    normal = normal[:24] + normal[24:]
    trace = sum(vsr[p, 21:22, :] for p in range(n_tm))
    prior = jnp.concatenate([owned, prior_ref[:, pl.ds(pl.multiple_of(tm * lanes, 128), lanes)]], axis=1)

    def source_entry(k, l):
        row = SRC_AT[k, l]
        value = normal[row : row + 1]
        return value + prior[k : k + 1] if k == l else value

    update, _ = ldl_solve(source_entry, lambda k: normal[15 + k : 16 + k], 5)
    resid_a = r_ref[...]
    for k in range(5):
        resid_a = resid_a - srcp[k] * update[k][:, :128]
    ra[...] = resid_a
    weighted = w_ref[...] * resid_a
    for j in range(21):
        vrow[j : j + 1, :] = jnp.sum(winp[j] * weighted, axis=0, keepdims=True)

    lane = iota((n_hi, 128), 1)

    def put_blocks(rows, centre_at, edge_at, extra=None):
        edges = jnp.where(lane < 64, pltpu.roll(rows, n_hi - 1, 0), pltpu.roll(rows, 1, 0))
        if extra is not None:
            edges = jnp.where((lane == 64) & (iota((n_hi, 128), 0) < n_src), extra, edges)
        pb[pl.ds(centre_at, n_hi, stride=8), :] = rows
        pb[pl.ds(edge_at, n_hi, stride=8), :] = edges

    trace = jnp.sum(trace, axis=1, keepdims=True)
    for c in range(3):
        rows = spread_rows(lambda m, c=c: vrow[3 * m + c : 3 * m + c + 1, :], 7)
        put_blocks(rows, c, 3 + c, trace if c == 0 else None)
    put_blocks(ex[...], 6, 7)

    def right_rows(j):
        return pb.at[pl.ds(pl.multiple_of(j * 8, 8), 8)]

    other_src(lambda p: start(right_rows(p), br.at[sr], 4, (tm, p)))
    pl.when(has_next)(lambda: start(right_rows(n_src), br.at[n_src + sr], 5, (next_tm, 0)))
    pl.when(has_prev)(lambda: start(right_rows(n_hi - 1), br.at[n_src + sr], 6, (prev_tm, last_sr)))

    flat_at, plane_at = iota((384, 384), 1), iota((384, 384), 0)
    mixed = hot(flat_at == 3 * (plane_at & 127) + (plane_at >> 7))
    flat_ridge = jnp.concatenate([ridge_ref[pl.ds(3 * sr + q, 1), :] for q in range(3)], axis=1)
    ridge_row = sum(dot_nt(jnp.broadcast_to(part, (16, 384)), mixed)[0:1] for part in pieces_3(flat_ridge))
    calf[...] = cal_ref[...].astype(F32).reshape(128 * 24, 128)
    for k in range(24):
        calp[k] = calf[pl.ds(k, 128, stride=24), :].T
    for kg in range(6):
        for lg in range(kg // 2, 3):

            def cal_terms(rows, kg=kg, lg=lg):
                w = w_ref[rows, :]
                y = [w * calp[4 * kg + k, rows, :] for k in range(4)]
                x = [calp[8 * lg + l, rows, :] for l in range(8)]
                return [y[k] * x[l] for k in range(4) for l in range(8)]

            sums = summed(32, cal_terms)
            for k in range(4):
                at = cal_row(4 * kg + k, 8 * lg)
                vc[at : at + 8, :] = jnp.concatenate(sums[8 * k : 8 * k + 8], axis=0)
    unit_hot = hot(iota((NCU, 128), 0) == unit_ref[...])
    unit_hot_2 = jnp.concatenate([unit_hot, unit_hot], axis=1)
    units = dot_nt(jnp.concatenate(pieces_2(vc[...]), axis=1), unit_hot_2)
    cp[...] = jnp.concatenate([units[:192], units[192:]], axis=1)

    def cal_share(p):
        return cp.at[pl.ds(pl.multiple_of(p * share, 8), share)]

    def send_cal(p):
        pl.when(p < n_own)(lambda: start(cal_share(p), cr.at[sr], 3, (tm, p)))

    other_src(send_cal)

    for k in range(5):
        sub[tm, k : k + 1, :] = update[k][:, 128:]
    other_tm(lambda p: start(sub.at[tm], sub.at[tm], 7, (p, sr)))

    mr[sr] = mb[pl.ds(pl.multiple_of(sr * MROWS, 8), MROWS), :]
    arrived(mr.at[pl.ds(0, last_sr)], 1)
    total = mr[0]
    for i in range(1, n_src):
        total = total + mr[i]
    mown[...] = total

    def add_carried():
        arrived(mr.at[pl.ds(n_src, n_src)], 2)
        total = mown[...]
        for i in range(n_src):
            total = total + mr[n_src + i]
        mown[...] = total

    pl.when(has_prev & first)(add_carried)
    for c in range(3):
        v = SLOT_AT[0, c, c]
        mown[v : v + 1, :] = mown[v : v + 1, :] + ridge_row[:, 128 * c : 128 * c + 128]
    lin = tm * n_src + sr
    lower, upper = jnp.maximum(lin - 1, 0), jnp.minimum(lin + 1, n_tm * n_src - 1)
    has_left, has_right = lin > 0, lin < n_tm * n_src - 1
    pl.when(has_left)(lambda: start(mown, halo.at[1], 8, (lower // n_src, lower % n_src)))
    pl.when(has_right)(lambda: start(mown, halo.at[0], 9, (upper // n_src, upper % n_src)))

    pl.when(has_left)(lambda: arrived(halo.at[0], 9))
    pl.when(has_right)(lambda: arrived(halo.at[1], 8))
    br[sr] = pb[pl.ds(pl.multiple_of(sr * 8, 8), 8), :]
    arrived(br.at[pl.ds(0, last_sr)], 4)
    basis[0] = jnp.zeros((8, 384), F32)
    total = br[0]
    for i in range(1, n_src):
        total = total + br[i]
    gt[0:8, :] = total
    trace = total[3:4, 64:65]

    def add_other(at):
        arrived(br.at[pl.ds(n_src, n_src)], at)
        total = gt[0:8, :]
        for i in range(n_src):
            total = total + br[n_src + i]
        gt[0:8, :] = total

    pl.when(has_prev & first)(lambda: add_other(5))
    pl.when(has_next & final)(lambda: add_other(6))
    lane = iota((8, 128), 1)

    def widened(centre, edge):
        return jnp.concatenate([jnp.where(lane >= 110, edge, 0.0), centre, jnp.where(lane < 18, edge, 0.0)], axis=1)

    total = gt[0:8, :]
    edge = jnp.concatenate([total[3:8], total[0:3]], axis=0)
    basis[1] = jnp.where(iota((8, 384), 0) < 3, widened(total, edge), 0.0)
    last = widened(total[6:7] + jnp.zeros((8, 128), F32), total[7:8] + jnp.zeros((8, 128), F32))[0:1]
    full = jnp.concatenate([halo[0], mown[...], halo[1]], axis=1)
    full = jnp.concatenate([full, jnp.broadcast_to(last, (8, 384))], axis=0)
    band[...] = jnp.zeros_like(band)
    for d in range(3):
        for c in range(3):
            v = SLOT_AT[0, min(c, d), max(c, d)]
            band[9 + d, c : c + 1, :] = full[v : v + 1]
    for delta in range(1, 4):
        base = SLOT_AT[delta, 0, 0]
        moved = pltpu.roll(full, delta, 1)
        for d in range(3):
            for c in range(3):
                v = base + 3 * c + d
                band[3 * (3 + delta) + d, c : c + 1, :] = full[v : v + 1]
                v = base + 3 * d + c
                band[3 * (3 - delta) + d, c : c + 1, :] = moved[v : v + 1]

    mean = trace * (1.0 / (384 * n_src * n_tm))
    centre = jnp.broadcast_to(mean * 1.2, (8, 384))
    scale = jnp.broadcast_to(2.0 / (mean * 1.1), (8, 384))

    def grow(k, carry):
        x = basis[k + 1]
        y = jnp.zeros((8, 384), F32)
        for delta in range(-3, 4):
            moved = x if delta == 0 else pltpu.roll(x, (-delta) % 384, 1)
            for d in range(3):
                y = y + band[3 * (3 + delta) + d] * moved[d : d + 1]
        image[k] = y[:, 128:256]
        basis[k + 2] = scale * (y - centre * x) - basis[k]
        return carry

    lax.fori_loop(0, CG_ITERS, grow, 0)
    own = [basis[k + 1][:, 128:256] for k in range(CG_ITERS)]
    images = [image[k] for k in range(CG_ITERS)]
    rows = [jnp.sum(own[i] * images[j], axis=0, keepdims=True) for i, j in GRAM_PAIRS]
    rows += [jnp.sum(own[0] * own[i], axis=0, keepdims=True) for i in range(CG_ITERS)]
    for e, row in enumerate(rows):
        gt[e : e + 1, :] = row
    n_gram = len(rows)
    in_gram = iota((32, 128), 0) < n_gram
    same = iota((32, 128), 0) == iota((32, 128), 1)
    sums = jnp.sum(jnp.where(in_gram, gt[...], 0.0), axis=1, keepdims=True)
    gs[0] = jnp.broadcast_to(jnp.sum(jnp.where(same, sums, 0.0), axis=0, keepdims=True), (8, 128))
    g1[sr] = gs[0]
    other_src(lambda p: start(gs.at[0], g1.at[sr], 12, (tm, p)))
    for k in range(CG_ITERS):
        xm[3 * k : 3 * k + 3, :] = own[k][0:3]

    def slab_rows(i):
        return xr.at[pl.ds(pl.multiple_of(i * XROWS, 8), XROWS)]

    other_src(lambda p: start(xm, slab_rows(sr), 14, (tm, p)))
    pl.when(has_prev & first)(
        lambda: each(n_src, lambda i: start(xm, slab_rows(n_src), 15, (prev_tm, i)))
    )
    xr[pl.ds(pl.multiple_of(sr * XROWS, 8), XROWS), :] = xm[...]

    def sum_cal():
        cr[sr] = cp[pl.ds(pl.multiple_of(sr * share, 8), share), :]
        arrived(cr.at[pl.ds(0, last_sr)], 3)
        total = cr[0]
        for i in range(1, n_src):
            total = total + cr[i]
        c2s[...] = total
        c2r[tm] = total
        other_tm(lambda p: start(c2s, c2r.at[tm], 10, (p, sr)))

    pl.when(owner)(sum_cal)

    def sweep(j, carry):
        row_of = iota((24, 128), 0)
        column = inv[pl.ds(pl.multiple_of(24 * j, 8), 24), :]
        pivot = jnp.sum(jnp.where(row_of == j, column, 0.0), axis=0, keepdims=True)
        over = 1.0 / pivot
        scaled = column * over
        for k in range(24):
            at = inv[24 * k : 24 * k + 24, :]
            factor = scaled[k : k + 1]
            inv[24 * k : 24 * k + 24, :] = jnp.where(row_of == j, factor, at - factor * column)
        inv[pl.ds(pl.multiple_of(24 * j, 8), 24), :] = jnp.where(row_of == j, -over, scaled)
        return carry

    arrived(g1.at[pl.ds(0, last_sr)], 12)
    total = g1[0]
    for i in range(1, n_src):
        total = total + g1[i]
    gs[1] = total
    g2[tm] = total
    other_tm(lambda p: start(gs.at[1], g2.at[tm], 13, (p, sr)))
    def finish_cal():
        arrived(c2r.at[pl.ds(0, last_tm)], 10)
        total = c2r[0]
        for i in range(1, n_tm):
            total = total + c2r[i]
        c3s[...] = total
        cf[sr] = total
        other_src(lambda p: start(c3s, cf.at[sr], 11, (tm, p)))

    pl.when(owner)(finish_cal)

    arrived(g2.at[pl.ds(0, last_tm)], 13)
    total = g2[0]
    for i in range(1, n_tm):
        total = total + g2[i]
    sums = jnp.sum(jnp.where(same, total[0:1], 0.0), axis=1, keepdims=True)
    gt[...] = jnp.broadcast_to(sums, (32, 128))
    gram_at = {pair: e for e, pair in enumerate(GRAM_PAIRS)}
    n_pairs = len(GRAM_PAIRS)

    def gram(i, j):
        e = gram_at[i, j]
        return gt[e : e + 1, :]

    weights, shares = ldl_solve(gram, lambda i: gt[n_pairs + i : n_pairs + i + 1, :], CG_ITERS)
    least = shares[0]
    for value in shares[1:]:
        least = jnp.where(value >= least, least, value)
    trust_ref[...] = jnp.where(least > TRUST, 1.0, 0.0)[:, 0:1]
    arrived(sub.at[pl.ds(0, last_tm)], 7)
    for p in range(n_tm):
        update_ref[:, lanes * p : lanes * p + lanes] = sub[p, 0:5, :]

    here_3 = jnp.concatenate([here[:n_hi].astype(F32)] * 3 + [jnp.zeros((128 - 3 * n_hi, 128), F32)], axis=0).astype(BF16)
    after_3 = jnp.concatenate([after[:n_hi].astype(F32)] * 3 + [jnp.zeros((128 - 3 * n_hi, 128), F32)], axis=0).astype(BF16)
    arrived(xr.at[pl.ds(0, XROWS * last_sr)], 14)
    pl.when(has_next)(lambda: arrived(slab_rows(n_src), 15))
    resid_b = ra[...]
    planes = []
    for c in range(3):
        plane = weights[0] * xr[pl.ds(c, n_hi, stride=XROWS), :]
        for k in range(1, CG_ITERS):
            plane = plane + weights[k] * xr[pl.ds(3 * k + c, n_hi, stride=XROWS), :]
        planes.append(plane)
        parts = [part.astype(F32) for part in pieces_3(plane)]
        parts.append(jnp.zeros((128 - 3 * n_hi, 128), F32))
        turned = jnp.concatenate(parts, axis=0).T.astype(BF16)
        at_place = dot_nn(turned, here_3)
        past_place = dot_nn(turned[:16], after_3)[:8]
        for m in range(7):
            value = jnp.sum(jnp.where(inside == m, at_place, 0.0), axis=0, keepdims=True)
            value = value + jnp.sum(jnp.where(past == m, past_place, 0.0), axis=0, keepdims=True)
            resid_b = resid_b - winp[3 * m + c] * value

    weighted = w_ref[...] * resid_b
    for k in range(24):
        vrow[k : k + 1, :] = jnp.sum(calp[k] * weighted, axis=0, keepdims=True)
    units = dot_nt(jnp.concatenate(pieces_2(vrow[...]), axis=1), unit_hot_2)
    ks[0, 0:8, :] = jnp.concatenate([units[0:8], units[8:16]], axis=1)
    ks[0, 8:16, :] = jnp.concatenate([units[16:24], jnp.zeros((8, NCU), F32)], axis=1)

    def exchange(buffer, count, me, at, place, beside=None):
        buffer[me] = ks[at]
        each(
            count - 1,
            lambda d: start(ks.at[at], buffer.at[me], 16 + at, place((me + 1 + d) % count)),
        )
        if beside is not None:
            beside()
        arrived(buffer.at[pl.ds(0, count - 1)], 16 + at)
        total = buffer[0]
        for i in range(1, count):
            total = total + buffer[i]
        ks[at + 1] = total

    def write_attitude():
        slab = jnp.concatenate(planes, axis=1)
        flat = dot_nn(jnp.concatenate(pieces_3(slab), axis=0), mixed)
        flat = flat[:n_hi] + flat[n_hi : 2 * n_hi] + flat[2 * n_hi :]
        for q in range(3):
            att_ref[pl.ds(q, n_src, stride=3), :] = flat[:n_src, 128 * q : 128 * q + 128]

    def start_inverse():
        write_attitude()
        pl.when(owner)(lambda: arrived(cf.at[pl.ds(0, n_own - 1)], 11))
        pl.when(jnp.logical_not(owner))(lambda: arrived(cf, 11))
        packed = jnp.concatenate([cf[i] for i in range(n_own)], axis=0)
        other_half = pltpu.roll(packed, 64, 1)
        for k in range(24):
            size = 24 - 8 * (k // 8)
            at = cal_row(k, 8 * (k // 8))
            part = packed[at : at + size] if k < 8 else other_half[at - 192 : at - 192 + size]
            inv[24 * k + 8 * (k // 8) : 24 * k + 24, :] = part
        for k in range(8, 24):
            size = 8 * (k // 8)
            inv[24 * k : 24 * k + size, :] = inv[pl.ds(k, size, stride=24), :]
        lax.fori_loop(0, 12, sweep, 0)

    exchange(kz, nz, zz, 0, lambda p: (tm, p * ny + yy), start_inverse)
    exchange(ky, ny, yy, 1, lambda p: (tm, zz * ny + p), lambda: lax.fori_loop(12, 24, sweep, 0))
    exchange(kt, n_tm, tm, 2, lambda p: (p, sr))
    total = ks[3]
    right = jnp.concatenate([total[0:8, :NCU], total[0:8, NCU:], total[8:16, :NCU]], axis=0)
    calib = jnp.zeros((24, NCU), F32)
    for j in range(24):
        calib = calib - inv[24 * j : 24 * j + 24, :NCU] * right[j : j + 1]
    calib_ref[...] = calib
    spread = dot_nn(jnp.concatenate(pieces_3(calib), axis=0), unit_hot)
    spread = spread[0:24] + spread[24:48] + spread[48:72]
    out = resid_b
    for k in range(24):
        out = out - calp[k] * spread[k : k + 1]
    resid_ref[...] = out.T

    left_us(vsr.at[pl.ds(0, last_tm)], 0)
    left_us(mr.at[pl.ds(0, last_sr)], 1)
    pl.when(has_next)(lambda: left_us(mr.at[0], 2))
    pl.when(owner)(lambda: left_us(cr.at[pl.ds(0, n_own - 1)], 3))
    pl.when(jnp.logical_not(owner))(lambda: left_us(cr.at[pl.ds(0, n_own)], 3))
    left_us(br.at[pl.ds(0, last_sr)], 4)
    pl.when(has_next)(lambda: left_us(br.at[0], 5))
    pl.when(has_prev)(lambda: left_us(br.at[0], 6))
    left_us(sub.at[pl.ds(0, last_tm)], 7)
    pl.when(has_left)(lambda: left_us(mown, 8))
    pl.when(has_right)(lambda: left_us(mown, 9))
    pl.when(owner)(lambda: left_us(c2r.at[pl.ds(0, last_tm)], 10))
    pl.when(owner)(lambda: left_us(cr.at[pl.ds(0, last_sr)], 11))
    left_us(g1.at[pl.ds(0, last_sr)], 12)
    left_us(g2.at[pl.ds(0, last_tm)], 13)
    left_us(xr.at[pl.ds(0, XROWS * last_sr)], 14)
    pl.when(has_prev & first)(lambda: left_us(xr.at[pl.ds(0, XROWS * n_src)], 15))
    left_us(kz.at[pl.ds(0, nz - 1)], 16)
    left_us(ky.at[pl.ds(0, ny - 1)], 17)
    left_us(kt.at[pl.ds(0, last_tm)], 18)


def fast_shards(
    n_tm,
    n_src,
    src_deriv,
    att_deriv,
    cal_deriv,
    obs_resid,
    obs_weight,
    src_id,
    tile_knot,
    row_offset,
    cal_unit,
    src_prior,
    att_ridge,
):
    n_hi = (n_src + 1 + 7) // 8 * 8
    groups = src_prior.shape[1]
    lanes = groups // n_tm
    per_own = 24 // min(24, n_src)
    n_own, share = 24 // per_own, 8 * (24 // min(24, n_src))
    ny = min(4, n_src)
    nz = n_src // ny
    src_planes = jnp.transpose(src_deriv, (1, 2, 0))
    att_planes = jnp.transpose(att_deriv, (1, 2, 0))
    ridge = att_ridge.reshape(3 * n_src, 128)

    def f32(*shape):
        return jax.ShapeDtypeStruct(shape, F32)

    def vmem(*shape):
        return pltpu.VMEM(shape, F32)

    whole = pl.BlockSpec(memory_space=pltpu.VMEM)
    return pl.pallas_call(
        functools.partial(joint_kernel, n_tm, n_src, n_hi),
        out_shape=[f32(5, groups), f32(3 * n_src, 128), f32(24, NCU), f32(128, 128), f32(1, 1)],
        in_specs=[whole] * 11,
        out_specs=[whole] * 5,
        scratch_shapes=[
            vmem(8, groups),
            vmem(21, 128, 128),
            vmem(5, 128, 128),
            vmem(12, 128, 128),
            vmem(24, 128, 128),
            vmem(24 * 128, 128),
            pltpu.VMEM((128, 128), jnp.int32),
            vmem(128, 128),
            vmem(128, 128),
            vmem(7, MROWS + 8, 128),
            vmem(384, 128),
            vmem(24, 128),
            vmem(n_hi * MROWS, 128),
            vmem(n_hi, 128),
            vmem(192, 128),
            vmem(n_tm, 24, 128),
            vmem(2 * n_src, MROWS, 128),
            vmem(MROWS, 128),
            vmem(2, MROWS, 128),
            vmem(21, 8, 384),
            vmem(n_hi * 8, 128),
            vmem(2 * n_src, 8, 128),
            vmem(CG_ITERS + 2, 8, 384),
            vmem(CG_ITERS, 8, 128),
            vmem(2, 8, 128),
            vmem(n_src, 8, 128),
            vmem(n_tm, 8, 128),
            vmem(32, 128),
            vmem(XROWS, 128),
            vmem(n_hi * XROWS, 128),
            vmem(n_tm, 8, lanes),
            vmem(n_src, share, 128),
            vmem(share, 128),
            vmem(n_tm, share, 128),
            vmem(share, 128),
            vmem(n_own, share, 128),
            vmem(576, 128),
            vmem(128, 128),
            vmem(24, 128),
            vmem(nz, 16, 128),
            vmem(ny, 16, 128),
            vmem(n_tm, 16, 128),
            vmem(4, 16, 128),
            pltpu.SemaphoreType.DMA((19,)),
            pltpu.SemaphoreType.DMA((19,)),
        ],
        compiler_params=pltpu.CompilerParams(
            collective_id=0, has_side_effects=True, vmem_limit_bytes=48 << 20
        ),
        name="joint_solve",
    )(src_planes, att_planes, cal_deriv, obs_resid, obs_weight, row_offset, *(a.reshape(1, 128) for a in (src_id, tile_knot, cal_unit)), src_prior, ridge)


def hand_over(arrays):
    count = len(arrays)

    def kernel(*refs):
        for i in range(count):
            refs[count + i][...] = refs[i][...]

    whole = pl.BlockSpec(memory_space=pltpu.VMEM)
    return pl.pallas_call(
        kernel,
        out_shape=[jax.ShapeDtypeStruct(a.shape, a.dtype) for a in arrays],
        in_specs=[whole] * count,
        out_specs=[whole] * count,
        name="hand_over",
    )(*arrays)


def guarded_shards(n_tm, n_src, *arrays):
    update, attitude, calib, resid, trust = fast_shards(n_tm, n_src, *arrays)
    fast = (update, attitude, calib, resid)

    def slow():
        update, attitude, calib, resid = shards(*arrays)
        return update, attitude.reshape(-1, 128), calib, resid

    update, attitude, calib, resid = hand_over(lax.cond(trust[0, 0] > 0.5, lambda: fast, slow))
    return update, attitude.reshape(-1), calib, resid


def solution(mesh):
    placed = (
        P(("tm", "src"), None, None),
        P(("tm", "src"), None, None),
        P(("tm", "src"), None, None),
        P(("tm", "src"), None),
        P(("tm", "src"), None),
        P(("tm", "src")),
        P(("tm", "src")),
        P(("tm", "src"), None),
        P(("tm", "src")),
        P(None, "src"),
        P("tm"),
    )
    return jax.shard_map(
        functools.partial(guarded_shards, mesh.shape["tm"], mesh.shape["src"]),
        mesh=mesh,
        in_specs=placed,
        out_specs=(P(None, "src"), P("tm"), P(), P(("tm", "src"), None)),
        check_vma=False,
    )
```

```python
import functools

import jax
import jax.numpy as jnp
import numpy as np
from jax import lax
from jax.experimental import pallas as pl
from jax.experimental.pallas import tpu as pltpu
from jax.sharding import PartitionSpec as P

NCU = 64
CG_ITERS = 6


HIGH = lax.Precision.HIGHEST


def padded_2(cells, sides, width):
    for axis, dim in sides:
        count = lax.axis_size(axis)
        ends = count - 1
        head = lax.slice_in_dim(cells, 0, width, axis=dim)
        tail = lax.slice_in_dim(cells, cells.shape[dim] - width, cells.shape[dim], axis=dim)
        cells = jnp.concatenate(
            [
                lax.ppermute(tail, axis, [(i, (i + 1) % count) for i in range(ends)]),
                cells,
                lax.ppermute(head, axis, [((i + 1) % count, i) for i in range(ends)]),
            ],
            axis=dim,
        )
    return cells


def all_sum(array, axis):
    devices, step = lax.axis_size(axis), 1
    while step < devices:
        array = array + lax.ppermute(array, axis, [(i, i ^ step) for i in range(devices)])
        step *= 2
    return array


def from_behind(array, axis, by):
    devices = lax.axis_size(axis)
    pairs = [(i, i + by) for i in range(devices) if 0 <= i + by < devices]
    return lax.ppermute(array, axis, pairs)


def lag_table():
    first_index = np.arange(21)[None, :]
    lag_rows = np.arange(12)[:, None]
    second = first_index + lag_rows
    flat_index = first_index * 21 + np.minimum(second, 20)
    return (flat_index, (second < 21).astype(np.float32))


def solve_spd(matrix, right):
    order = right.shape[0]
    rows = jnp.arange(order)[:, None]

    def column(j, state):
        rest, factor = state
        col = jnp.where(rows >= j, rest[:, j] / jnp.sqrt(rest[j, j]), 0.0)
        return rest - col[:, None, :] * col[None, :, :], factor.at[:, j].set(col)

    factor = lax.fori_loop(0, order, column, (matrix, jnp.zeros_like(matrix)))[1]

    def forward(i, answer):
        value = right[i] - jnp.sum(jnp.where(rows < i, factor[i] * answer, 0.0), axis=0)
        return answer.at[i].set(value / factor[i, i])

    halfway = lax.fori_loop(0, order, forward, jnp.zeros_like(right))

    def backward(step, answer):
        i = order - 1 - step
        value = halfway[i] - jnp.sum(jnp.where(rows > i, factor[:, i] * answer, 0.0), axis=0)
        return answer.at[i].set(value / factor[i, i])

    return lax.fori_loop(0, order, backward, jnp.zeros_like(right))


def tile_normals(deriv, weight, resid):
    values = deriv.astype(jnp.float32)
    weighted = values * weight[:, None, :]
    normal = jnp.einsum("tkr,tlr->tkl", weighted, values, precision=HIGH)
    right = jnp.einsum("tkr,tr->tk", weighted, resid, precision=HIGH)
    return jnp.concatenate([normal.reshape(normal.shape[0], -1), right], axis=1)


def small_solve(sums, prior, order):
    count = sums.shape[1]
    matrix = sums[: order * order].reshape(order, order, count)
    if prior is not None:
        matrix = matrix + jnp.eye(order, dtype=jnp.float32)[:, :, None] * prior[:, None, :]
    return solve_spd(matrix, sums[order * order :])


def window_rows(att_deriv, row_offset):
    values = att_deriv.astype(jnp.float32)
    window = jnp.zeros((values.shape[0], 21, values.shape[2]), jnp.float32)
    for knot_step in range(4):
        placed = jnp.pad(values, ((0, 0), (3 * knot_step, 9 - 3 * knot_step), (0, 0)))
        window = window + jnp.where((row_offset == knot_step)[:, None, :], placed, 0.0)
    return window


def attitude_terms(window, weight, resid):
    weighted = window * weight[:, None, :]
    normal = jnp.einsum("tjr,tlr->tjl", weighted, window, precision=HIGH)
    right = jnp.einsum("tjr,tr->tj", weighted, resid, precision=HIGH)
    flat_index, valid_lag = lag_table()
    banded = normal.reshape(normal.shape[0], 441)[:, flat_index] * valid_lag
    return jnp.concatenate([banded, right[:, None, :]], axis=1)


def conjugate(band_rows, right, ridge_part, band_edge, extend, inner_sum):
    count = right.shape[0]
    lagged = jnp.concatenate([band_edge, band_rows[1:]], axis=1)
    solution = jnp.zeros_like(right)
    residual = right
    direction = right
    norm_now = inner_sum(residual, residual)
    for iteration in range(CG_ITERS):
        padded = extend(direction)
        result = ridge_part * direction
        for d in range(12):
            result = result + band_rows[d] * padded[11 + d : 11 + d + count]
        for d in range(1, 12):
            result = (
                result + lagged[d - 1, 11 - d : 11 - d + count] * padded[11 - d : 11 - d + count]
            )
        step_size = norm_now / inner_sum(direction, result)
        solution = solution + step_size * direction
        residual = residual - step_size * result
        norm_next = inner_sum(residual, residual)
        direction = residual + norm_next / norm_now * direction
        norm_now = norm_next
    return solution


def slab_extend(vector):
    return padded_2(vector, (("tm", 0),), 11)


def slab_dot(first_vec, second_vec):
    return all_sum(jnp.sum(first_vec * second_vec), "tm")


def shards(
    src_deriv,
    att_deriv,
    cal_deriv,
    obs_resid,
    obs_weight,
    src_id,
    tile_knot,
    row_offset,
    cal_unit,
    src_prior,
    att_ridge,
):
    slab_pos = lax.axis_index("tm")
    groups = src_prior.shape[1]
    normal_sums = jax.ops.segment_sum(
        tile_normals(src_deriv, obs_weight, obs_resid), src_id, num_segments=groups
    ).T
    summed = all_sum(normal_sums, "tm")
    source_update = small_solve(summed, src_prior, 5)
    resid_a = obs_resid - jnp.einsum(
        "tkr,kt->tr", src_deriv.astype(jnp.float32), source_update[:, src_id], precision=HIGH
    )
    slab_params = att_ridge.shape[0]
    window = window_rows(att_deriv, row_offset)
    local_knot = tile_knot - slab_pos * (slab_params // 3)
    columns = 3 * local_knot[:, None] + jnp.arange(21, dtype=jnp.int32)[None, :]
    values = attitude_terms(window, obs_weight, resid_a)
    slab_sums = jax.ops.segment_sum(
        values.transpose(0, 2, 1).reshape(-1, 13),
        columns.reshape(-1),
        num_segments=slab_params + 21,
    ).T
    carried = from_behind(slab_sums[:, slab_params:], "tm", 1)
    head_sums = slab_sums[:, :slab_params].at[:, :21].add(carried)
    summed_band = all_sum(head_sums, "src")
    band_edge = from_behind(summed_band[1:12, -11:], "tm", 1)
    attitude_update = conjugate(
        summed_band[:12], summed_band[12], att_ridge, band_edge, slab_extend, slab_dot
    )
    next_params = from_behind(attitude_update[:21], "tm", -1)
    extended = jnp.concatenate([attitude_update, next_params])
    resid_b = resid_a - jnp.einsum("tjr,tj->tr", window, extended[columns], precision=HIGH)
    calib_sums = jax.ops.segment_sum(
        tile_normals(cal_deriv, obs_weight, resid_b), cal_unit, num_segments=NCU
    ).T
    calib_total = all_sum(all_sum(calib_sums, "tm"), "src")
    calib_update = small_solve(calib_total, None, 24)
    residual_out = resid_b - jnp.einsum(
        "tkr,kt->tr", cal_deriv.astype(jnp.float32), calib_update[:, cal_unit], precision=HIGH
    )
    return (source_update, attitude_update, calib_update, residual_out)


F32 = jnp.float32
BF16 = jnp.bfloat16
MESH = pl.DeviceIdType.MESH
MROWS = 32
XROWS = 24
TRUST = 0.01


def pieces_2(x):
    high = x.astype(BF16)
    return high, (x - high.astype(F32)).astype(BF16)


def pieces_3(x):
    high = x.astype(BF16)
    rest = x - high.astype(F32)
    mid = rest.astype(BF16)
    return high, mid, (rest - mid.astype(F32)).astype(BF16)


def dot_nn(a, b):
    return lax.dot_general(a, b, (((1,), (0,)), ((), ())), preferred_element_type=F32)


def dot_nt(a, b):
    return lax.dot_general(a, b, (((1,), (1,)), ((), ())), preferred_element_type=F32)


def iota(shape, dim):
    return lax.broadcasted_iota(jnp.int32, shape, dim)


def hot(match):
    return jnp.where(match, 1.0, 0.0).astype(BF16)


def band_slots():
    slots = [(0, c, d) for c in range(3) for d in range(c, 3)]
    for delta in range(1, 4):
        slots += [(delta, c, d) for c in range(3) for d in range(3)]
    return slots


SLOTS = band_slots()
SLOT_AT = {slot: v for v, slot in enumerate(SLOTS)}
SRC_PAIRS = [(k, l) for k in range(5) for l in range(k, 5)]
SRC_AT = {pair: e for e, pair in enumerate(SRC_PAIRS)}
GRAM_PAIRS = [(i, j) for i in range(CG_ITERS) for j in range(i, CG_ITERS)]


def cal_row(k, l):
    if k < 8:
        return 24 * k + l
    if k < 16:
        return 192 + 16 * (k - 8) + l - 8
    return 320 + 8 * (k - 16) + l - 16


def place_lanes(lo_row):
    inside = iota((128, 128), 0) - lo_row
    return inside, iota((8, 128), 0) + 128 - lo_row


def ldl_solve(entry, right, order):
    low = {}
    pivots, inverse, shares = [], [], []
    for j in range(order):
        pivot = entry(j, j)
        for m in range(j):
            pivot = pivot - low[j, m] * low[j, m] * pivots[m]
        shares.append(pivot / entry(j, j))
        pivots.append(pivot)
        inverse.append(1.0 / pivot)
        for i in range(j + 1, order):
            value = entry(j, i)
            for m in range(j):
                value = value - low[i, m] * (low[j, m] * pivots[m])
            low[i, j] = value * inverse[j]
    forward = []
    for i in range(order):
        value = right(i)
        for m in range(i):
            value = value - low[i, m] * forward[m]
        forward.append(value)
    answer = [None] * order
    for i in range(order - 1, -1, -1):
        value = forward[i] * inverse[i]
        for m in range(i + 1, order):
            value = value - low[m, i] * answer[m]
        answer[i] = value
    return answer, shares


def joint_kernel(
    n_tm,
    n_src,
    n_hi,
    src_ref,
    att_in_ref,
    cal_ref,
    resid_in_ref,
    weight_ref,
    offset_ref,
    id_ref,
    knot_ref,
    unit_ref,
    raw_prior_ref,
    ridge_ref,
    update_ref,
    att_ref,
    calib_ref,
    resid_ref,
    trust_ref,
    prior_ref,
    winp,
    srcp,
    attp,
    calp,
    calf,
    offp,
    w_ref,
    r_ref,
    vm,
    vc,
    vs,
    mb,
    ex,
    cp,
    vsr,
    mr,
    mown,
    halo,
    band,
    pb,
    br,
    basis,
    image,
    gs,
    g1,
    g2,
    gt,
    xm,
    xr,
    sub,
    cr,
    c2s,
    c2r,
    c3s,
    cf,
    inv,
    ra,
    vrow,
    kz,
    ky,
    ks,
    send,
    recv,
):
    tm, sr = lax.axis_index("tm"), lax.axis_index("src")
    last_tm, last_sr = n_tm - 1, n_src - 1
    has_next, has_prev = tm < last_tm, tm > 0
    ny = min(4, n_src)
    nz = n_src // ny
    yy, zz = sr % ny, sr // ny
    per_own = 24 // min(24, n_src)
    n_own = 24 // per_own
    share = 8 * per_own
    owner = sr < n_own

    def block_of(p):
        return p // ny * ny + (p % ny + p // ny) % ny

    def device_of(b):
        return b // ny * ny + (b % ny + nz * ny - b // ny) % ny

    block_at = block_of(sr)
    final_sr = device_of(last_sr)
    first, final = sr == 0, sr == final_sr
    lanes = prior_ref.shape[1] // n_tm

    def start(source, target, at, place):
        pltpu.make_async_remote_copy(
            src_ref=source,
            dst_ref=target,
            send_sem=send.at[at],
            recv_sem=recv.at[at],
            device_id=place,
            device_id_type=MESH,
        ).start()

    def arrived(part, at):
        pltpu.make_async_copy(part, part, recv.at[at]).wait()

    def left_us(part, at):
        pltpu.make_async_copy(part, part, send.at[at]).wait()

    def each(count, body):
        def run(d, carry):
            body(d)
            return carry

        lax.fori_loop(0, count, run, 0)

    def other_src(body):
        each(last_sr, lambda d: body((sr + 1 + d) % n_src))

    def other_tm(body):
        each(last_tm, lambda d: body((tm + 1 + d) % n_tm))

    next_tm, prev_tm = jnp.minimum(tm + 1, last_tm), jnp.maximum(tm - 1, 0)
    halo[...] = jnp.zeros_like(halo)
    xr[XROWS * n_src :, :] = jnp.zeros((XROWS * (n_hi - n_src), 128), F32)

    barrier = pltpu.get_barrier_semaphore()

    def greet(a, b):
        pl.semaphore_signal(barrier, inc=1, device_id=(a, b), device_id_type=MESH)

    other_tm(lambda p: greet(p, sr))
    other_src(lambda p: greet(tm, p))

    w_ref[...] = weight_ref[...].T
    r_ref[...] = resid_in_ref[...].T
    offp[...] = offset_ref[...].astype(F32).T.astype(jnp.int32)
    for k in range(5):
        srcp[k] = src_ref[k].astype(F32).T
    for k in range(12):
        attp[k] = att_in_ref[k].astype(F32).T
    vm[...] = jnp.zeros_like(vm)
    prior_ref[...] = jnp.ones_like(prior_ref)
    prior_ref[0:5, :] = raw_prior_ref[...]
    pb[...] = jnp.zeros_like(pb)

    def windows(i, carry):
        rows = pl.ds(pl.multiple_of(i * 16, 16), 16)
        values = [attp[k, rows, :] for k in range(12)]
        step = offp[rows, :]
        for j in range(21):
            placed = jnp.zeros((16, 128), F32)
            for o in range(4):
                if 0 <= j - 3 * o < 12:
                    placed = jnp.where(step == o, values[j - 3 * o], placed)
            winp[j, rows, :] = placed
        return carry

    lax.fori_loop(0, 8, windows, 0)

    def summed(count, terms):
        def body(i, sums):
            rows = pl.ds(pl.multiple_of(i * 8, 8), 8)
            return tuple(s + t for s, t in zip(sums, terms(rows)))

        sums = lax.fori_loop(0, 16, body, tuple(jnp.zeros((8, 128), F32) for _ in range(count)))
        return [jnp.sum(s, axis=0, keepdims=True) for s in sums]

    def src_terms(rows):
        x = [srcp[k, rows, :] for k in range(5)]
        w = w_ref[rows, :]
        y = [w * v for v in x]
        r = r_ref[rows, :]
        return [y[k] * x[l] for k, l in SRC_PAIRS] + [v * r for v in y]

    vs[...] = jnp.zeros_like(vs)
    for e, row in enumerate(summed(20, src_terms)):
        vs[e : e + 1, :] = row
    vs[20:21, :] = id_ref[...].astype(F32)

    trace = jnp.sum(ridge_ref[...], axis=0, keepdims=True) * (1.0 / n_src)
    for m in range(7):
        slots = [s for s in SLOTS if m + s[0] < 7]

        def att_terms(rows, m=m, slots=slots):
            x = [winp[j, rows, :] for j in range(3 * m, min(3 * m + 12, 21))]
            w = w_ref[rows, :]
            y = [w * x[c] for c in range(3)]
            return [y[c] * x[3 * delta + d] for delta, c, d in slots]

        for slot, row in zip(slots, summed(len(slots), att_terms)):
            vm[m, SLOT_AT[slot] : SLOT_AT[slot] + 1, :] = row
            if slot[0] == 0 and slot[1] == slot[2]:
                trace = trace + row
    vs[21:22, :] = trace

    pl.semaphore_wait(barrier, last_tm + last_sr)
    other_tm(lambda p: start(vs, vsr.at[tm], 0, (p, sr)))

    knot = knot_ref[...] - tm * (128 * n_src)
    block, place = knot >> 7, knot & 127
    inside, past = place_lanes(place)
    blocks = iota((n_hi + 8, 128), 0)
    here, after = hot(blocks == block), hot(blocks == block + 1)
    spreads = jnp.concatenate([here, here, after, after], axis=1)
    rest = jnp.zeros((120, 128), F32)

    def spread_rows(row_of, count):
        spread = jnp.zeros((128, 128), F32)
        over = jnp.zeros((8, 128), F32)
        for m in range(count):
            row = row_of(m)
            spread = jnp.where(inside == m, row, spread)
            over = jnp.where(past == m, row, over)
        over = jnp.concatenate([over, rest], axis=0)
        right = jnp.concatenate(pieces_2(spread) + pieces_2(over), axis=1)
        return dot_nt(spreads, right)[:n_hi]

    for v, (delta, c, d) in enumerate(SLOTS):
        rows = spread_rows(lambda m, v=v: vm[m, v : v + 1, :], 7 - delta)
        if v < MROWS:
            mb[pl.ds(v, n_hi, stride=MROWS), :] = rows
        else:
            ex[...] = rows

    def band_rows(j):
        return mb.at[pl.ds(pl.multiple_of(j * MROWS, 8), MROWS)]

    ids = jnp.broadcast_to(id_ref[...].astype(F32), (128, 128)).T
    sources = (iota((lanes, 128), 0) + tm * lanes).astype(F32)
    wanted = jnp.concatenate([ids, sources], axis=0)
    groups = prior_ref.shape[1]
    source_hot = hot(iota((groups, 128), 0) == id_ref[...])
    owned = dot_nn(jnp.concatenate(pieces_3(prior_ref[...]), axis=0), source_hot)
    owned = owned[0:8] + owned[8:16] + owned[16:24]

    other_src(lambda p: start(band_rows(block_of(p)), mr.at[sr], 1, (tm, p)))

    vsr[tm] = vs[...]
    arrived(vsr.at[pl.ds(0, last_tm)], 0)
    pl.when(has_next)(lambda: start(band_rows(n_src), mr.at[n_src + sr], 2, (next_tm, 0)))
    normal = jnp.zeros((48, 128 + lanes), F32)
    for p in range(0, n_tm, 2):
        match = [hot(wanted == vsr[q, 20:21, :]) for q in (p, p + 1)]
        parts = [pieces_2(vsr[q]) for q in (p, p + 1)]
        left = jnp.concatenate([jnp.concatenate([part[i] for part in parts], axis=1) for i in range(2)], axis=0)
        normal = normal + dot_nt(left, jnp.concatenate(match, axis=1))
    normal = normal[:24] + normal[24:]
    trace = sum(vsr[p, 21:22, :] for p in range(n_tm))
    prior = jnp.concatenate([owned, prior_ref[:, pl.ds(pl.multiple_of(tm * lanes, 128), lanes)]], axis=1)

    def source_entry(k, l):
        row = SRC_AT[k, l]
        value = normal[row : row + 1]
        return value + prior[k : k + 1] if k == l else value

    update, _ = ldl_solve(source_entry, lambda k: normal[15 + k : 16 + k], 5)
    resid_a = r_ref[...]
    for k in range(5):
        resid_a = resid_a - srcp[k] * update[k][:, :128]
    ra[...] = resid_a
    weighted = w_ref[...] * resid_a
    for j in range(21):
        vrow[j : j + 1, :] = jnp.sum(winp[j] * weighted, axis=0, keepdims=True)

    lane = iota((n_hi, 128), 1)

    def put_blocks(rows, centre_at, edge_at, extra=None):
        edges = jnp.where(lane < 64, pltpu.roll(rows, n_hi - 1, 0), pltpu.roll(rows, 1, 0))
        if extra is not None:
            edges = jnp.where((lane == 64) & (iota((n_hi, 128), 0) < n_src), extra, edges)
        pb[pl.ds(centre_at, n_hi, stride=8), :] = rows
        pb[pl.ds(edge_at, n_hi, stride=8), :] = edges

    trace = jnp.sum(trace, axis=1, keepdims=True)
    for c in range(3):
        rows = spread_rows(lambda m, c=c: vrow[3 * m + c : 3 * m + c + 1, :], 7)
        put_blocks(rows, c, 3 + c, trace if c == 0 else None)
    put_blocks(ex[...], 6, 7)

    def right_rows(j):
        return pb.at[pl.ds(pl.multiple_of(j * 8, 8), 8)]

    other_src(lambda p: start(right_rows(block_of(p)), br.at[sr], 4, (tm, p)))
    pl.when(has_next)(lambda: start(right_rows(n_src), br.at[n_src + sr], 5, (next_tm, 0)))
    pl.when(has_prev)(lambda: start(right_rows(n_hi - 1), br.at[n_src + sr], 6, (prev_tm, final_sr)))

    flat_at, plane_at = iota((384, 384), 1), iota((384, 384), 0)
    mixed = hot(flat_at == 3 * (plane_at & 127) + (plane_at >> 7))
    flat_ridge = jnp.concatenate([ridge_ref[pl.ds(3 * block_at + q, 1), :] for q in range(3)], axis=1)
    ridge_row = sum(dot_nt(jnp.broadcast_to(part, (16, 384)), mixed)[0:1] for part in pieces_3(flat_ridge))
    calf[...] = cal_ref[...].astype(F32).reshape(128 * 24, 128)
    for k in range(24):
        calp[k] = calf[pl.ds(k, 128, stride=24), :].T
    for kg in range(6):
        for lg in range(kg // 2, 3):

            def cal_terms(rows, kg=kg, lg=lg):
                w = w_ref[rows, :]
                y = [w * calp[4 * kg + k, rows, :] for k in range(4)]
                x = [calp[8 * lg + l, rows, :] for l in range(8)]
                return [y[k] * x[l] for k in range(4) for l in range(8)]

            sums = summed(32, cal_terms)
            for k in range(4):
                at = cal_row(4 * kg + k, 8 * lg)
                vc[at : at + 8, :] = jnp.concatenate(sums[8 * k : 8 * k + 8], axis=0)
    unit_hot = hot(iota((NCU, 128), 0) == unit_ref[...])
    unit_hot_2 = jnp.concatenate([unit_hot, unit_hot], axis=1)
    units = dot_nt(jnp.concatenate(pieces_2(vc[...]), axis=1), unit_hot_2)
    cp[...] = jnp.concatenate([units[:192], units[192:]], axis=1)

    def cal_share(p):
        return cp.at[pl.ds(pl.multiple_of(p * share, 8), share)]

    def send_cal(p):
        pl.when(p < n_own)(lambda: start(cal_share(p), cr.at[sr], 3, (tm, p)))

    other_src(send_cal)

    for k in range(5):
        sub[tm, k : k + 1, :] = update[k][:, 128:]
    other_tm(lambda p: start(sub.at[tm], sub.at[tm], 7, (p, sr)))

    mr[sr] = mb[pl.ds(pl.multiple_of(block_at * MROWS, 8), MROWS), :]
    arrived(mr.at[pl.ds(0, last_sr)], 1)
    total = mr[0]
    for i in range(1, n_src):
        total = total + mr[i]
    mown[...] = total

    def add_carried():
        arrived(mr.at[pl.ds(n_src, n_src)], 2)
        total = mown[...]
        for i in range(n_src):
            total = total + mr[n_src + i]
        mown[...] = total

    pl.when(has_prev & first)(add_carried)
    for c in range(3):
        v = SLOT_AT[0, c, c]
        mown[v : v + 1, :] = mown[v : v + 1, :] + ridge_row[:, 128 * c : 128 * c + 128]
    lin = tm * n_src + block_at
    lower, upper = jnp.maximum(lin - 1, 0), jnp.minimum(lin + 1, n_tm * n_src - 1)
    has_left, has_right = lin > 0, lin < n_tm * n_src - 1
    pl.when(has_left)(lambda: start(mown, halo.at[1], 8, (lower // n_src, device_of(lower % n_src))))
    pl.when(has_right)(lambda: start(mown, halo.at[0], 9, (upper // n_src, device_of(upper % n_src))))

    pl.when(has_left)(lambda: arrived(halo.at[0], 9))
    pl.when(has_right)(lambda: arrived(halo.at[1], 8))
    br[sr] = pb[pl.ds(pl.multiple_of(block_at * 8, 8), 8), :]
    arrived(br.at[pl.ds(0, last_sr)], 4)
    basis[0] = jnp.zeros((8, 384), F32)
    total = br[0]
    for i in range(1, n_src):
        total = total + br[i]
    gt[0:8, :] = total
    trace = total[3:4, 64:65]

    def add_other(at):
        arrived(br.at[pl.ds(n_src, n_src)], at)
        total = gt[0:8, :]
        for i in range(n_src):
            total = total + br[n_src + i]
        gt[0:8, :] = total

    pl.when(has_prev & first)(lambda: add_other(5))
    pl.when(has_next & final)(lambda: add_other(6))
    lane = iota((8, 128), 1)

    def widened(centre, edge):
        return jnp.concatenate([jnp.where(lane >= 110, edge, 0.0), centre, jnp.where(lane < 18, edge, 0.0)], axis=1)

    total = gt[0:8, :]
    edge = jnp.concatenate([total[3:8], total[0:3]], axis=0)
    basis[1] = jnp.where(iota((8, 384), 0) < 3, widened(total, edge), 0.0)
    last = widened(total[6:7] + jnp.zeros((8, 128), F32), total[7:8] + jnp.zeros((8, 128), F32))[0:1]
    full = jnp.concatenate([halo[0], mown[...], halo[1]], axis=1)
    full = jnp.concatenate([full, jnp.broadcast_to(last, (8, 384))], axis=0)
    band[...] = jnp.zeros_like(band)
    for d in range(3):
        for c in range(3):
            v = SLOT_AT[0, min(c, d), max(c, d)]
            band[9 + d, c : c + 1, :] = full[v : v + 1]
    for delta in range(1, 4):
        base = SLOT_AT[delta, 0, 0]
        moved = pltpu.roll(full, delta, 1)
        for d in range(3):
            for c in range(3):
                v = base + 3 * c + d
                band[3 * (3 + delta) + d, c : c + 1, :] = full[v : v + 1]
                v = base + 3 * d + c
                band[3 * (3 - delta) + d, c : c + 1, :] = moved[v : v + 1]

    mean = trace * (1.0 / (384 * n_src * n_tm))
    centre = jnp.broadcast_to(mean * 1.2, (8, 384))
    scale = jnp.broadcast_to(2.0 / (mean * 1.1), (8, 384))

    def grow(k, carry):
        x = basis[k + 1]
        y = jnp.zeros((8, 384), F32)
        for delta in range(-3, 4):
            moved = x if delta == 0 else pltpu.roll(x, (-delta) % 384, 1)
            for d in range(3):
                y = y + band[3 * (3 + delta) + d] * moved[d : d + 1]
        image[k] = y[:, 128:256]
        basis[k + 2] = scale * (y - centre * x) - basis[k]
        return carry

    lax.fori_loop(0, CG_ITERS, grow, 0)
    own = [basis[k + 1][:, 128:256] for k in range(CG_ITERS)]
    images = [image[k] for k in range(CG_ITERS)]
    rows = [jnp.sum(own[i] * images[j], axis=0, keepdims=True) for i, j in GRAM_PAIRS]
    rows += [jnp.sum(own[0] * own[i], axis=0, keepdims=True) for i in range(CG_ITERS)]
    for e, row in enumerate(rows):
        gt[e : e + 1, :] = row
    n_gram = len(rows)
    in_gram = iota((32, 128), 0) < n_gram
    same = iota((32, 128), 0) == iota((32, 128), 1)
    sums = jnp.sum(jnp.where(in_gram, gt[...], 0.0), axis=1, keepdims=True)
    gs[0] = jnp.broadcast_to(jnp.sum(jnp.where(same, sums, 0.0), axis=0, keepdims=True), (8, 128))
    g1[sr] = gs[0]
    other_src(lambda p: start(gs.at[0], g1.at[sr], 12, (tm, p)))
    for k in range(CG_ITERS):
        xm[3 * k : 3 * k + 3, :] = own[k][0:3]

    def slab_rows(i):
        return xr.at[pl.ds(pl.multiple_of(i * XROWS, 8), XROWS)]

    other_src(lambda p: start(xm, slab_rows(block_at), 14, (tm, p)))
    pl.when(has_prev & first)(
        lambda: each(n_src, lambda i: start(xm, slab_rows(n_src), 15, (prev_tm, i)))
    )
    xr[pl.ds(pl.multiple_of(block_at * XROWS, 8), XROWS), :] = xm[...]

    def sum_cal():
        cr[sr] = cp[pl.ds(pl.multiple_of(sr * share, 8), share), :]
        arrived(cr.at[pl.ds(0, last_sr)], 3)
        total = cr[0]
        for i in range(1, n_src):
            total = total + cr[i]
        c2s[...] = total
        c2r[tm] = total
        other_tm(lambda p: start(c2s, c2r.at[tm], 10, (p, sr)))

    pl.when(owner)(sum_cal)

    def sweep(j, carry):
        row_of = iota((24, 128), 0)
        column = inv[pl.ds(pl.multiple_of(24 * j, 8), 24), :]
        pivot = jnp.sum(jnp.where(row_of == j, column, 0.0), axis=0, keepdims=True)
        over = 1.0 / pivot
        scaled = column * over
        for k in range(24):
            at = inv[24 * k : 24 * k + 24, :]
            factor = scaled[k : k + 1]
            inv[24 * k : 24 * k + 24, :] = jnp.where(row_of == j, factor, at - factor * column)
        inv[pl.ds(pl.multiple_of(24 * j, 8), 24), :] = jnp.where(row_of == j, -over, scaled)
        return carry

    arrived(g1.at[pl.ds(0, last_sr)], 12)
    total = g1[0]
    for i in range(1, n_src):
        total = total + g1[i]
    gs[1] = total
    g2[tm] = total
    other_tm(lambda p: start(gs.at[1], g2.at[tm], 13, (p, sr)))
    def finish_cal():
        arrived(c2r.at[pl.ds(0, last_tm)], 10)
        total = c2r[0]
        for i in range(1, n_tm):
            total = total + c2r[i]
        c3s[...] = total
        cf[sr] = total
        other_src(lambda p: start(c3s, cf.at[sr], 11, (tm, p)))

    pl.when(owner)(finish_cal)

    arrived(g2.at[pl.ds(0, last_tm)], 13)
    total = g2[0]
    for i in range(1, n_tm):
        total = total + g2[i]
    sums = jnp.sum(jnp.where(same, total[0:1], 0.0), axis=1, keepdims=True)
    gt[...] = jnp.broadcast_to(sums, (32, 128))
    gram_at = {pair: e for e, pair in enumerate(GRAM_PAIRS)}
    n_pairs = len(GRAM_PAIRS)

    def gram(i, j):
        e = gram_at[i, j]
        return gt[e : e + 1, :]

    weights, shares = ldl_solve(gram, lambda i: gt[n_pairs + i : n_pairs + i + 1, :], CG_ITERS)
    least = shares[0]
    for value in shares[1:]:
        least = jnp.where(value >= least, least, value)
    trust_ref[...] = jnp.where(least > TRUST, 1.0, 0.0)[:, 0:1]
    arrived(sub.at[pl.ds(0, last_tm)], 7)
    for p in range(n_tm):
        update_ref[:, lanes * p : lanes * p + lanes] = sub[p, 0:5, :]

    here_3 = jnp.concatenate([here[:n_hi].astype(F32)] * 3 + [jnp.zeros((128 - 3 * n_hi, 128), F32)], axis=0).astype(BF16)
    after_3 = jnp.concatenate([after[:n_hi].astype(F32)] * 3 + [jnp.zeros((128 - 3 * n_hi, 128), F32)], axis=0).astype(BF16)
    arrived(xr.at[pl.ds(0, XROWS * last_sr)], 14)
    pl.when(has_next)(lambda: arrived(slab_rows(n_src), 15))
    resid_b = ra[...]
    planes = []
    for c in range(3):
        plane = weights[0] * xr[pl.ds(c, n_hi, stride=XROWS), :]
        for k in range(1, CG_ITERS):
            plane = plane + weights[k] * xr[pl.ds(3 * k + c, n_hi, stride=XROWS), :]
        planes.append(plane)
        parts = [part.astype(F32) for part in pieces_3(plane)]
        parts.append(jnp.zeros((128 - 3 * n_hi, 128), F32))
        turned = jnp.concatenate(parts, axis=0).T.astype(BF16)
        at_place = dot_nn(turned, here_3)
        past_place = dot_nn(turned[:16], after_3)[:8]
        for m in range(7):
            value = jnp.sum(jnp.where(inside == m, at_place, 0.0), axis=0, keepdims=True)
            value = value + jnp.sum(jnp.where(past == m, past_place, 0.0), axis=0, keepdims=True)
            resid_b = resid_b - winp[3 * m + c] * value

    weighted = w_ref[...] * resid_b
    for k in range(24):
        vrow[k : k + 1, :] = jnp.sum(calp[k] * weighted, axis=0, keepdims=True)
    units = dot_nt(jnp.concatenate(pieces_2(vrow[...]), axis=1), unit_hot_2)
    ks[0, 0:8, :] = jnp.concatenate([units[0:8], units[8:16]], axis=1)
    ks[0, 8:16, :] = jnp.concatenate([units[16:24], jnp.zeros((8, NCU), F32)], axis=1)

    def exchange(buffer, count, me, at, place, beside=None):
        buffer[me] = ks[at]
        each(
            count - 1,
            lambda d: start(ks.at[at], buffer.at[me], 16 + at, place((me + 1 + d) % count)),
        )
        if beside is not None:
            beside()
        arrived(buffer.at[pl.ds(0, count - 1)], 16 + at)
        total = buffer[0]
        for i in range(1, count):
            total = total + buffer[i]
        ks[at + 1] = total

    def write_attitude():
        slab = jnp.concatenate(planes, axis=1)
        flat = dot_nn(jnp.concatenate(pieces_3(slab), axis=0), mixed)
        flat = flat[:n_hi] + flat[n_hi : 2 * n_hi] + flat[2 * n_hi :]
        for q in range(3):
            att_ref[pl.ds(q, n_src, stride=3), :] = flat[:n_src, 128 * q : 128 * q + 128]

    def start_inverse():
        write_attitude()
        pl.when(owner)(lambda: arrived(cf.at[pl.ds(0, n_own - 1)], 11))
        pl.when(jnp.logical_not(owner))(lambda: arrived(cf, 11))
        packed = jnp.concatenate([cf[i] for i in range(n_own)], axis=0)
        other_half = pltpu.roll(packed, 64, 1)
        for k in range(24):
            size = 24 - 8 * (k // 8)
            at = cal_row(k, 8 * (k // 8))
            part = packed[at : at + size] if k < 8 else other_half[at - 192 : at - 192 + size]
            inv[24 * k + 8 * (k // 8) : 24 * k + 24, :] = part
        for k in range(8, 24):
            size = 8 * (k // 8)
            inv[24 * k : 24 * k + size, :] = inv[pl.ds(k, size, stride=24), :]
        lax.fori_loop(0, 12, sweep, 0)

    core, xx = tm % 2, tm // 2
    exchange(kz, 2 * nz, 2 * zz + core, 0, lambda p: (2 * xx + p % 2, p // 2 * ny + yy), start_inverse)
    exchange(
        ky,
        n_tm // 2 * ny,
        xx * ny + yy,
        1,
        lambda p: (p // ny * 2 + core, zz * ny + p % ny),
        lambda: lax.fori_loop(12, 24, sweep, 0),
    )
    total = ks[2]
    right = jnp.concatenate([total[0:8, :NCU], total[0:8, NCU:], total[8:16, :NCU]], axis=0)
    calib = jnp.zeros((24, NCU), F32)
    for j in range(24):
        calib = calib - inv[24 * j : 24 * j + 24, :NCU] * right[j : j + 1]
    calib_ref[...] = calib
    spread = dot_nn(jnp.concatenate(pieces_3(calib), axis=0), unit_hot)
    spread = spread[0:24] + spread[24:48] + spread[48:72]
    out = resid_b
    for k in range(24):
        out = out - calp[k] * spread[k : k + 1]
    resid_ref[...] = out.T

    left_us(vsr.at[pl.ds(0, last_tm)], 0)
    left_us(mr.at[pl.ds(0, last_sr)], 1)
    pl.when(has_next)(lambda: left_us(mr.at[0], 2))
    pl.when(owner)(lambda: left_us(cr.at[pl.ds(0, n_own - 1)], 3))
    pl.when(jnp.logical_not(owner))(lambda: left_us(cr.at[pl.ds(0, n_own)], 3))
    left_us(br.at[pl.ds(0, last_sr)], 4)
    pl.when(has_next)(lambda: left_us(br.at[0], 5))
    pl.when(has_prev)(lambda: left_us(br.at[0], 6))
    left_us(sub.at[pl.ds(0, last_tm)], 7)
    pl.when(has_left)(lambda: left_us(mown, 8))
    pl.when(has_right)(lambda: left_us(mown, 9))
    pl.when(owner)(lambda: left_us(c2r.at[pl.ds(0, last_tm)], 10))
    pl.when(owner)(lambda: left_us(cr.at[pl.ds(0, last_sr)], 11))
    left_us(g1.at[pl.ds(0, last_sr)], 12)
    left_us(g2.at[pl.ds(0, last_tm)], 13)
    left_us(xr.at[pl.ds(0, XROWS * last_sr)], 14)
    pl.when(has_prev & first)(lambda: left_us(xr.at[pl.ds(0, XROWS * n_src)], 15))
    left_us(kz.at[pl.ds(0, 2 * nz - 1)], 16)
    left_us(ky.at[pl.ds(0, n_tm // 2 * ny - 1)], 17)


def fast_shards(
    n_tm,
    n_src,
    src_deriv,
    att_deriv,
    cal_deriv,
    obs_resid,
    obs_weight,
    src_id,
    tile_knot,
    row_offset,
    cal_unit,
    src_prior,
    att_ridge,
):
    n_hi = (n_src + 1 + 7) // 8 * 8
    groups = src_prior.shape[1]
    lanes = groups // n_tm
    per_own = 24 // min(24, n_src)
    n_own, share = 24 // per_own, 8 * (24 // min(24, n_src))
    ny = min(4, n_src)
    nz = n_src // ny
    src_planes = jnp.transpose(src_deriv, (1, 0, 2))
    att_planes = jnp.transpose(att_deriv, (1, 0, 2))
    ridge = att_ridge.reshape(3 * n_src, 128)

    def f32(*shape):
        return jax.ShapeDtypeStruct(shape, F32)

    def vmem(*shape):
        return pltpu.VMEM(shape, F32)

    whole = pl.BlockSpec(memory_space=pltpu.VMEM)
    return pl.pallas_call(
        functools.partial(joint_kernel, n_tm, n_src, n_hi),
        out_shape=[f32(5, groups), f32(3 * n_src, 128), f32(24, NCU), f32(128, 128), f32(1, 1)],
        in_specs=[whole] * 11,
        out_specs=[whole] * 5,
        scratch_shapes=[
            vmem(8, groups),
            vmem(21, 128, 128),
            vmem(5, 128, 128),
            vmem(12, 128, 128),
            vmem(24, 128, 128),
            vmem(24 * 128, 128),
            pltpu.VMEM((128, 128), jnp.int32),
            vmem(128, 128),
            vmem(128, 128),
            vmem(7, MROWS + 8, 128),
            vmem(384, 128),
            vmem(24, 128),
            vmem(n_hi * MROWS, 128),
            vmem(n_hi, 128),
            vmem(192, 128),
            vmem(n_tm, 24, 128),
            vmem(2 * n_src, MROWS, 128),
            vmem(MROWS, 128),
            vmem(2, MROWS, 128),
            vmem(21, 8, 384),
            vmem(n_hi * 8, 128),
            vmem(2 * n_src, 8, 128),
            vmem(CG_ITERS + 2, 8, 384),
            vmem(CG_ITERS, 8, 128),
            vmem(2, 8, 128),
            vmem(n_src, 8, 128),
            vmem(n_tm, 8, 128),
            vmem(32, 128),
            vmem(XROWS, 128),
            vmem(n_hi * XROWS, 128),
            vmem(n_tm, 8, lanes),
            vmem(n_src, share, 128),
            vmem(share, 128),
            vmem(n_tm, share, 128),
            vmem(share, 128),
            vmem(n_own, share, 128),
            vmem(576, 128),
            vmem(128, 128),
            vmem(24, 128),
            vmem(2 * nz, 16, 128),
            vmem(n_tm // 2 * ny, 16, 128),
            vmem(3, 16, 128),
            pltpu.SemaphoreType.DMA((18,)),
            pltpu.SemaphoreType.DMA((18,)),
        ],
        compiler_params=pltpu.CompilerParams(
            collective_id=0, has_side_effects=True, vmem_limit_bytes=48 << 20
        ),
        name="joint_solve",
    )(src_planes, att_planes, cal_deriv, obs_resid, obs_weight, row_offset, *(a.reshape(1, 128) for a in (src_id, tile_knot, cal_unit)), src_prior, ridge)


def hand_over(arrays):
    count = len(arrays)

    def kernel(*refs):
        for i in range(count):
            refs[count + i][...] = refs[i][...]

    whole = pl.BlockSpec(memory_space=pltpu.VMEM)
    return pl.pallas_call(
        kernel,
        out_shape=[jax.ShapeDtypeStruct(a.shape, a.dtype) for a in arrays],
        in_specs=[whole] * count,
        out_specs=[whole] * count,
        name="hand_over",
    )(*arrays)


def guarded_shards(n_tm, n_src, *arrays):
    update, attitude, calib, resid, trust = fast_shards(n_tm, n_src, *arrays)
    fast = (update, attitude, calib, resid)

    def slow():
        update, attitude, calib, resid = shards(*arrays)
        return update, attitude.reshape(-1, 128), calib, resid

    update, attitude, calib, resid = hand_over(lax.cond(trust[0, 0] > 0.5, lambda: fast, slow))
    return update, attitude.reshape(-1), calib, resid


def solution(mesh):
    placed = (
        P(("tm", "src"), None, None),
        P(("tm", "src"), None, None),
        P(("tm", "src"), None, None),
        P(("tm", "src"), None),
        P(("tm", "src"), None),
        P(("tm", "src")),
        P(("tm", "src")),
        P(("tm", "src"), None),
        P(("tm", "src")),
        P(None, "src"),
        P("tm"),
    )
    return jax.shard_map(
        functools.partial(guarded_shards, mesh.shape["tm"], mesh.shape["src"]),
        mesh=mesh,
        in_specs=placed,
        out_specs=(P(None, "src"), P("tm"), P(), P(("tm", "src"), None)),
        check_vma=False,
    )
```

```python
import functools

import jax
import jax.numpy as jnp
import numpy as np
from jax import lax
from jax.experimental import pallas as pl
from jax.experimental.pallas import tpu as pltpu
from jax.sharding import PartitionSpec as P

NCU = 64
CG_ITERS = 6


HIGH = lax.Precision.HIGHEST


def padded_2(cells, sides, width):
    for axis, dim in sides:
        count = lax.axis_size(axis)
        ends = count - 1
        head = lax.slice_in_dim(cells, 0, width, axis=dim)
        tail = lax.slice_in_dim(cells, cells.shape[dim] - width, cells.shape[dim], axis=dim)
        cells = jnp.concatenate(
            [
                lax.ppermute(tail, axis, [(i, (i + 1) % count) for i in range(ends)]),
                cells,
                lax.ppermute(head, axis, [((i + 1) % count, i) for i in range(ends)]),
            ],
            axis=dim,
        )
    return cells


def all_sum(array, axis):
    devices, step = lax.axis_size(axis), 1
    while step < devices:
        array = array + lax.ppermute(array, axis, [(i, i ^ step) for i in range(devices)])
        step *= 2
    return array


def from_behind(array, axis, by):
    devices = lax.axis_size(axis)
    pairs = [(i, i + by) for i in range(devices) if 0 <= i + by < devices]
    return lax.ppermute(array, axis, pairs)


def lag_table():
    first_index = np.arange(21)[None, :]
    lag_rows = np.arange(12)[:, None]
    second = first_index + lag_rows
    flat_index = first_index * 21 + np.minimum(second, 20)
    return (flat_index, (second < 21).astype(np.float32))


def solve_spd(matrix, right):
    order = right.shape[0]
    rows = jnp.arange(order)[:, None]

    def column(j, state):
        rest, factor = state
        col = jnp.where(rows >= j, rest[:, j] / jnp.sqrt(rest[j, j]), 0.0)
        return rest - col[:, None, :] * col[None, :, :], factor.at[:, j].set(col)

    factor = lax.fori_loop(0, order, column, (matrix, jnp.zeros_like(matrix)))[1]

    def forward(i, answer):
        value = right[i] - jnp.sum(jnp.where(rows < i, factor[i] * answer, 0.0), axis=0)
        return answer.at[i].set(value / factor[i, i])

    halfway = lax.fori_loop(0, order, forward, jnp.zeros_like(right))

    def backward(step, answer):
        i = order - 1 - step
        value = halfway[i] - jnp.sum(jnp.where(rows > i, factor[:, i] * answer, 0.0), axis=0)
        return answer.at[i].set(value / factor[i, i])

    return lax.fori_loop(0, order, backward, jnp.zeros_like(right))


def tile_normals(deriv, weight, resid):
    values = deriv.astype(jnp.float32)
    weighted = values * weight[:, None, :]
    normal = jnp.einsum("tkr,tlr->tkl", weighted, values, precision=HIGH)
    right = jnp.einsum("tkr,tr->tk", weighted, resid, precision=HIGH)
    return jnp.concatenate([normal.reshape(normal.shape[0], -1), right], axis=1)


def small_solve(sums, prior, order):
    count = sums.shape[1]
    matrix = sums[: order * order].reshape(order, order, count)
    if prior is not None:
        matrix = matrix + jnp.eye(order, dtype=jnp.float32)[:, :, None] * prior[:, None, :]
    return solve_spd(matrix, sums[order * order :])


def window_rows(att_deriv, row_offset):
    values = att_deriv.astype(jnp.float32)
    window = jnp.zeros((values.shape[0], 21, values.shape[2]), jnp.float32)
    for knot_step in range(4):
        placed = jnp.pad(values, ((0, 0), (3 * knot_step, 9 - 3 * knot_step), (0, 0)))
        window = window + jnp.where((row_offset == knot_step)[:, None, :], placed, 0.0)
    return window


def attitude_terms(window, weight, resid):
    weighted = window * weight[:, None, :]
    normal = jnp.einsum("tjr,tlr->tjl", weighted, window, precision=HIGH)
    right = jnp.einsum("tjr,tr->tj", weighted, resid, precision=HIGH)
    flat_index, valid_lag = lag_table()
    banded = normal.reshape(normal.shape[0], 441)[:, flat_index] * valid_lag
    return jnp.concatenate([banded, right[:, None, :]], axis=1)


def conjugate(band_rows, right, ridge_part, band_edge, extend, inner_sum):
    count = right.shape[0]
    lagged = jnp.concatenate([band_edge, band_rows[1:]], axis=1)
    solution = jnp.zeros_like(right)
    residual = right
    direction = right
    norm_now = inner_sum(residual, residual)
    for iteration in range(CG_ITERS):
        padded = extend(direction)
        result = ridge_part * direction
        for d in range(12):
            result = result + band_rows[d] * padded[11 + d : 11 + d + count]
        for d in range(1, 12):
            result = (
                result + lagged[d - 1, 11 - d : 11 - d + count] * padded[11 - d : 11 - d + count]
            )
        step_size = norm_now / inner_sum(direction, result)
        solution = solution + step_size * direction
        residual = residual - step_size * result
        norm_next = inner_sum(residual, residual)
        direction = residual + norm_next / norm_now * direction
        norm_now = norm_next
    return solution


def slab_extend(vector):
    return padded_2(vector, (("tm", 0),), 11)


def slab_dot(first_vec, second_vec):
    return all_sum(jnp.sum(first_vec * second_vec), "tm")


def shards(
    src_deriv,
    att_deriv,
    cal_deriv,
    obs_resid,
    obs_weight,
    src_id,
    tile_knot,
    row_offset,
    cal_unit,
    src_prior,
    att_ridge,
):
    slab_pos = lax.axis_index("tm")
    groups = src_prior.shape[1]
    normal_sums = jax.ops.segment_sum(
        tile_normals(src_deriv, obs_weight, obs_resid), src_id, num_segments=groups
    ).T
    summed = all_sum(normal_sums, "tm")
    source_update = small_solve(summed, src_prior, 5)
    resid_a = obs_resid - jnp.einsum(
        "tkr,kt->tr", src_deriv.astype(jnp.float32), source_update[:, src_id], precision=HIGH
    )
    slab_params = att_ridge.shape[0]
    window = window_rows(att_deriv, row_offset)
    local_knot = tile_knot - slab_pos * (slab_params // 3)
    columns = 3 * local_knot[:, None] + jnp.arange(21, dtype=jnp.int32)[None, :]
    values = attitude_terms(window, obs_weight, resid_a)
    slab_sums = jax.ops.segment_sum(
        values.transpose(0, 2, 1).reshape(-1, 13),
        columns.reshape(-1),
        num_segments=slab_params + 21,
    ).T
    carried = from_behind(slab_sums[:, slab_params:], "tm", 1)
    head_sums = slab_sums[:, :slab_params].at[:, :21].add(carried)
    summed_band = all_sum(head_sums, "src")
    band_edge = from_behind(summed_band[1:12, -11:], "tm", 1)
    attitude_update = conjugate(
        summed_band[:12], summed_band[12], att_ridge, band_edge, slab_extend, slab_dot
    )
    next_params = from_behind(attitude_update[:21], "tm", -1)
    extended = jnp.concatenate([attitude_update, next_params])
    resid_b = resid_a - jnp.einsum("tjr,tj->tr", window, extended[columns], precision=HIGH)
    calib_sums = jax.ops.segment_sum(
        tile_normals(cal_deriv, obs_weight, resid_b), cal_unit, num_segments=NCU
    ).T
    calib_total = all_sum(all_sum(calib_sums, "tm"), "src")
    calib_update = small_solve(calib_total, None, 24)
    residual_out = resid_b - jnp.einsum(
        "tkr,kt->tr", cal_deriv.astype(jnp.float32), calib_update[:, cal_unit], precision=HIGH
    )
    return (source_update, attitude_update, calib_update, residual_out)


F32 = jnp.float32
BF16 = jnp.bfloat16
MESH = pl.DeviceIdType.MESH
MROWS = 32
XROWS = 18
TRUST = 0.01


def pieces_2(x):
    high = x.astype(BF16)
    return high, (x - high.astype(F32)).astype(BF16)


def pieces_3(x):
    high = x.astype(BF16)
    rest = x - high.astype(F32)
    mid = rest.astype(BF16)
    return high, mid, (rest - mid.astype(F32)).astype(BF16)


def dot_nn(a, b):
    return lax.dot_general(a, b, (((1,), (0,)), ((), ())), preferred_element_type=F32)


def dot_nt(a, b):
    return lax.dot_general(a, b, (((1,), (1,)), ((), ())), preferred_element_type=F32)


def iota(shape, dim):
    return lax.broadcasted_iota(jnp.int32, shape, dim)


def hot(match):
    return jnp.where(match, 1.0, 0.0).astype(BF16)


def band_slots():
    slots = [(0, c, d) for c in range(3) for d in range(c, 3)]
    for delta in range(1, 4):
        slots += [(delta, c, d) for c in range(3) for d in range(3)]
    return slots


SLOTS = band_slots()
SLOT_AT = {slot: v for v, slot in enumerate(SLOTS)}
SRC_PAIRS = [(k, l) for k in range(5) for l in range(k, 5)]
SRC_AT = {pair: e for e, pair in enumerate(SRC_PAIRS)}
GRAM_PAIRS = [(i, j) for i in range(CG_ITERS) for j in range(i, CG_ITERS)]


def cal_row(k, l):
    if k < 8:
        return 24 * k + l
    if k < 16:
        return 192 + 16 * (k - 8) + l - 8
    return 320 + 8 * (k - 16) + l - 16


def place_lanes(lo_row):
    inside = iota((128, 128), 0) - lo_row
    return inside, iota((8, 128), 0) + 128 - lo_row


def ldl_solve(entry, right, order):
    low = {}
    pivots, inverse, shares = [], [], []
    for j in range(order):
        pivot = entry(j, j)
        for m in range(j):
            pivot = pivot - low[j, m] * low[j, m] * pivots[m]
        shares.append(pivot / entry(j, j))
        pivots.append(pivot)
        inverse.append(1.0 / pivot)
        for i in range(j + 1, order):
            value = entry(j, i)
            for m in range(j):
                value = value - low[i, m] * (low[j, m] * pivots[m])
            low[i, j] = value * inverse[j]
    forward = []
    for i in range(order):
        value = right(i)
        for m in range(i):
            value = value - low[i, m] * forward[m]
        forward.append(value)
    answer = [None] * order
    for i in range(order - 1, -1, -1):
        value = forward[i] * inverse[i]
        for m in range(i + 1, order):
            value = value - low[m, i] * answer[m]
        answer[i] = value
    return answer, shares


def joint_kernel(
    n_tm,
    n_src,
    n_hi,
    src_ref,
    att_in_ref,
    cal_ref,
    resid_in_ref,
    weight_ref,
    offset_ref,
    id_ref,
    knot_ref,
    unit_ref,
    raw_prior_ref,
    ridge_ref,
    update_ref,
    att_ref,
    calib_ref,
    resid_ref,
    trust_ref,
    prior_ref,
    winp,
    srcp,
    attp,
    calp,
    calf,
    offp,
    w_ref,
    r_ref,
    vm,
    vc,
    vs,
    mb,
    ex,
    cp,
    vsr,
    mr,
    mown,
    halo,
    band,
    pb,
    br,
    basis,
    image,
    gs,
    g1,
    g2,
    gt,
    xm,
    xr,
    sub,
    cr,
    c2s,
    c2r,
    c3s,
    cf,
    inv,
    ra,
    vrow,
    kz,
    ky,
    ks,
    send,
    recv,
):
    tm, sr = lax.axis_index("tm"), lax.axis_index("src")
    last_tm, last_sr = n_tm - 1, n_src - 1
    has_next, has_prev = tm < last_tm, tm > 0
    ny = min(4, n_src)
    nz = n_src // ny
    yy, zz = sr % ny, sr // ny
    per_own = 24 // min(24, n_src)
    n_own = 24 // per_own
    share = 8 * per_own
    owner = sr < n_own

    def block_of(p):
        return p // ny * ny + (p % ny + p // ny) % ny

    def device_of(b):
        return b // ny * ny + (b % ny + nz * ny - b // ny) % ny

    block_at = block_of(sr)
    final_sr = device_of(last_sr)
    first, final = sr == 0, sr == final_sr
    lanes = prior_ref.shape[1] // n_tm

    def start(source, target, at, place):
        pltpu.make_async_remote_copy(
            src_ref=source,
            dst_ref=target,
            send_sem=send.at[at],
            recv_sem=recv.at[at],
            device_id=place,
            device_id_type=MESH,
        ).start()

    def arrived(part, at):
        pltpu.make_async_copy(part, part, recv.at[at]).wait()

    def left_us(part, at):
        pltpu.make_async_copy(part, part, send.at[at]).wait()

    def each(count, body):
        def run(d, carry):
            body(d)
            return carry

        lax.fori_loop(0, count, run, 0)

    def other_src(body):
        each(last_sr, lambda d: body((sr + 1 + d) % n_src))

    def other_tm(body):
        each(last_tm, lambda d: body((tm + 1 + d) % n_tm))

    next_tm, prev_tm = jnp.minimum(tm + 1, last_tm), jnp.maximum(tm - 1, 0)
    halo[...] = jnp.zeros_like(halo)
    xr[n_src:] = jnp.zeros((n_hi - n_src, XROWS, 128), F32)

    barrier = pltpu.get_barrier_semaphore()

    def greet(a, b):
        pl.semaphore_signal(barrier, inc=1, device_id=(a, b), device_id_type=MESH)

    other_tm(lambda p: greet(p, sr))
    other_src(lambda p: greet(tm, p))

    w_ref[...] = weight_ref[...].T
    r_ref[...] = resid_in_ref[...].T
    offp[...] = offset_ref[...].astype(F32).T.astype(jnp.int32)
    for k in range(5):
        srcp[k] = src_ref[k].astype(F32).T
    for k in range(12):
        attp[k] = att_in_ref[k].astype(F32).T
    vm[...] = jnp.zeros_like(vm)
    prior_ref[...] = jnp.ones_like(prior_ref)
    prior_ref[0:5, :] = raw_prior_ref[...]
    pb[...] = jnp.zeros_like(pb)

    def windows(i, carry):
        rows = pl.ds(pl.multiple_of(i * 16, 16), 16)
        values = [attp[k, rows, :] for k in range(12)]
        step = offp[rows, :]
        for j in range(21):
            placed = jnp.zeros((16, 128), F32)
            for o in range(4):
                if 0 <= j - 3 * o < 12:
                    placed = jnp.where(step == o, values[j - 3 * o], placed)
            winp[j, rows, :] = placed
        return carry

    lax.fori_loop(0, 8, windows, 0)

    def summed(count, terms):
        def body(i, sums):
            rows = pl.ds(pl.multiple_of(i * 8, 8), 8)
            return tuple(s + t for s, t in zip(sums, terms(rows)))

        sums = lax.fori_loop(0, 16, body, tuple(jnp.zeros((8, 128), F32) for _ in range(count)))
        return [jnp.sum(s, axis=0, keepdims=True) for s in sums]

    def src_terms(rows):
        x = [srcp[k, rows, :] for k in range(5)]
        w = w_ref[rows, :]
        y = [w * v for v in x]
        r = r_ref[rows, :]
        return [y[k] * x[l] for k, l in SRC_PAIRS] + [v * r for v in y]

    vs[...] = jnp.zeros_like(vs)
    for e, row in enumerate(summed(20, src_terms)):
        vs[e : e + 1, :] = row
    vs[20:21, :] = id_ref[...].astype(F32)

    trace = jnp.sum(ridge_ref[...], axis=0, keepdims=True) * (1.0 / n_src)
    for m in range(7):
        slots = [s for s in SLOTS if m + s[0] < 7]

        def att_terms(rows, m=m, slots=slots):
            x = [winp[j, rows, :] for j in range(3 * m, min(3 * m + 12, 21))]
            w = w_ref[rows, :]
            y = [w * x[c] for c in range(3)]
            return [y[c] * x[3 * delta + d] for delta, c, d in slots]

        for slot, row in zip(slots, summed(len(slots), att_terms)):
            vm[m, SLOT_AT[slot] : SLOT_AT[slot] + 1, :] = row
            if slot[0] == 0 and slot[1] == slot[2]:
                trace = trace + row
    vs[21:22, :] = trace

    pl.semaphore_wait(barrier, last_tm + last_sr)
    other_tm(lambda p: start(vs, vsr.at[tm], 0, (p, sr)))

    knot = knot_ref[...] - tm * (128 * n_src)
    block, place = knot >> 7, knot & 127
    inside, past = place_lanes(place)
    blocks = iota((n_hi + 8, 128), 0)
    here, after = hot(blocks == block), hot(blocks == block + 1)
    spreads = jnp.concatenate([here, here, after, after], axis=1)
    rest = jnp.zeros((120, 128), F32)

    def spread_rows(row_of, count):
        spread = jnp.zeros((128, 128), F32)
        over = jnp.zeros((8, 128), F32)
        for m in range(count):
            row = row_of(m)
            spread = jnp.where(inside == m, row, spread)
            over = jnp.where(past == m, row, over)
        over = jnp.concatenate([over, rest], axis=0)
        right = jnp.concatenate(pieces_2(spread) + pieces_2(over), axis=1)
        return dot_nt(spreads, right)[:n_hi]

    def band_rows(j, at=0, size=MROWS):
        return mb.at[pl.ds(pl.multiple_of(j * MROWS + at, 8), size)]

    half = MROWS // 2
    for v, (delta, c, d) in enumerate(SLOTS):
        rows = spread_rows(lambda m, v=v: vm[m, v : v + 1, :], 7 - delta)
        if v < MROWS:
            mb[pl.ds(v, n_hi, stride=MROWS), :] = rows
            if v + 1 in (half, MROWS):
                at, sem = v + 1 - half, 1 if v < half else 18
                other_src(
                    lambda p, at=at, sem=sem: start(
                        band_rows(block_of(p), at, half), mr.at[sr, pl.ds(at, half)], sem, (tm, p)
                    )
                )
        else:
            ex[...] = rows


    ids = jnp.broadcast_to(id_ref[...].astype(F32), (128, 128)).T
    sources = (iota((lanes, 128), 0) + tm * lanes).astype(F32)
    wanted = jnp.concatenate([ids, sources], axis=0)
    groups = prior_ref.shape[1]
    source_hot = hot(iota((groups, 128), 0) == id_ref[...])
    owned = dot_nn(jnp.concatenate(pieces_3(prior_ref[...]), axis=0), source_hot)
    owned = owned[0:8] + owned[8:16] + owned[16:24]


    vsr[tm] = vs[...]
    arrived(vsr.at[pl.ds(0, last_tm)], 0)
    pl.when(has_next)(lambda: start(band_rows(n_src), mr.at[n_src + sr], 2, (next_tm, 0)))
    normal = jnp.zeros((48, 128 + lanes), F32)
    for p in range(0, n_tm, 2):
        match = [hot(wanted == vsr[q, 20:21, :]) for q in (p, p + 1)]
        parts = [pieces_2(vsr[q]) for q in (p, p + 1)]
        left = jnp.concatenate([jnp.concatenate([part[i] for part in parts], axis=1) for i in range(2)], axis=0)
        normal = normal + dot_nt(left, jnp.concatenate(match, axis=1))
    normal = normal[:24] + normal[24:]
    trace = sum(vsr[p, 21:22, :] for p in range(n_tm))
    prior = jnp.concatenate([owned, prior_ref[:, pl.ds(pl.multiple_of(tm * lanes, 128), lanes)]], axis=1)

    def source_entry(k, l):
        row = SRC_AT[k, l]
        value = normal[row : row + 1]
        return value + prior[k : k + 1] if k == l else value

    update, _ = ldl_solve(source_entry, lambda k: normal[15 + k : 16 + k], 5)
    resid_a = r_ref[...]
    for k in range(5):
        resid_a = resid_a - srcp[k] * update[k][:, :128]
    ra[...] = resid_a
    weighted = w_ref[...] * resid_a
    for j in range(21):
        vrow[j : j + 1, :] = jnp.sum(winp[j] * weighted, axis=0, keepdims=True)

    lane = iota((n_hi, 128), 1)

    def put_blocks(rows, centre_at, edge_at, extra=None):
        edges = jnp.where(lane < 64, pltpu.roll(rows, n_hi - 1, 0), pltpu.roll(rows, 1, 0))
        if extra is not None:
            edges = jnp.where((lane == 64) & (iota((n_hi, 128), 0) < n_src), extra, edges)
        pb[pl.ds(centre_at, n_hi, stride=8), :] = rows
        pb[pl.ds(edge_at, n_hi, stride=8), :] = edges

    trace = jnp.sum(trace, axis=1, keepdims=True)
    for c in range(3):
        rows = spread_rows(lambda m, c=c: vrow[3 * m + c : 3 * m + c + 1, :], 7)
        put_blocks(rows, c, 3 + c, trace if c == 0 else None)
    put_blocks(ex[...], 6, 7)

    def right_rows(j):
        return pb.at[pl.ds(pl.multiple_of(j * 8, 8), 8)]

    other_src(lambda p: start(right_rows(block_of(p)), br.at[sr], 4, (tm, p)))
    pl.when(has_next)(lambda: start(right_rows(n_src), br.at[n_src + sr], 5, (next_tm, 0)))
    pl.when(has_prev)(lambda: start(right_rows(n_hi - 1), br.at[n_src + sr], 6, (prev_tm, final_sr)))

    flat_at, plane_at = iota((384, 384), 1), iota((384, 384), 0)
    mixed = hot(flat_at == 3 * (plane_at & 127) + (plane_at >> 7))
    flat_ridge = jnp.concatenate([ridge_ref[pl.ds(3 * block_at + q, 1), :] for q in range(3)], axis=1)
    ridge_row = sum(dot_nt(jnp.broadcast_to(part, (16, 384)), mixed)[0:1] for part in pieces_3(flat_ridge))
    calf[...] = cal_ref[...].astype(F32).reshape(128 * 24, 128)
    for k in range(24):
        calp[k] = calf[pl.ds(k, 128, stride=24), :].T
    for kg in range(6):
        for lg in range(kg // 2, 3):

            def cal_terms(rows, kg=kg, lg=lg):
                w = w_ref[rows, :]
                y = [w * calp[4 * kg + k, rows, :] for k in range(4)]
                x = [calp[8 * lg + l, rows, :] for l in range(8)]
                return [y[k] * x[l] for k in range(4) for l in range(8)]

            sums = summed(32, cal_terms)
            for k in range(4):
                at = cal_row(4 * kg + k, 8 * lg)
                vc[at : at + 8, :] = jnp.concatenate(sums[8 * k : 8 * k + 8], axis=0)
    unit_hot = hot(iota((NCU, 128), 0) == unit_ref[...])
    unit_hot_2 = jnp.concatenate([unit_hot, unit_hot], axis=1)
    units = dot_nt(jnp.concatenate(pieces_2(vc[...]), axis=1), unit_hot_2)
    cp[...] = jnp.concatenate([units[:192], units[192:]], axis=1)

    def cal_share(p):
        return cp.at[pl.ds(pl.multiple_of(p * share, 8), share)]

    def send_cal(p):
        pl.when(p < n_own)(lambda: start(cal_share(p), cr.at[sr], 3, (tm, p)))

    other_src(send_cal)

    for k in range(5):
        sub[tm, k : k + 1, :] = update[k][:, 128:]
    other_tm(lambda p: start(sub.at[tm], sub.at[tm], 7, (p, sr)))

    mr[sr] = mb[pl.ds(pl.multiple_of(block_at * MROWS, 8), MROWS), :]
    arrived(mr.at[pl.ds(0, last_sr), pl.ds(0, half)], 1)
    arrived(mr.at[pl.ds(0, last_sr), pl.ds(0, half)], 18)
    total = mr[0]
    for i in range(1, n_src):
        total = total + mr[i]
    mown[...] = total

    def add_carried():
        arrived(mr.at[pl.ds(n_src, n_src)], 2)
        total = mown[...]
        for i in range(n_src):
            total = total + mr[n_src + i]
        mown[...] = total

    pl.when(has_prev & first)(add_carried)
    for c in range(3):
        v = SLOT_AT[0, c, c]
        mown[v : v + 1, :] = mown[v : v + 1, :] + ridge_row[:, 128 * c : 128 * c + 128]
    lin = tm * n_src + block_at
    lower, upper = jnp.maximum(lin - 1, 0), jnp.minimum(lin + 1, n_tm * n_src - 1)
    has_left, has_right = lin > 0, lin < n_tm * n_src - 1
    pl.when(has_left)(lambda: start(mown, halo.at[1], 8, (lower // n_src, device_of(lower % n_src))))
    pl.when(has_right)(lambda: start(mown, halo.at[0], 9, (upper // n_src, device_of(upper % n_src))))

    pl.when(has_left)(lambda: arrived(halo.at[0], 9))
    pl.when(has_right)(lambda: arrived(halo.at[1], 8))
    br[sr] = pb[pl.ds(pl.multiple_of(block_at * 8, 8), 8), :]
    arrived(br.at[pl.ds(0, last_sr)], 4)
    basis[0] = jnp.zeros((8, 384), F32)
    total = br[0]
    for i in range(1, n_src):
        total = total + br[i]
    gt[0:8, :] = total
    trace = total[3:4, 64:65]

    def add_other(at):
        arrived(br.at[pl.ds(n_src, n_src)], at)
        total = gt[0:8, :]
        for i in range(n_src):
            total = total + br[n_src + i]
        gt[0:8, :] = total

    pl.when(has_prev & first)(lambda: add_other(5))
    pl.when(has_next & final)(lambda: add_other(6))
    lane = iota((8, 128), 1)

    def widened(centre, edge):
        return jnp.concatenate([jnp.where(lane >= 110, edge, 0.0), centre, jnp.where(lane < 18, edge, 0.0)], axis=1)

    total = gt[0:8, :]
    edge = jnp.concatenate([total[3:8], total[0:3]], axis=0)
    basis[1] = jnp.where(iota((8, 384), 0) < 3, widened(total, edge), 0.0)
    last = widened(total[6:7] + jnp.zeros((8, 128), F32), total[7:8] + jnp.zeros((8, 128), F32))[0:1]
    full = jnp.concatenate([halo[0], mown[...], halo[1]], axis=1)
    full = jnp.concatenate([full, jnp.broadcast_to(last, (8, 384))], axis=0)
    band[...] = jnp.zeros_like(band)
    for d in range(3):
        for c in range(3):
            v = SLOT_AT[0, min(c, d), max(c, d)]
            band[9 + d, c : c + 1, :] = full[v : v + 1]
    for delta in range(1, 4):
        base = SLOT_AT[delta, 0, 0]
        moved = pltpu.roll(full, delta, 1)
        for d in range(3):
            for c in range(3):
                v = base + 3 * c + d
                band[3 * (3 + delta) + d, c : c + 1, :] = full[v : v + 1]
                v = base + 3 * d + c
                band[3 * (3 - delta) + d, c : c + 1, :] = moved[v : v + 1]

    mean = trace * (1.0 / (384 * n_src * n_tm))
    centre = jnp.broadcast_to(mean * 1.2, (8, 384))
    scale = jnp.broadcast_to(2.0 / (mean * 1.1), (8, 384))

    def grow(k, carry):
        x = basis[k + 1]
        y = jnp.zeros((8, 384), F32)
        for delta in range(-3, 4):
            moved = x if delta == 0 else pltpu.roll(x, (-delta) % 384, 1)
            for d in range(3):
                y = y + band[3 * (3 + delta) + d] * moved[d : d + 1]
        image[k] = y[:, 128:256]
        basis[k + 2] = scale * (y - centre * x) - basis[k]
        return carry

    lax.fori_loop(0, CG_ITERS, grow, 0)
    own = [basis[k + 1][:, 128:256] for k in range(CG_ITERS)]
    images = [image[k] for k in range(CG_ITERS)]
    rows = [jnp.sum(own[i] * images[j], axis=0, keepdims=True) for i, j in GRAM_PAIRS]
    rows += [jnp.sum(own[0] * own[i], axis=0, keepdims=True) for i in range(CG_ITERS)]
    for e, row in enumerate(rows):
        gt[e : e + 1, :] = row
    n_gram = len(rows)
    in_gram = iota((32, 128), 0) < n_gram
    same = iota((32, 128), 0) == iota((32, 128), 1)
    sums = jnp.sum(jnp.where(in_gram, gt[...], 0.0), axis=1, keepdims=True)
    gs[0] = jnp.broadcast_to(jnp.sum(jnp.where(same, sums, 0.0), axis=0, keepdims=True), (8, 128))
    core, xx = tm % 2, tm // 2
    g1[2 * zz + core] = gs[0]
    each(
        2 * nz - 1,
        lambda d: start(
            gs.at[0],
            g1.at[2 * zz + core],
            12,
            (2 * xx + (2 * zz + core + 1 + d) % 2, (2 * zz + core + 1 + d) % (2 * nz) // 2 * ny + yy),
        ),
    )
    for k in range(CG_ITERS):
        xm[3 * k : 3 * k + 3, :] = own[k][0:3]

    def slab_rows(i):
        return xr.at[i]

    other_src(lambda p: start(xm, slab_rows(block_at), 14, (tm, p)))
    pl.when(has_prev & first)(
        lambda: each(n_src, lambda i: start(xm, slab_rows(n_src), 15, (prev_tm, i)))
    )
    xr[block_at] = xm[...]

    def sum_cal():
        cr[sr] = cp[pl.ds(pl.multiple_of(sr * share, 8), share), :]
        arrived(cr.at[pl.ds(0, last_sr)], 3)
        total = cr[0]
        for i in range(1, n_src):
            total = total + cr[i]
        c2s[...] = total
        c2r[tm] = total
        other_tm(lambda p: start(c2s, c2r.at[tm], 10, (p, sr)))

    pl.when(owner)(sum_cal)

    def sweep(j, carry):
        row_of = iota((24, 128), 0)
        column = inv[pl.ds(pl.multiple_of(24 * j, 8), 24), :]
        pivot = jnp.sum(jnp.where(row_of == j, column, 0.0), axis=0, keepdims=True)
        over = 1.0 / pivot
        scaled = column * over
        for k in range(24):
            at = inv[24 * k : 24 * k + 24, :]
            factor = scaled[k : k + 1]
            inv[24 * k : 24 * k + 24, :] = jnp.where(row_of == j, factor, at - factor * column)
        inv[pl.ds(pl.multiple_of(24 * j, 8), 24), :] = jnp.where(row_of == j, -over, scaled)
        return carry

    arrived(g1.at[pl.ds(0, 2 * nz - 1)], 12)
    total = g1[0]
    for i in range(1, 2 * nz):
        total = total + g1[i]
    gs[1] = total
    n_xy = n_tm // 2 * ny
    at_xy = xx * ny + yy
    g2[at_xy] = total
    each(
        n_xy - 1,
        lambda d: start(
            gs.at[1],
            g2.at[at_xy],
            13,
            ((at_xy + 1 + d) % n_xy // ny * 2 + core, zz * ny + (at_xy + 1 + d) % n_xy % ny),
        ),
    )
    def finish_cal():
        arrived(c2r.at[pl.ds(0, last_tm)], 10)
        total = c2r[0]
        for i in range(1, n_tm):
            total = total + c2r[i]
        c3s[...] = total
        cf[sr] = total
        other_src(lambda p: start(c3s, cf.at[sr], 11, (tm, p)))

    pl.when(owner)(finish_cal)

    arrived(g2.at[pl.ds(0, n_xy - 1)], 13)
    total = g2[0]
    for i in range(1, n_xy):
        total = total + g2[i]
    sums = jnp.sum(jnp.where(same, total[0:1], 0.0), axis=1, keepdims=True)
    gt[...] = jnp.broadcast_to(sums, (32, 128))
    gram_at = {pair: e for e, pair in enumerate(GRAM_PAIRS)}
    n_pairs = len(GRAM_PAIRS)

    def gram(i, j):
        e = gram_at[i, j]
        return gt[e : e + 1, :]

    weights, shares = ldl_solve(gram, lambda i: gt[n_pairs + i : n_pairs + i + 1, :], CG_ITERS)
    least = shares[0]
    for value in shares[1:]:
        least = jnp.where(value >= least, least, value)
    trust_ref[...] = jnp.where(least > TRUST, 1.0, 0.0)[:, 0:1]
    arrived(sub.at[pl.ds(0, last_tm)], 7)
    for p in range(n_tm):
        update_ref[:, lanes * p : lanes * p + lanes] = sub[p, 0:5, :]

    here_3 = jnp.concatenate([here[:n_hi].astype(F32)] * 3 + [jnp.zeros((128 - 3 * n_hi, 128), F32)], axis=0).astype(BF16)
    after_3 = jnp.concatenate([after[:n_hi].astype(F32)] * 3 + [jnp.zeros((128 - 3 * n_hi, 128), F32)], axis=0).astype(BF16)
    arrived(xr.at[pl.ds(0, last_sr)], 14)
    pl.when(has_next)(lambda: arrived(slab_rows(n_src), 15))
    resid_b = ra[...]
    planes = []
    for c in range(3):
        plane = weights[0] * xr[:, c, :]
        for k in range(1, CG_ITERS):
            plane = plane + weights[k] * xr[:, 3 * k + c, :]
        planes.append(plane)
        parts = [part.astype(F32) for part in pieces_3(plane)]
        parts.append(jnp.zeros((128 - 3 * n_hi, 128), F32))
        turned = jnp.concatenate(parts, axis=0).T.astype(BF16)
        at_place = dot_nn(turned, here_3)
        past_place = dot_nn(turned[:16], after_3)[:8]
        for m in range(7):
            value = jnp.sum(jnp.where(inside == m, at_place, 0.0), axis=0, keepdims=True)
            value = value + jnp.sum(jnp.where(past == m, past_place, 0.0), axis=0, keepdims=True)
            resid_b = resid_b - winp[3 * m + c] * value

    weighted = w_ref[...] * resid_b
    for k in range(24):
        vrow[k : k + 1, :] = jnp.sum(calp[k] * weighted, axis=0, keepdims=True)
    units = dot_nt(jnp.concatenate(pieces_2(vrow[...]), axis=1), unit_hot_2)
    ks[0] = jnp.concatenate([units[0:12], units[12:24]], axis=1)

    def exchange(buffer, count, me, at, place, beside=None):
        buffer[me] = ks[at]
        each(
            count - 1,
            lambda d: start(ks.at[at], buffer.at[me], 16 + at, place((me + 1 + d) % count)),
        )
        if beside is not None:
            beside()
        arrived(buffer.at[pl.ds(0, count - 1)], 16 + at)
        total = buffer[0]
        for i in range(1, count):
            total = total + buffer[i]
        ks[at + 1] = total

    def write_attitude():
        slab = jnp.concatenate(planes, axis=1)
        flat = dot_nn(jnp.concatenate(pieces_3(slab), axis=0), mixed)
        flat = flat[:n_hi] + flat[n_hi : 2 * n_hi] + flat[2 * n_hi :]
        for q in range(3):
            att_ref[pl.ds(q, n_src, stride=3), :] = flat[:n_src, 128 * q : 128 * q + 128]

    def start_inverse():
        write_attitude()
        pl.when(owner)(lambda: arrived(cf.at[pl.ds(0, n_own - 1)], 11))
        pl.when(jnp.logical_not(owner))(lambda: arrived(cf, 11))
        packed = jnp.concatenate([cf[i] for i in range(n_own)], axis=0)
        other_half = pltpu.roll(packed, 64, 1)
        for k in range(24):
            size = 24 - 8 * (k // 8)
            at = cal_row(k, 8 * (k // 8))
            part = packed[at : at + size] if k < 8 else other_half[at - 192 : at - 192 + size]
            inv[24 * k + 8 * (k // 8) : 24 * k + 24, :] = part
        for k in range(8, 24):
            size = 8 * (k // 8)
            inv[24 * k : 24 * k + size, :] = inv[pl.ds(k, size, stride=24), :]
        lax.fori_loop(0, 12, sweep, 0)

    core, xx = tm % 2, tm // 2
    exchange(kz, 2 * nz, 2 * zz + core, 0, lambda p: (2 * xx + p % 2, p // 2 * ny + yy), start_inverse)
    exchange(
        ky,
        n_tm // 2 * ny,
        xx * ny + yy,
        1,
        lambda p: (p // ny * 2 + core, zz * ny + p % ny),
        lambda: lax.fori_loop(12, 24, sweep, 0),
    )
    total = ks[2]
    right = jnp.concatenate([total[:, :NCU], total[:, NCU:]], axis=0)
    calib = jnp.zeros((24, NCU), F32)
    for j in range(24):
        calib = calib - inv[24 * j : 24 * j + 24, :NCU] * right[j : j + 1]
    calib_ref[...] = calib
    spread = dot_nn(jnp.concatenate(pieces_3(calib), axis=0), unit_hot)
    spread = spread[0:24] + spread[24:48] + spread[48:72]
    out = resid_b
    for k in range(24):
        out = out - calp[k] * spread[k : k + 1]
    resid_ref[...] = out.T

    left_us(vsr.at[pl.ds(0, last_tm)], 0)
    left_us(mr.at[pl.ds(0, last_sr), pl.ds(0, half)], 1)
    left_us(mr.at[pl.ds(0, last_sr), pl.ds(0, half)], 18)
    pl.when(has_next)(lambda: left_us(mr.at[0], 2))
    pl.when(owner)(lambda: left_us(cr.at[pl.ds(0, n_own - 1)], 3))
    pl.when(jnp.logical_not(owner))(lambda: left_us(cr.at[pl.ds(0, n_own)], 3))
    left_us(br.at[pl.ds(0, last_sr)], 4)
    pl.when(has_next)(lambda: left_us(br.at[0], 5))
    pl.when(has_prev)(lambda: left_us(br.at[0], 6))
    left_us(sub.at[pl.ds(0, last_tm)], 7)
    pl.when(has_left)(lambda: left_us(mown, 8))
    pl.when(has_right)(lambda: left_us(mown, 9))
    pl.when(owner)(lambda: left_us(c2r.at[pl.ds(0, last_tm)], 10))
    pl.when(owner)(lambda: left_us(cr.at[pl.ds(0, last_sr)], 11))
    left_us(g1.at[pl.ds(0, 2 * nz - 1)], 12)
    left_us(g2.at[pl.ds(0, n_xy - 1)], 13)
    left_us(xr.at[pl.ds(0, last_sr)], 14)
    pl.when(has_prev & first)(lambda: left_us(xr.at[pl.ds(0, n_src)], 15))
    left_us(kz.at[pl.ds(0, 2 * nz - 1)], 16)
    left_us(ky.at[pl.ds(0, n_tm // 2 * ny - 1)], 17)


def fast_shards(
    n_tm,
    n_src,
    src_deriv,
    att_deriv,
    cal_deriv,
    obs_resid,
    obs_weight,
    src_id,
    tile_knot,
    row_offset,
    cal_unit,
    src_prior,
    att_ridge,
):
    n_hi = (n_src + 1 + 7) // 8 * 8
    groups = src_prior.shape[1]
    lanes = groups // n_tm
    per_own = 24 // min(24, n_src)
    n_own, share = 24 // per_own, 8 * (24 // min(24, n_src))
    ny = min(4, n_src)
    nz = n_src // ny
    src_planes = jnp.transpose(src_deriv, (1, 0, 2))
    att_planes = jnp.transpose(att_deriv, (1, 0, 2))
    ridge = att_ridge.reshape(3 * n_src, 128)

    def f32(*shape):
        return jax.ShapeDtypeStruct(shape, F32)

    def vmem(*shape):
        return pltpu.VMEM(shape, F32)

    whole = pl.BlockSpec(memory_space=pltpu.VMEM)
    return pl.pallas_call(
        functools.partial(joint_kernel, n_tm, n_src, n_hi),
        out_shape=[f32(5, groups), f32(3 * n_src, 128), f32(24, NCU), f32(128, 128), f32(1, 1)],
        in_specs=[whole] * 11,
        out_specs=[whole] * 5,
        scratch_shapes=[
            vmem(8, groups),
            vmem(21, 128, 128),
            vmem(5, 128, 128),
            vmem(12, 128, 128),
            vmem(24, 128, 128),
            vmem(24 * 128, 128),
            pltpu.VMEM((128, 128), jnp.int32),
            vmem(128, 128),
            vmem(128, 128),
            vmem(7, MROWS + 8, 128),
            vmem(384, 128),
            vmem(24, 128),
            vmem(n_hi * MROWS, 128),
            vmem(n_hi, 128),
            vmem(192, 128),
            vmem(n_tm, 24, 128),
            vmem(2 * n_src, MROWS, 128),
            vmem(MROWS, 128),
            vmem(2, MROWS, 128),
            vmem(21, 8, 384),
            vmem(n_hi * 8, 128),
            vmem(2 * n_src, 8, 128),
            vmem(CG_ITERS + 2, 8, 384),
            vmem(CG_ITERS, 8, 128),
            vmem(2, 8, 128),
            vmem(2 * nz, 8, 128),
            vmem(n_tm // 2 * ny, 8, 128),
            vmem(32, 128),
            vmem(XROWS, 128),
            vmem(n_hi, XROWS, 128),
            vmem(n_tm, 8, lanes),
            vmem(n_src, share, 128),
            vmem(share, 128),
            vmem(n_tm, share, 128),
            vmem(share, 128),
            vmem(n_own, share, 128),
            vmem(576, 128),
            vmem(128, 128),
            vmem(24, 128),
            vmem(2 * nz, 12, 128),
            vmem(n_tm // 2 * ny, 12, 128),
            vmem(3, 12, 128),
            pltpu.SemaphoreType.DMA((19,)),
            pltpu.SemaphoreType.DMA((19,)),
        ],
        compiler_params=pltpu.CompilerParams(
            collective_id=0, has_side_effects=True, vmem_limit_bytes=48 << 20
        ),
        name="joint_solve",
    )(src_planes, att_planes, cal_deriv, obs_resid, obs_weight, row_offset, *(a.reshape(1, 128) for a in (src_id, tile_knot, cal_unit)), src_prior, ridge)


def hand_over(arrays):
    count = len(arrays)

    def kernel(*refs):
        for i in range(count):
            refs[count + i][...] = refs[i][...]

    whole = pl.BlockSpec(memory_space=pltpu.VMEM)
    return pl.pallas_call(
        kernel,
        out_shape=[jax.ShapeDtypeStruct(a.shape, a.dtype) for a in arrays],
        in_specs=[whole] * count,
        out_specs=[whole] * count,
        name="hand_over",
    )(*arrays)


def guarded_shards(n_tm, n_src, *arrays):
    update, attitude, calib, resid, trust = fast_shards(n_tm, n_src, *arrays)
    fast = (update, attitude, calib, resid)

    def slow():
        update, attitude, calib, resid = shards(*arrays)
        return update, attitude.reshape(-1, 128), calib, resid

    update, attitude, calib, resid = hand_over(lax.cond(trust[0, 0] > 0.5, lambda: fast, slow))
    return update, attitude.reshape(-1), calib, resid


def solution(mesh):
    placed = (
        P(("tm", "src"), None, None),
        P(("tm", "src"), None, None),
        P(("tm", "src"), None, None),
        P(("tm", "src"), None),
        P(("tm", "src"), None),
        P(("tm", "src")),
        P(("tm", "src")),
        P(("tm", "src"), None),
        P(("tm", "src")),
        P(None, "src"),
        P("tm"),
    )
    return jax.shard_map(
        functools.partial(guarded_shards, mesh.shape["tm"], mesh.shape["src"]),
        mesh=mesh,
        in_specs=placed,
        out_specs=(P(None, "src"), P("tm"), P(), P(("tm", "src"), None)),
        check_vma=False,
    )
```

```python
import functools

import jax
import jax.numpy as jnp
import numpy as np
from jax import lax
from jax.experimental import pallas as pl
from jax.experimental.pallas import tpu as pltpu
from jax.sharding import PartitionSpec as P

NCU = 64
CG_ITERS = 6


HIGH = lax.Precision.HIGHEST


def padded_2(cells, sides, width):
    for axis, dim in sides:
        count = lax.axis_size(axis)
        ends = count - 1
        head = lax.slice_in_dim(cells, 0, width, axis=dim)
        tail = lax.slice_in_dim(cells, cells.shape[dim] - width, cells.shape[dim], axis=dim)
        cells = jnp.concatenate(
            [
                lax.ppermute(tail, axis, [(i, (i + 1) % count) for i in range(ends)]),
                cells,
                lax.ppermute(head, axis, [((i + 1) % count, i) for i in range(ends)]),
            ],
            axis=dim,
        )
    return cells


def all_sum(array, axis):
    devices, step = lax.axis_size(axis), 1
    while step < devices:
        array = array + lax.ppermute(array, axis, [(i, i ^ step) for i in range(devices)])
        step *= 2
    return array


def from_behind(array, axis, by):
    devices = lax.axis_size(axis)
    pairs = [(i, i + by) for i in range(devices) if 0 <= i + by < devices]
    return lax.ppermute(array, axis, pairs)


def lag_table():
    first_index = np.arange(21)[None, :]
    lag_rows = np.arange(12)[:, None]
    second = first_index + lag_rows
    flat_index = first_index * 21 + np.minimum(second, 20)
    return (flat_index, (second < 21).astype(np.float32))


def solve_spd(matrix, right):
    order = right.shape[0]
    rows = jnp.arange(order)[:, None]

    def column(j, state):
        rest, factor = state
        col = jnp.where(rows >= j, rest[:, j] / jnp.sqrt(rest[j, j]), 0.0)
        return rest - col[:, None, :] * col[None, :, :], factor.at[:, j].set(col)

    factor = lax.fori_loop(0, order, column, (matrix, jnp.zeros_like(matrix)))[1]

    def forward(i, answer):
        value = right[i] - jnp.sum(jnp.where(rows < i, factor[i] * answer, 0.0), axis=0)
        return answer.at[i].set(value / factor[i, i])

    halfway = lax.fori_loop(0, order, forward, jnp.zeros_like(right))

    def backward(step, answer):
        i = order - 1 - step
        value = halfway[i] - jnp.sum(jnp.where(rows > i, factor[:, i] * answer, 0.0), axis=0)
        return answer.at[i].set(value / factor[i, i])

    return lax.fori_loop(0, order, backward, jnp.zeros_like(right))


def tile_normals(deriv, weight, resid):
    values = deriv.astype(jnp.float32)
    weighted = values * weight[:, None, :]
    normal = jnp.einsum("tkr,tlr->tkl", weighted, values, precision=HIGH)
    right = jnp.einsum("tkr,tr->tk", weighted, resid, precision=HIGH)
    return jnp.concatenate([normal.reshape(normal.shape[0], -1), right], axis=1)


def small_solve(sums, prior, order):
    count = sums.shape[1]
    matrix = sums[: order * order].reshape(order, order, count)
    if prior is not None:
        matrix = matrix + jnp.eye(order, dtype=jnp.float32)[:, :, None] * prior[:, None, :]
    return solve_spd(matrix, sums[order * order :])


def window_rows(att_deriv, row_offset):
    values = att_deriv.astype(jnp.float32)
    window = jnp.zeros((values.shape[0], 21, values.shape[2]), jnp.float32)
    for knot_step in range(4):
        placed = jnp.pad(values, ((0, 0), (3 * knot_step, 9 - 3 * knot_step), (0, 0)))
        window = window + jnp.where((row_offset == knot_step)[:, None, :], placed, 0.0)
    return window


def attitude_terms(window, weight, resid):
    weighted = window * weight[:, None, :]
    normal = jnp.einsum("tjr,tlr->tjl", weighted, window, precision=HIGH)
    right = jnp.einsum("tjr,tr->tj", weighted, resid, precision=HIGH)
    flat_index, valid_lag = lag_table()
    banded = normal.reshape(normal.shape[0], 441)[:, flat_index] * valid_lag
    return jnp.concatenate([banded, right[:, None, :]], axis=1)


def conjugate(band_rows, right, ridge_part, band_edge, extend, inner_sum):
    count = right.shape[0]
    lagged = jnp.concatenate([band_edge, band_rows[1:]], axis=1)
    solution = jnp.zeros_like(right)
    residual = right
    direction = right
    norm_now = inner_sum(residual, residual)
    for iteration in range(CG_ITERS):
        padded = extend(direction)
        result = ridge_part * direction
        for d in range(12):
            result = result + band_rows[d] * padded[11 + d : 11 + d + count]
        for d in range(1, 12):
            result = (
                result + lagged[d - 1, 11 - d : 11 - d + count] * padded[11 - d : 11 - d + count]
            )
        step_size = norm_now / inner_sum(direction, result)
        solution = solution + step_size * direction
        residual = residual - step_size * result
        norm_next = inner_sum(residual, residual)
        direction = residual + norm_next / norm_now * direction
        norm_now = norm_next
    return solution


def slab_extend(vector):
    return padded_2(vector, (("tm", 0),), 11)


def slab_dot(first_vec, second_vec):
    return all_sum(jnp.sum(first_vec * second_vec), "tm")


def shards(
    src_deriv,
    att_deriv,
    cal_deriv,
    obs_resid,
    obs_weight,
    src_id,
    tile_knot,
    row_offset,
    cal_unit,
    src_prior,
    att_ridge,
):
    slab_pos = lax.axis_index("tm")
    groups = src_prior.shape[1]
    normal_sums = jax.ops.segment_sum(
        tile_normals(src_deriv, obs_weight, obs_resid), src_id, num_segments=groups
    ).T
    summed = all_sum(normal_sums, "tm")
    source_update = small_solve(summed, src_prior, 5)
    resid_a = obs_resid - jnp.einsum(
        "tkr,kt->tr", src_deriv.astype(jnp.float32), source_update[:, src_id], precision=HIGH
    )
    slab_params = att_ridge.shape[0]
    window = window_rows(att_deriv, row_offset)
    local_knot = tile_knot - slab_pos * (slab_params // 3)
    columns = 3 * local_knot[:, None] + jnp.arange(21, dtype=jnp.int32)[None, :]
    values = attitude_terms(window, obs_weight, resid_a)
    slab_sums = jax.ops.segment_sum(
        values.transpose(0, 2, 1).reshape(-1, 13),
        columns.reshape(-1),
        num_segments=slab_params + 21,
    ).T
    carried = from_behind(slab_sums[:, slab_params:], "tm", 1)
    head_sums = slab_sums[:, :slab_params].at[:, :21].add(carried)
    summed_band = all_sum(head_sums, "src")
    band_edge = from_behind(summed_band[1:12, -11:], "tm", 1)
    attitude_update = conjugate(
        summed_band[:12], summed_band[12], att_ridge, band_edge, slab_extend, slab_dot
    )
    next_params = from_behind(attitude_update[:21], "tm", -1)
    extended = jnp.concatenate([attitude_update, next_params])
    resid_b = resid_a - jnp.einsum("tjr,tj->tr", window, extended[columns], precision=HIGH)
    calib_sums = jax.ops.segment_sum(
        tile_normals(cal_deriv, obs_weight, resid_b), cal_unit, num_segments=NCU
    ).T
    calib_total = all_sum(all_sum(calib_sums, "tm"), "src")
    calib_update = small_solve(calib_total, None, 24)
    residual_out = resid_b - jnp.einsum(
        "tkr,kt->tr", cal_deriv.astype(jnp.float32), calib_update[:, cal_unit], precision=HIGH
    )
    return (source_update, attitude_update, calib_update, residual_out)


F32 = jnp.float32
BF16 = jnp.bfloat16
MESH = pl.DeviceIdType.MESH
MROWS = 32
XROWS = 18
TRUST = 0.01


def pieces_2(x):
    high = x.astype(BF16)
    return high, (x - high.astype(F32)).astype(BF16)


def pieces_3(x):
    high = x.astype(BF16)
    rest = x - high.astype(F32)
    mid = rest.astype(BF16)
    return high, mid, (rest - mid.astype(F32)).astype(BF16)


def dot_nn(a, b):
    return lax.dot_general(a, b, (((1,), (0,)), ((), ())), preferred_element_type=F32)


def dot_nt(a, b):
    return lax.dot_general(a, b, (((1,), (1,)), ((), ())), preferred_element_type=F32)


def iota(shape, dim):
    return lax.broadcasted_iota(jnp.int32, shape, dim)


def hot(match):
    return jnp.where(match, 1.0, 0.0).astype(BF16)


def band_slots():
    slots = [(0, c, d) for c in range(3) for d in range(c, 3)]
    for delta in range(1, 4):
        slots += [(delta, c, d) for c in range(3) for d in range(3)]
    return slots


SLOTS = band_slots()
SLOT_AT = {slot: v for v, slot in enumerate(SLOTS)}
SRC_PAIRS = [(k, l) for k in range(5) for l in range(k, 5)]
SRC_AT = {pair: e for e, pair in enumerate(SRC_PAIRS)}
GRAM_PAIRS = [(i, j) for i in range(CG_ITERS) for j in range(i, CG_ITERS)]


def cal_row(k, l):
    if k < 8:
        return 24 * k + l
    if k < 16:
        return 192 + 16 * (k - 8) + l - 8
    return 320 + 8 * (k - 16) + l - 16


def place_lanes(lo_row):
    inside = iota((128, 128), 0) - lo_row
    return inside, iota((8, 128), 0) + 128 - lo_row


def ldl_solve(entry, right, order):
    low = {}
    pivots, inverse, shares = [], [], []
    for j in range(order):
        pivot = entry(j, j)
        for m in range(j):
            pivot = pivot - low[j, m] * low[j, m] * pivots[m]
        shares.append(pivot / entry(j, j))
        pivots.append(pivot)
        inverse.append(1.0 / pivot)
        for i in range(j + 1, order):
            value = entry(j, i)
            for m in range(j):
                value = value - low[i, m] * (low[j, m] * pivots[m])
            low[i, j] = value * inverse[j]
    forward = []
    for i in range(order):
        value = right(i)
        for m in range(i):
            value = value - low[i, m] * forward[m]
        forward.append(value)
    answer = [None] * order
    for i in range(order - 1, -1, -1):
        value = forward[i] * inverse[i]
        for m in range(i + 1, order):
            value = value - low[m, i] * answer[m]
        answer[i] = value
    return answer, shares


def joint_kernel(
    n_tm,
    n_src,
    n_hi,
    src_ref,
    att_in_ref,
    cal_ref,
    resid_in_ref,
    weight_ref,
    offset_ref,
    id_ref,
    knot_ref,
    unit_ref,
    raw_prior_ref,
    ridge_ref,
    update_ref,
    att_ref,
    calib_ref,
    resid_ref,
    trust_ref,
    prior_ref,
    winp,
    srcp,
    attp,
    calp,
    calf,
    offp,
    w_ref,
    r_ref,
    vm,
    vc,
    vs,
    mb,
    ex,
    cp,
    vsr,
    mr,
    mown,
    halo,
    band,
    pb,
    br,
    basis,
    image,
    gs,
    g1,
    g2,
    gt,
    xm,
    xr,
    sub,
    cr,
    c2s,
    c2r,
    c3s,
    cf,
    inv,
    ra,
    vrow,
    kz,
    ky,
    ks,
    send,
    recv,
):
    tm, sr = lax.axis_index("tm"), lax.axis_index("src")
    last_tm, last_sr = n_tm - 1, n_src - 1
    has_next, has_prev = tm < last_tm, tm > 0
    ny = min(4, n_src)
    nz = n_src // ny
    yy, zz = sr % ny, sr // ny
    per_own = 24 // min(24, n_src)
    n_own = 24 // per_own
    share = 8 * per_own
    owner = sr < n_own

    def block_of(p):
        return p // ny * ny + (p % ny + p // ny) % ny

    def device_of(b):
        return b // ny * ny + (b % ny + nz * ny - b // ny) % ny

    block_at = block_of(sr)
    final_sr = device_of(last_sr)
    first, final = sr == 0, sr == final_sr
    lanes = prior_ref.shape[1] // n_tm

    def start(source, target, at, place):
        pltpu.make_async_remote_copy(
            src_ref=source,
            dst_ref=target,
            send_sem=send.at[at],
            recv_sem=recv.at[at],
            device_id=place,
            device_id_type=MESH,
        ).start()

    def arrived(part, at):
        pltpu.make_async_copy(part, part, recv.at[at]).wait()

    def left_us(part, at):
        pltpu.make_async_copy(part, part, send.at[at]).wait()

    def each(count, body):
        def run(d, carry):
            body(d)
            return carry

        lax.fori_loop(0, count, run, 0)

    def other_src(body):
        each(last_sr, lambda d: body((sr + 1 + d) % n_src))

    def other_tm(body):
        each(last_tm, lambda d: body((tm + 1 + d) % n_tm))

    next_tm, prev_tm = jnp.minimum(tm + 1, last_tm), jnp.maximum(tm - 1, 0)
    halo[...] = jnp.zeros_like(halo)
    xr[n_src:] = jnp.zeros((n_hi - n_src, XROWS, 128), F32)

    barrier = pltpu.get_barrier_semaphore()

    def greet(a, b):
        pl.semaphore_signal(barrier, inc=1, device_id=(a, b), device_id_type=MESH)

    other_tm(lambda p: greet(p, sr))
    other_src(lambda p: greet(tm, p))

    w_ref[...] = weight_ref[...].T
    r_ref[...] = resid_in_ref[...].T
    offp[...] = offset_ref[...].astype(F32).T.astype(jnp.int32)
    for k in range(5):
        srcp[k] = src_ref[k].astype(F32).T
    for k in range(12):
        attp[k] = att_in_ref[k].astype(F32).T
    vm[...] = jnp.zeros_like(vm)
    prior_ref[...] = jnp.ones_like(prior_ref)
    prior_ref[0:5, :] = raw_prior_ref[...]
    pb[...] = jnp.zeros_like(pb)

    def windows(i, carry):
        rows = pl.ds(pl.multiple_of(i * 16, 16), 16)
        values = [attp[k, rows, :] for k in range(12)]
        step = offp[rows, :]
        for j in range(21):
            placed = jnp.zeros((16, 128), F32)
            for o in range(4):
                if 0 <= j - 3 * o < 12:
                    placed = jnp.where(step == o, values[j - 3 * o], placed)
            winp[j, rows, :] = placed
        return carry

    lax.fori_loop(0, 8, windows, 0)

    def summed(count, terms):
        def body(i, sums):
            rows = pl.ds(pl.multiple_of(i * 8, 8), 8)
            return tuple(s + t for s, t in zip(sums, terms(rows)))

        sums = lax.fori_loop(0, 16, body, tuple(jnp.zeros((8, 128), F32) for _ in range(count)))
        return [jnp.sum(s, axis=0, keepdims=True) for s in sums]

    def src_terms(rows):
        x = [srcp[k, rows, :] for k in range(5)]
        w = w_ref[rows, :]
        y = [w * v for v in x]
        r = r_ref[rows, :]
        return [y[k] * x[l] for k, l in SRC_PAIRS] + [v * r for v in y]

    vs[...] = jnp.zeros_like(vs)
    for e, row in enumerate(summed(20, src_terms)):
        vs[e : e + 1, :] = row
    vs[20:21, :] = id_ref[...].astype(F32)

    trace = jnp.sum(ridge_ref[...], axis=0, keepdims=True) * (1.0 / n_src)
    for m in range(7):
        slots = [s for s in SLOTS if m + s[0] < 7]

        def att_terms(rows, m=m, slots=slots):
            x = [winp[j, rows, :] for j in range(3 * m, min(3 * m + 12, 21))]
            w = w_ref[rows, :]
            y = [w * x[c] for c in range(3)]
            return [y[c] * x[3 * delta + d] for delta, c, d in slots]

        for slot, row in zip(slots, summed(len(slots), att_terms)):
            vm[m, SLOT_AT[slot] : SLOT_AT[slot] + 1, :] = row
            if slot[0] == 0 and slot[1] == slot[2]:
                trace = trace + row
    vs[21:22, :] = trace

    pl.semaphore_wait(barrier, last_tm + last_sr)
    other_tm(lambda p: start(vs, vsr.at[tm], 0, (p, sr)))

    knot = knot_ref[...] - tm * (128 * n_src)
    block, place = knot >> 7, knot & 127
    inside, past = place_lanes(place)
    blocks = iota((n_hi + 8, 128), 0)
    here, after = hot(blocks == block), hot(blocks == block + 1)
    spreads = jnp.concatenate([here, here, after, after], axis=1)
    rest = jnp.zeros((120, 128), F32)

    def spread_rows(row_of, count):
        spread = jnp.zeros((128, 128), F32)
        over = jnp.zeros((8, 128), F32)
        for m in range(count):
            row = row_of(m)
            spread = jnp.where(inside == m, row, spread)
            over = jnp.where(past == m, row, over)
        over = jnp.concatenate([over, rest], axis=0)
        right = jnp.concatenate(pieces_2(spread) + pieces_2(over), axis=1)
        return dot_nt(spreads, right)[:n_hi]

    def band_rows(j, at=0, size=MROWS):
        return mb.at[pl.ds(pl.multiple_of(j * MROWS + at, 8), size)]

    half = MROWS // 2
    for v, (delta, c, d) in enumerate(SLOTS):
        rows = spread_rows(lambda m, v=v: vm[m, v : v + 1, :], 7 - delta)
        if v < MROWS:
            mb[pl.ds(v, n_hi, stride=MROWS), :] = rows
            if v + 1 in (half, MROWS):
                at, sem = v + 1 - half, 1 if v < half else 18
                other_src(
                    lambda p, at=at, sem=sem: start(
                        band_rows(block_of(p), at, half), mr.at[sr, pl.ds(at, half)], sem, (tm, p)
                    )
                )
        else:
            ex[...] = rows


    ids = jnp.broadcast_to(id_ref[...].astype(F32), (128, 128)).T
    sources = (iota((lanes, 128), 0) + tm * lanes).astype(F32)
    wanted = jnp.concatenate([ids, sources], axis=0)
    groups = prior_ref.shape[1]
    source_hot = hot(iota((groups, 128), 0) == id_ref[...])
    owned = dot_nn(jnp.concatenate(pieces_3(prior_ref[...]), axis=0), source_hot)
    owned = owned[0:8] + owned[8:16] + owned[16:24]


    vsr[tm] = vs[...]
    arrived(vsr.at[pl.ds(0, last_tm)], 0)
    pl.when(has_next)(lambda: start(band_rows(n_src), mr.at[n_src + sr], 2, (next_tm, 0)))
    normal = jnp.zeros((48, 128 + lanes), F32)
    for p in range(0, n_tm, 2):
        match = [hot(wanted == vsr[q, 20:21, :]) for q in (p, p + 1)]
        parts = [pieces_2(vsr[q]) for q in (p, p + 1)]
        left = jnp.concatenate([jnp.concatenate([part[i] for part in parts], axis=1) for i in range(2)], axis=0)
        normal = normal + dot_nt(left, jnp.concatenate(match, axis=1))
    normal = normal[:24] + normal[24:]
    trace = sum(vsr[p, 21:22, :] for p in range(n_tm))
    prior = jnp.concatenate([owned, prior_ref[:, pl.ds(pl.multiple_of(tm * lanes, 128), lanes)]], axis=1)

    def source_entry(k, l):
        row = SRC_AT[k, l]
        value = normal[row : row + 1]
        return value + prior[k : k + 1] if k == l else value

    update, _ = ldl_solve(source_entry, lambda k: normal[15 + k : 16 + k], 5)
    resid_a = r_ref[...]
    for k in range(5):
        resid_a = resid_a - srcp[k] * update[k][:, :128]
    ra[...] = resid_a
    weighted = w_ref[...] * resid_a
    for j in range(21):
        vrow[j : j + 1, :] = jnp.sum(winp[j] * weighted, axis=0, keepdims=True)

    lane = iota((n_hi, 128), 1)

    def put_blocks(rows, centre_at, edge_at, extra=None):
        edges = jnp.where(lane < 64, pltpu.roll(rows, n_hi - 1, 0), pltpu.roll(rows, 1, 0))
        if extra is not None:
            edges = jnp.where((lane == 64) & (iota((n_hi, 128), 0) < n_src), extra, edges)
        pb[pl.ds(centre_at, n_hi, stride=8), :] = rows
        pb[pl.ds(edge_at, n_hi, stride=8), :] = edges

    trace = jnp.sum(trace, axis=1, keepdims=True)
    for c in range(3):
        rows = spread_rows(lambda m, c=c: vrow[3 * m + c : 3 * m + c + 1, :], 7)
        put_blocks(rows, c, 3 + c, trace if c == 0 else None)
    put_blocks(ex[...], 6, 7)

    def right_rows(j):
        return pb.at[pl.ds(pl.multiple_of(j * 8, 8), 8)]

    other_src(lambda p: start(right_rows(block_of(p)), br.at[sr], 4, (tm, p)))
    pl.when(has_next)(lambda: start(right_rows(n_src), br.at[n_src + sr], 5, (next_tm, 0)))
    pl.when(has_prev)(lambda: start(right_rows(n_hi - 1), br.at[n_src + sr], 6, (prev_tm, final_sr)))

    flat_at, plane_at = iota((384, 384), 1), iota((384, 384), 0)
    mixed = hot(flat_at == 3 * (plane_at & 127) + (plane_at >> 7))
    flat_ridge = jnp.concatenate([ridge_ref[pl.ds(3 * block_at + q, 1), :] for q in range(3)], axis=1)
    ridge_row = sum(dot_nt(jnp.broadcast_to(part, (16, 384)), mixed)[0:1] for part in pieces_3(flat_ridge))
    for k in range(5):
        sub[tm, k : k + 1, :] = update[k][:, 128:]
    other_tm(lambda p: start(sub.at[tm], sub.at[tm], 7, (p, sr)))

    mr[sr] = mb[pl.ds(pl.multiple_of(block_at * MROWS, 8), MROWS), :]
    arrived(mr.at[pl.ds(0, last_sr), pl.ds(0, half)], 1)
    arrived(mr.at[pl.ds(0, last_sr), pl.ds(0, half)], 18)
    total = mr[0]
    for i in range(1, n_src):
        total = total + mr[i]
    mown[...] = total

    def add_carried():
        arrived(mr.at[pl.ds(n_src, n_src)], 2)
        total = mown[...]
        for i in range(n_src):
            total = total + mr[n_src + i]
        mown[...] = total

    pl.when(has_prev & first)(add_carried)
    for c in range(3):
        v = SLOT_AT[0, c, c]
        mown[v : v + 1, :] = mown[v : v + 1, :] + ridge_row[:, 128 * c : 128 * c + 128]
    lin = tm * n_src + block_at
    lower, upper = jnp.maximum(lin - 1, 0), jnp.minimum(lin + 1, n_tm * n_src - 1)
    has_left, has_right = lin > 0, lin < n_tm * n_src - 1
    pl.when(has_left)(lambda: start(mown, halo.at[1], 8, (lower // n_src, device_of(lower % n_src))))
    pl.when(has_right)(lambda: start(mown, halo.at[0], 9, (upper // n_src, device_of(upper % n_src))))

    calf[...] = cal_ref[...].astype(F32).reshape(128 * 24, 128)
    for k in range(24):
        calp[k] = calf[pl.ds(k, 128, stride=24), :].T
    for kg in range(6):
        for lg in range(kg // 2, 3):

            def cal_terms(rows, kg=kg, lg=lg):
                w = w_ref[rows, :]
                y = [w * calp[4 * kg + k, rows, :] for k in range(4)]
                x = [calp[8 * lg + l, rows, :] for l in range(8)]
                return [y[k] * x[l] for k in range(4) for l in range(8)]

            sums = summed(32, cal_terms)
            for k in range(4):
                at = cal_row(4 * kg + k, 8 * lg)
                vc[at : at + 8, :] = jnp.concatenate(sums[8 * k : 8 * k + 8], axis=0)
    unit_hot = hot(iota((NCU, 128), 0) == unit_ref[...])
    unit_hot_2 = jnp.concatenate([unit_hot, unit_hot], axis=1)
    units = dot_nt(jnp.concatenate(pieces_2(vc[...]), axis=1), unit_hot_2)
    cp[...] = jnp.concatenate([units[:192], units[192:]], axis=1)

    def cal_share(p):
        return cp.at[pl.ds(pl.multiple_of(p * share, 8), share)]

    def send_cal(p):
        pl.when(p < n_own)(lambda: start(cal_share(p), cr.at[sr], 3, (tm, p)))

    other_src(send_cal)

    pl.when(has_left)(lambda: arrived(halo.at[0], 9))
    pl.when(has_right)(lambda: arrived(halo.at[1], 8))
    br[sr] = pb[pl.ds(pl.multiple_of(block_at * 8, 8), 8), :]
    arrived(br.at[pl.ds(0, last_sr)], 4)
    basis[0] = jnp.zeros((8, 384), F32)
    total = br[0]
    for i in range(1, n_src):
        total = total + br[i]
    gt[0:8, :] = total
    trace = total[3:4, 64:65]

    def add_other(at):
        arrived(br.at[pl.ds(n_src, n_src)], at)
        total = gt[0:8, :]
        for i in range(n_src):
            total = total + br[n_src + i]
        gt[0:8, :] = total

    pl.when(has_prev & first)(lambda: add_other(5))
    pl.when(has_next & final)(lambda: add_other(6))
    lane = iota((8, 128), 1)

    def widened(centre, edge):
        return jnp.concatenate([jnp.where(lane >= 110, edge, 0.0), centre, jnp.where(lane < 18, edge, 0.0)], axis=1)

    total = gt[0:8, :]
    edge = jnp.concatenate([total[3:8], total[0:3]], axis=0)
    basis[1] = jnp.where(iota((8, 384), 0) < 3, widened(total, edge), 0.0)
    last = widened(total[6:7] + jnp.zeros((8, 128), F32), total[7:8] + jnp.zeros((8, 128), F32))[0:1]
    full = jnp.concatenate([halo[0], mown[...], halo[1]], axis=1)
    full = jnp.concatenate([full, jnp.broadcast_to(last, (8, 384))], axis=0)
    band[...] = jnp.zeros_like(band)
    for d in range(3):
        for c in range(3):
            v = SLOT_AT[0, min(c, d), max(c, d)]
            band[9 + d, c : c + 1, :] = full[v : v + 1]
    for delta in range(1, 4):
        base = SLOT_AT[delta, 0, 0]
        moved = pltpu.roll(full, delta, 1)
        for d in range(3):
            for c in range(3):
                v = base + 3 * c + d
                band[3 * (3 + delta) + d, c : c + 1, :] = full[v : v + 1]
                v = base + 3 * d + c
                band[3 * (3 - delta) + d, c : c + 1, :] = moved[v : v + 1]

    mean = trace * (1.0 / (384 * n_src * n_tm))
    centre = jnp.broadcast_to(mean * 1.2, (8, 384))
    scale = jnp.broadcast_to(2.0 / (mean * 1.1), (8, 384))

    def grow(k, carry):
        x = basis[k + 1]
        y = jnp.zeros((8, 384), F32)
        for delta in range(-3, 4):
            moved = x if delta == 0 else pltpu.roll(x, (-delta) % 384, 1)
            for d in range(3):
                y = y + band[3 * (3 + delta) + d] * moved[d : d + 1]
        image[k] = y[:, 128:256]
        basis[k + 2] = scale * (y - centre * x) - basis[k]
        return carry

    lax.fori_loop(0, CG_ITERS, grow, 0)
    own = [basis[k + 1][:, 128:256] for k in range(CG_ITERS)]
    images = [image[k] for k in range(CG_ITERS)]
    rows = [jnp.sum(own[i] * images[j], axis=0, keepdims=True) for i, j in GRAM_PAIRS]
    rows += [jnp.sum(own[0] * own[i], axis=0, keepdims=True) for i in range(CG_ITERS)]
    for e, row in enumerate(rows):
        gt[e : e + 1, :] = row
    n_gram = len(rows)
    in_gram = iota((32, 128), 0) < n_gram
    same = iota((32, 128), 0) == iota((32, 128), 1)
    sums = jnp.sum(jnp.where(in_gram, gt[...], 0.0), axis=1, keepdims=True)
    gs[0] = jnp.broadcast_to(jnp.sum(jnp.where(same, sums, 0.0), axis=0, keepdims=True), (8, 128))
    core, xx = tm % 2, tm // 2
    g1[2 * zz + core] = gs[0]
    each(
        2 * nz - 1,
        lambda d: start(
            gs.at[0],
            g1.at[2 * zz + core],
            12,
            (2 * xx + (2 * zz + core + 1 + d) % 2, (2 * zz + core + 1 + d) % (2 * nz) // 2 * ny + yy),
        ),
    )
    for k in range(CG_ITERS):
        xm[3 * k : 3 * k + 3, :] = own[k][0:3]

    def slab_rows(i):
        return xr.at[i]

    other_src(lambda p: start(xm, slab_rows(block_at), 14, (tm, p)))
    pl.when(has_prev & first)(
        lambda: each(n_src, lambda i: start(xm, slab_rows(n_src), 15, (prev_tm, i)))
    )
    xr[block_at] = xm[...]

    def sum_cal():
        cr[sr] = cp[pl.ds(pl.multiple_of(sr * share, 8), share), :]
        arrived(cr.at[pl.ds(0, last_sr)], 3)
        total = cr[0]
        for i in range(1, n_src):
            total = total + cr[i]
        c2s[...] = total
        c2r[tm] = total
        other_tm(lambda p: start(c2s, c2r.at[tm], 10, (p, sr)))

    pl.when(owner)(sum_cal)

    def sweep(j, carry):
        row_of = iota((24, 128), 0)
        column = inv[pl.ds(pl.multiple_of(24 * j, 8), 24), :]
        pivot = jnp.sum(jnp.where(row_of == j, column, 0.0), axis=0, keepdims=True)
        over = 1.0 / pivot
        scaled = column * over
        for k in range(24):
            at = inv[24 * k : 24 * k + 24, :]
            factor = scaled[k : k + 1]
            inv[24 * k : 24 * k + 24, :] = jnp.where(row_of == j, factor, at - factor * column)
        inv[pl.ds(pl.multiple_of(24 * j, 8), 24), :] = jnp.where(row_of == j, -over, scaled)
        return carry

    arrived(g1.at[pl.ds(0, 2 * nz - 1)], 12)
    total = g1[0]
    for i in range(1, 2 * nz):
        total = total + g1[i]
    gs[1] = total
    n_xy = n_tm // 2 * ny
    at_xy = xx * ny + yy
    g2[at_xy] = total
    each(
        n_xy - 1,
        lambda d: start(
            gs.at[1],
            g2.at[at_xy],
            13,
            ((at_xy + 1 + d) % n_xy // ny * 2 + core, zz * ny + (at_xy + 1 + d) % n_xy % ny),
        ),
    )
    def finish_cal():
        arrived(c2r.at[pl.ds(0, last_tm)], 10)
        total = c2r[0]
        for i in range(1, n_tm):
            total = total + c2r[i]
        c3s[...] = total
        cf[sr] = total
        other_src(lambda p: start(c3s, cf.at[sr], 11, (tm, p)))

    pl.when(owner)(finish_cal)

    arrived(g2.at[pl.ds(0, n_xy - 1)], 13)
    total = g2[0]
    for i in range(1, n_xy):
        total = total + g2[i]
    sums = jnp.sum(jnp.where(same, total[0:1], 0.0), axis=1, keepdims=True)
    gt[...] = jnp.broadcast_to(sums, (32, 128))
    gram_at = {pair: e for e, pair in enumerate(GRAM_PAIRS)}
    n_pairs = len(GRAM_PAIRS)

    def gram(i, j):
        e = gram_at[i, j]
        return gt[e : e + 1, :]

    weights, shares = ldl_solve(gram, lambda i: gt[n_pairs + i : n_pairs + i + 1, :], CG_ITERS)
    least = shares[0]
    for value in shares[1:]:
        least = jnp.where(value >= least, least, value)
    trust_ref[...] = jnp.where(least > TRUST, 1.0, 0.0)[:, 0:1]
    arrived(sub.at[pl.ds(0, last_tm)], 7)
    for p in range(n_tm):
        update_ref[:, lanes * p : lanes * p + lanes] = sub[p, 0:5, :]

    here_3 = jnp.concatenate([here[:n_hi].astype(F32)] * 3 + [jnp.zeros((128 - 3 * n_hi, 128), F32)], axis=0).astype(BF16)
    after_3 = jnp.concatenate([after[:n_hi].astype(F32)] * 3 + [jnp.zeros((128 - 3 * n_hi, 128), F32)], axis=0).astype(BF16)
    arrived(xr.at[pl.ds(0, last_sr)], 14)
    pl.when(has_next)(lambda: arrived(slab_rows(n_src), 15))
    resid_b = ra[...]
    planes = []
    for c in range(3):
        plane = weights[0] * xr[:, c, :]
        for k in range(1, CG_ITERS):
            plane = plane + weights[k] * xr[:, 3 * k + c, :]
        planes.append(plane)
        parts = [part.astype(F32) for part in pieces_3(plane)]
        parts.append(jnp.zeros((128 - 3 * n_hi, 128), F32))
        turned = jnp.concatenate(parts, axis=0).T.astype(BF16)
        at_place = dot_nn(turned, here_3)
        past_place = dot_nn(turned[:16], after_3)[:8]
        for m in range(7):
            value = jnp.sum(jnp.where(inside == m, at_place, 0.0), axis=0, keepdims=True)
            value = value + jnp.sum(jnp.where(past == m, past_place, 0.0), axis=0, keepdims=True)
            resid_b = resid_b - winp[3 * m + c] * value

    weighted = w_ref[...] * resid_b
    for k in range(24):
        vrow[k : k + 1, :] = jnp.sum(calp[k] * weighted, axis=0, keepdims=True)
    units = dot_nt(jnp.concatenate(pieces_2(vrow[...]), axis=1), unit_hot_2)
    ks[0] = jnp.concatenate([units[0:12], units[12:24]], axis=1)

    def exchange(buffer, count, me, at, place, beside=None):
        buffer[me] = ks[at]
        each(
            count - 1,
            lambda d: start(ks.at[at], buffer.at[me], 16 + at, place((me + 1 + d) % count)),
        )
        if beside is not None:
            beside()
        arrived(buffer.at[pl.ds(0, count - 1)], 16 + at)
        total = buffer[0]
        for i in range(1, count):
            total = total + buffer[i]
        ks[at + 1] = total

    def write_attitude():
        slab = jnp.concatenate(planes, axis=1)
        flat = dot_nn(jnp.concatenate(pieces_3(slab), axis=0), mixed)
        flat = flat[:n_hi] + flat[n_hi : 2 * n_hi] + flat[2 * n_hi :]
        for q in range(3):
            att_ref[pl.ds(q, n_src, stride=3), :] = flat[:n_src, 128 * q : 128 * q + 128]

    def start_inverse():
        write_attitude()
        pl.when(owner)(lambda: arrived(cf.at[pl.ds(0, n_own - 1)], 11))
        pl.when(jnp.logical_not(owner))(lambda: arrived(cf, 11))
        packed = jnp.concatenate([cf[i] for i in range(n_own)], axis=0)
        other_half = pltpu.roll(packed, 64, 1)
        for k in range(24):
            size = 24 - 8 * (k // 8)
            at = cal_row(k, 8 * (k // 8))
            part = packed[at : at + size] if k < 8 else other_half[at - 192 : at - 192 + size]
            inv[24 * k + 8 * (k // 8) : 24 * k + 24, :] = part
        for k in range(8, 24):
            size = 8 * (k // 8)
            inv[24 * k : 24 * k + size, :] = inv[pl.ds(k, size, stride=24), :]
        lax.fori_loop(0, 12, sweep, 0)

    core, xx = tm % 2, tm // 2
    exchange(kz, 2 * nz, 2 * zz + core, 0, lambda p: (2 * xx + p % 2, p // 2 * ny + yy), start_inverse)
    exchange(
        ky,
        n_tm // 2 * ny,
        xx * ny + yy,
        1,
        lambda p: (p // ny * 2 + core, zz * ny + p % ny),
        lambda: lax.fori_loop(12, 24, sweep, 0),
    )
    total = ks[2]
    right = jnp.concatenate([total[:, :NCU], total[:, NCU:]], axis=0)
    calib = jnp.zeros((24, NCU), F32)
    for j in range(24):
        calib = calib - inv[24 * j : 24 * j + 24, :NCU] * right[j : j + 1]
    calib_ref[...] = calib
    spread = dot_nn(jnp.concatenate(pieces_3(calib), axis=0), unit_hot)
    spread = spread[0:24] + spread[24:48] + spread[48:72]
    out = resid_b
    for k in range(24):
        out = out - calp[k] * spread[k : k + 1]
    resid_ref[...] = out.T

    left_us(vsr.at[pl.ds(0, last_tm)], 0)
    left_us(mr.at[pl.ds(0, last_sr), pl.ds(0, half)], 1)
    left_us(mr.at[pl.ds(0, last_sr), pl.ds(0, half)], 18)
    pl.when(has_next)(lambda: left_us(mr.at[0], 2))
    pl.when(owner)(lambda: left_us(cr.at[pl.ds(0, n_own - 1)], 3))
    pl.when(jnp.logical_not(owner))(lambda: left_us(cr.at[pl.ds(0, n_own)], 3))
    left_us(br.at[pl.ds(0, last_sr)], 4)
    pl.when(has_next)(lambda: left_us(br.at[0], 5))
    pl.when(has_prev)(lambda: left_us(br.at[0], 6))
    left_us(sub.at[pl.ds(0, last_tm)], 7)
    pl.when(has_left)(lambda: left_us(mown, 8))
    pl.when(has_right)(lambda: left_us(mown, 9))
    pl.when(owner)(lambda: left_us(c2r.at[pl.ds(0, last_tm)], 10))
    pl.when(owner)(lambda: left_us(cr.at[pl.ds(0, last_sr)], 11))
    left_us(g1.at[pl.ds(0, 2 * nz - 1)], 12)
    left_us(g2.at[pl.ds(0, n_xy - 1)], 13)
    left_us(xr.at[pl.ds(0, last_sr)], 14)
    pl.when(has_prev & first)(lambda: left_us(xr.at[pl.ds(0, n_src)], 15))
    left_us(kz.at[pl.ds(0, 2 * nz - 1)], 16)
    left_us(ky.at[pl.ds(0, n_tm // 2 * ny - 1)], 17)


def fast_shards(
    n_tm,
    n_src,
    src_deriv,
    att_deriv,
    cal_deriv,
    obs_resid,
    obs_weight,
    src_id,
    tile_knot,
    row_offset,
    cal_unit,
    src_prior,
    att_ridge,
):
    n_hi = (n_src + 1 + 7) // 8 * 8
    groups = src_prior.shape[1]
    lanes = groups // n_tm
    per_own = 24 // min(24, n_src)
    n_own, share = 24 // per_own, 8 * (24 // min(24, n_src))
    ny = min(4, n_src)
    nz = n_src // ny
    src_planes = jnp.transpose(src_deriv, (1, 0, 2))
    att_planes = jnp.transpose(att_deriv, (1, 0, 2))
    ridge = att_ridge.reshape(3 * n_src, 128)

    def f32(*shape):
        return jax.ShapeDtypeStruct(shape, F32)

    def vmem(*shape):
        return pltpu.VMEM(shape, F32)

    whole = pl.BlockSpec(memory_space=pltpu.VMEM)
    return pl.pallas_call(
        functools.partial(joint_kernel, n_tm, n_src, n_hi),
        out_shape=[f32(5, groups), f32(3 * n_src, 128), f32(24, NCU), f32(128, 128), f32(1, 1)],
        in_specs=[whole] * 11,
        out_specs=[whole] * 5,
        scratch_shapes=[
            vmem(8, groups),
            vmem(21, 128, 128),
            vmem(5, 128, 128),
            vmem(12, 128, 128),
            vmem(24, 128, 128),
            vmem(24 * 128, 128),
            pltpu.VMEM((128, 128), jnp.int32),
            vmem(128, 128),
            vmem(128, 128),
            vmem(7, MROWS + 8, 128),
            vmem(384, 128),
            vmem(24, 128),
            vmem(n_hi * MROWS, 128),
            vmem(n_hi, 128),
            vmem(192, 128),
            vmem(n_tm, 24, 128),
            vmem(2 * n_src, MROWS, 128),
            vmem(MROWS, 128),
            vmem(2, MROWS, 128),
            vmem(21, 8, 384),
            vmem(n_hi * 8, 128),
            vmem(2 * n_src, 8, 128),
            vmem(CG_ITERS + 2, 8, 384),
            vmem(CG_ITERS, 8, 128),
            vmem(2, 8, 128),
            vmem(2 * nz, 8, 128),
            vmem(n_tm // 2 * ny, 8, 128),
            vmem(32, 128),
            vmem(XROWS, 128),
            vmem(n_hi, XROWS, 128),
            vmem(n_tm, 8, lanes),
            vmem(n_src, share, 128),
            vmem(share, 128),
            vmem(n_tm, share, 128),
            vmem(share, 128),
            vmem(n_own, share, 128),
            vmem(576, 128),
            vmem(128, 128),
            vmem(24, 128),
            vmem(2 * nz, 12, 128),
            vmem(n_tm // 2 * ny, 12, 128),
            vmem(3, 12, 128),
            pltpu.SemaphoreType.DMA((19,)),
            pltpu.SemaphoreType.DMA((19,)),
        ],
        compiler_params=pltpu.CompilerParams(
            collective_id=0, has_side_effects=True, vmem_limit_bytes=48 << 20
        ),
        name="joint_solve",
    )(src_planes, att_planes, cal_deriv, obs_resid, obs_weight, row_offset, *(a.reshape(1, 128) for a in (src_id, tile_knot, cal_unit)), src_prior, ridge)


def hand_over(arrays):
    count = len(arrays)

    def kernel(*refs):
        for i in range(count):
            refs[count + i][...] = refs[i][...]

    whole = pl.BlockSpec(memory_space=pltpu.VMEM)
    return pl.pallas_call(
        kernel,
        out_shape=[jax.ShapeDtypeStruct(a.shape, a.dtype) for a in arrays],
        in_specs=[whole] * count,
        out_specs=[whole] * count,
        name="hand_over",
    )(*arrays)


def guarded_shards(n_tm, n_src, *arrays):
    update, attitude, calib, resid, trust = fast_shards(n_tm, n_src, *arrays)
    fast = (update, attitude, calib, resid)

    def slow():
        update, attitude, calib, resid = shards(*arrays)
        return update, attitude.reshape(-1, 128), calib, resid

    update, attitude, calib, resid = hand_over(lax.cond(trust[0, 0] > 0.5, lambda: fast, slow))
    return update, attitude.reshape(-1), calib, resid


def solution(mesh):
    placed = (
        P(("tm", "src"), None, None),
        P(("tm", "src"), None, None),
        P(("tm", "src"), None, None),
        P(("tm", "src"), None),
        P(("tm", "src"), None),
        P(("tm", "src")),
        P(("tm", "src")),
        P(("tm", "src"), None),
        P(("tm", "src")),
        P(None, "src"),
        P("tm"),
    )
    return jax.shard_map(
        functools.partial(guarded_shards, mesh.shape["tm"], mesh.shape["src"]),
        mesh=mesh,
        in_specs=placed,
        out_specs=(P(None, "src"), P("tm"), P(), P(("tm", "src"), None)),
        check_vma=False,
    )
```
